256 devices in a mesh: dp: 16 (over z, core), expert: 16 (over x, y).
Axes of the slice: x: 4, y: 4, z: 8, core: 2. Of those that a mesh axis runs over, the one named last changes fastest.
Arguments:
- tokens_in: bfloat16 [16, 4096, 2048], P('expert', 'dp'), may hold values from -6 to 6
- out_grads: bfloat16 [16, 4096, 768], P('expert', 'dp'), may hold values from -6 to 6
- counts: int32 [16, 16, 2], P('expert', 'dp'), may hold values from 32 to 128, as said below
- copy_list: int32 [16], replicated, may hold values from 0 to 15, as said below
- weights: bfloat16 [16, 2048, 768], P('expert', 'dp'), may hold values from -0.125 to 0.125
- momentum: float32 [16, 2048, 768], P('expert', 'dp'), may hold values from -1920 to 1920
Outputs:
- new_momentum: float32 [16, 2048, 768], P('expert', 'dp')
- home_update: float32 [16, 2048, 768], P('expert', 'dp')
- replica_weight: bfloat16 [16, 2048, 768], P('expert')
The draws below stay inside these ranges and needn't reach their ends.
Inputs may be any that keep to these rules, and one draw needn't show every extreme that they name: Each count lies between 32 and 128; both ends are taken by some device in every draw; slots past the two counts are padding. copy_list[j] is never j; an expert may sit in several copy slots.
All inputs are finite; a program needn't handle non-finite values.
Results may differ from the reference program's by a relative error of at most 0.011.
Values may be sent and summed in bfloat16 or wider, within the bound.
No kernel may reach another device: no remote copies, remote signals or barrier semaphores. Data moves between devices by JAX's collectives and lax.ppermute only.
A program may use at most 64 MiB of HBM per device.

```python
import math
import jax
import jax.numpy as jnp
from jax import lax

D = 2048
FF = 768
TOK_DEV = 256
ITERS = 3
EXPERTS = 16
ROWS = 4096
N_DP = 16


def draw_counts(key, part):
    key = jax.random.fold_in(key, 3)
    key_vals, key_first, key_gap = jax.random.split(key, 3)
    lowest = TOK_DEV // 8
    highest_count = TOK_DEV // 2
    total = EXPERTS * N_DP * 2
    values = jax.random.randint(key_vals, (total,), lowest, highest_count + 1)
    first = jax.random.randint(key_first, (), 0, total)
    second = (first + 1 + jax.random.randint(key_gap, (), 0, total - 1)) % total
    places = jnp.arange(total, dtype=jnp.int32)
    values = jnp.where(places == first, lowest, values)
    values = jnp.where(places == second, highest_count, values)
    return values.reshape(EXPERTS, N_DP, 2).astype(jnp.int32)


def draw_copy_list(key, part):
    key = jax.random.fold_in(key, 7)
    key_hot, key_offs, key_coin = jax.random.split(key, 3)
    places = jnp.arange(EXPERTS, dtype=jnp.int32)
    hotter = jax.random.randint(key_hot, (), 0, EXPERTS)
    offsets = jax.random.randint(key_offs, (EXPERTS,), 1, EXPERTS)
    others = (places + offsets) % EXPERTS
    coins = jax.random.randint(key_coin, (EXPERTS,), 0, 2) == 1
    picked = jnp.where(coins & (places != hotter), hotter, others)
    picked = jnp.where(places == 0, EXPERTS - 1, picked)
    picked = jnp.where(places == EXPERTS - 1, 0, picked)
    return picked.astype(jnp.int32)


def scaled_rows(noise, rise):
    base = 0.5 * (N_DP * TOK_DEV) ** 0.5
    fraction = jnp.arange(D, dtype=jnp.float32) / (D - 1.0)
    row_scale = base * jnp.exp(jnp.log(rise) * fraction)
    return noise * row_scale[None, :, None]


def draw_momentum(key, part):
    key = jax.random.fold_in(key, 11)
    noise = jnp.clip(jax.random.normal(key, (EXPERTS, D, FF), jnp.float32), -6.0, 6.0)
    return scaled_rows(noise, 10.0).astype(jnp.float32)


def block_levels(rng, extent, pieces, least, largest):
    gain = 1.0
    for position, parts in pieces:
        draws = jax.random.uniform(jax.random.fold_in(jax.random.fold_in(rng, 6), position), (parts,), jnp.float32, least / len(pieces), largest / len(pieces))
        gain = gain * jnp.repeat(jnp.exp(draws), extent[position] // parts).reshape((-1,) + (1,) * (len(extent) - 1 - position))
    return gain


def normal_values(own_key, shape, scale, most, cuts=(), kind=jnp.bfloat16):
    values = scale * jax.random.normal(own_key, shape, jnp.float32)
    if cuts:
        values = values * block_levels(own_key, shape, cuts, -0.22, 0.18)
    return jnp.clip(values, -most, most).astype(kind)


def setup_inputs(seed: int = 0) -> dict:
    streams_of = jax.random.split(jax.random.key(seed), 7)
    return {
        "tokens_in": normal_values(streams_of[0], (EXPERTS, ROWS, D), 1.0, 6.0, ((0, 16), (1, 16))),
        "out_grads": normal_values(streams_of[1], (EXPERTS, ROWS, FF), 1.0, 6.0, ((0, 16), (1, 16))),
        "counts": draw_counts(jax.random.fold_in(streams_of[6], 71), 0),
        "copy_list": draw_copy_list(jax.random.fold_in(streams_of[6], 71), 0),
        "weights": normal_values(streams_of[4], (EXPERTS, D, FF), D ** -0.5, 0.125, ((0, 16), (1, 16))),
        "momentum": draw_momentum(jax.random.fold_in(streams_of[6], 71), 0),
    }


coef_a = 3.4445
coef_b = -4.775
coef_c = 2.0315
beta_mom = 0.95
learn_rate = 0.02
norm_eps = 1e-07
highest = lax.Precision.HIGHEST

def device_term(activations, grads_out, count_pair):
    positions = jnp.arange(TOK_DEV, dtype=jnp.int32)[:, None]
    home_mask = positions < count_pair[0]
    copy_mask = (positions >= count_pair[0]) & (positions < count_pair[0] + count_pair[1])
    zeros_bf = jnp.zeros_like(grads_out)
    stacked = jnp.concatenate([jnp.where(home_mask, grads_out, zeros_bf), jnp.where(copy_mask, grads_out, zeros_bf)], axis=1)
    term = jnp.dot(activations.astype(jnp.float32).T, stacked.astype(jnp.float32), precision=highest, preferred_element_type=jnp.float32)
    rounded = lax.optimization_barrier(term.astype(jnp.bfloat16))
    return rounded.astype(jnp.float32)

def newton_schulz(matrix):
    iterate = matrix / (jnp.sqrt(jnp.sum(matrix * matrix)) + norm_eps)
    for step in range(ITERS):
        gram = jnp.dot(iterate.T, iterate, precision=highest, preferred_element_type=jnp.float32)
        poly = coef_b * gram + coef_c * jnp.dot(gram, gram, precision=highest, preferred_element_type=jnp.float32)
        iterate = coef_a * iterate + jnp.dot(iterate, poly, precision=highest, preferred_element_type=jnp.float32)
    return iterate

def reference(tokens_in, out_grads, counts, copy_list, weights, momentum):
    acts_dp = tokens_in.reshape(EXPERTS, N_DP, TOK_DEV, D).transpose(1, 0, 2, 3)
    grads_dp = out_grads.reshape(EXPERTS, N_DP, TOK_DEV, FF).transpose(1, 0, 2, 3)
    counts_dp = counts.transpose(1, 0, 2)

    def dp_step(carry, inputs):
        activations, grads_out, count_pair = inputs
        return (carry + jax.vmap(device_term)(activations, grads_out, count_pair), None)
    start_sum = jnp.zeros((EXPERTS, D, 2 * FF), jnp.float32)
    total, unused = lax.scan(dp_step, start_sum, (acts_dp, grads_dp, counts_dp))
    home_sum = total[:, :, :FF]
    copy_sum = total[:, :, FF:]
    owners = jnp.arange(EXPERTS, dtype=jnp.int32)[:, None]
    chosen = (copy_list[None, :] == owners).astype(jnp.float32)
    gradient = home_sum + jnp.einsum('ej,jdf->edf', chosen, copy_sum, precision=highest)
    new_momentum = beta_mom * momentum + gradient
    iterate = jax.vmap(newton_schulz)(new_momentum)
    home_update = 0.2 * math.sqrt(max(D, FF)) * iterate
    fresh_weight = (weights.astype(jnp.float32) - learn_rate * home_update).astype(jnp.bfloat16)
    replica_weight = jnp.take(fresh_weight, copy_list, axis=0)
    return (new_momentum, home_update, replica_weight)
```

```python
import math

import jax
import jax.numpy as jnp
from jax import lax
from jax.experimental import pallas as pl
from jax.experimental.pallas import tpu as pltpu
from jax.sharding import Mesh, PartitionSpec as P

coef_a = 3.4445
coef_b = -4.775
coef_c = 2.0315
beta_mom = 0.95
learn_rate = 0.02
norm_eps = 1e-07

NZ, NC, NX, NY = 8, 2, 4, 4
BF = jnp.bfloat16
F32 = jnp.float32


def shift(value, axis, size, offset):
    return lax.ppermute(value, axis, [(i, (i + offset) % size) for i in range(size)])


def up(value):
    return shift(value, "z", NZ, 1)


def down(value):
    return shift(value, "z", NZ, NZ - 1)


def swap(value):
    return shift(value, "core", NC, 1)


def add_bf(left, right):
    return (left.astype(F32) + right.astype(F32)).astype(BF)


def ring_sum(blocks, z):
    half = blocks.shape[1] // 2

    def mine(offset):
        return lax.dynamic_index_in_dim(blocks, lax.rem(z + offset + NZ, NZ), 0, keepdims=False)

    far = mine(4)
    going_up, going_down = up(far[:half]), down(far[half:])
    near = mine(3)
    going_up = jnp.concatenate([add_bf(near[:half], going_up), near[half:]], axis=0)
    near = mine(-3)
    going_down = jnp.concatenate([near[:half], add_bf(near[half:], going_down)], axis=0)
    for offset in (2, 1):
        going_up, going_down = up(going_up), down(going_down)
        going_up = add_bf(mine(offset), going_up)
        going_down = add_bf(mine(-offset), going_down)
    going_up, going_down = up(going_up), down(going_down)
    return mine(0).astype(F32) + going_up.astype(F32) + going_down.astype(F32)


def ring_gather(block):
    half = block.shape[0] // 2
    got = {0: (block, swap(block))}
    from_below, from_above = block, block
    for step in (1, 2, 3):
        from_below, from_above = up(from_below), down(from_above)
        other = swap(jnp.concatenate([from_below, from_above], axis=0))
        got[-step] = (from_below, other[: 2 * half])
        got[step] = (from_above, other[2 * half :])
    far = jnp.concatenate([up(from_below[:half]), down(from_above[half:])], axis=0)
    got[4] = (far, swap(far))
    return got


def place_kernel(order_ref, *refs):
    *pieces, out_ref, sems = refs
    rows = pieces[0].shape[0]
    copies = []
    for place, piece in enumerate(pieces):
        start = pl.multiple_of(order_ref[place] * rows, rows)
        copies.append(
            pltpu.make_async_copy(piece, out_ref.at[pl.ds(start, rows), :], sems.at[place])
        )
    for copy in copies:
        copy.start()
    for copy in copies:
        copy.wait()


def place(order, pieces):
    rows, width = pieces[0].shape
    count = len(pieces)
    return pl.pallas_call(
        place_kernel,
        out_shape=jax.ShapeDtypeStruct((count * rows, width), pieces[0].dtype),
        grid_spec=pltpu.PrefetchScalarGridSpec(
            num_scalar_prefetch=1,
            grid=(),
            in_specs=[pl.BlockSpec(memory_space=pl.ANY)] * count,
            out_specs=pl.BlockSpec(memory_space=pl.ANY),
            scratch_shapes=[pltpu.SemaphoreType.DMA((count,))],
        ),
        name="place",
    )(order, *pieces)


def mm(left, right):
    return jnp.dot(left, right, precision=lax.Precision.HIGHEST, preferred_element_type=F32)


def body(tokens_in, out_grads, counts, copy_list, weights, momentum):
    acts = tokens_in[0]
    grads = out_grads[0]
    tok_rows, model_width = acts.shape
    width = grads.shape[1]
    z = lax.axis_index("z")
    core = lax.axis_index("core")
    x = lax.axis_index("x")
    y = lax.axis_index("y")
    rows = model_width // (NZ * NC)

    split = acts.reshape(tok_rows, NZ, NC, rows)
    keep = jnp.where(core == 0, split[:, :, 0], split[:, :, 1]).reshape(tok_rows, NZ * rows)
    give = jnp.where(core == 0, split[:, :, 1], split[:, :, 0]).reshape(tok_rows, NZ * rows)
    both_acts = jnp.concatenate([keep, swap(give)], axis=0)
    both_grads = jnp.concatenate([grads, swap(grads)], axis=0)
    both_counts = jnp.concatenate([counts[0], swap(counts[0])], axis=0)
    positions = lax.broadcasted_iota(jnp.int32, (2 * tok_rows, 1), 0)
    first = positions < tok_rows
    slot = jnp.where(first, positions, positions - tok_rows)
    home_count = jnp.where(first, both_counts[0, 0], both_counts[1, 0])
    copy_count = jnp.where(first, both_counts[0, 1], both_counts[1, 1])
    home_mask = slot < home_count
    copy_mask = (slot >= home_count) & (slot < home_count + copy_count)
    zeros = jnp.zeros_like(both_grads)

    def terms(mask):
        out = lax.dot_general(
            both_acts,
            jnp.where(mask, both_grads, zeros),
            (((0,), (0,)), ((), ())),
            preferred_element_type=F32,
        )
        return out.astype(BF)

    copy_terms = terms(copy_mask)
    home_terms = terms(home_mask)
    home_sum = lax.psum_scatter(home_terms, "z", scatter_dimension=0, tiled=True)
    copy_sum = ring_sum(copy_terms.reshape(NZ, rows, width), z).astype(BF)

    buckets = [jnp.zeros((rows, width), F32) for _ in range(NX)]
    for offset in range(NY):
        piece = copy_sum if offset == 0 else shift(copy_sum, "y", NY, offset)
        target = copy_list[x * NY + lax.rem(y - offset + NY, NY)]
        for ahead in range(NX):
            here = target == lax.rem(x + ahead, NX) * NY + y
            buckets[ahead] = buckets[ahead] + jnp.where(here, piece.astype(F32), 0.0)
    gradient = home_sum.astype(F32) + buckets[0]
    for ahead in range(1, NX):
        gradient = gradient + shift(buckets[ahead].astype(BF), "x", NX, ahead).astype(F32)

    fresh_mom = beta_mom * momentum[0] + gradient

    gathered = ring_gather(fresh_mom.astype(BF))
    gram = jnp.zeros((width, width), F32)
    for group in ((0,), (-1, 1), (-2, 2), (-3, 3), (4,)):
        part = jnp.concatenate([b for offset in group for b in gathered[offset]], axis=0)
        gram = gram + lax.dot_general(
            part, part, (((0,), (0,)), ((), ())), preferred_element_type=F32
        )
    total_sq = jnp.trace(gram)
    scale = 1.0 / (jnp.sqrt(total_sq) + norm_eps)
    gram = gram * scale * scale
    iterate = fresh_mom * scale
    for step in range(3):
        poly = coef_b * gram + coef_c * mm(gram, gram)
        iterate = coef_a * iterate + mm(iterate, poly)
        if step < 2:
            side = coef_a * gram + mm(gram, poly)
            gram = coef_a * side + mm(side, poly)

    update = 0.2 * math.sqrt(max(model_width, width)) * iterate
    fresh = (weights[0].astype(F32) - learn_rate * update).astype(BF)

    column = [fresh] + [shift(fresh, "x", NX, offset) for offset in range(1, NX)]

    def wanted(offset):
        source_x = copy_list[x * NY + lax.rem(y + offset, NY)] // NY
        behind = lax.rem(x - source_x + NX, NX)
        picked = column[0]
        for k in range(1, NX):
            picked = jnp.where(behind == k, column[k], picked)
        return picked

    target = copy_list[x * NY + y]
    behind = lax.rem(y - target % NY + NY, NY)
    replica = wanted(0)
    for offset in range(1, NY):
        replica = jnp.where(behind == offset, shift(wanted(offset), "y", NY, offset), replica)

    gathered = ring_gather(replica)
    pieces, order = [], []
    for offset, pair in gathered.items():
        there = lax.rem(z + offset + NZ, NZ)
        pieces += list(pair)
        order += [there * NC + core, there * NC + 1 - core]
    full = place(jnp.stack(order).astype(jnp.int32), pieces)
    return (fresh_mom[None], update[None], full[None])


def solution(mesh):
    grid = Mesh(mesh.devices.reshape(NZ, NC, NX, NY), ("z", "core", "x", "y"))
    split = P(("x", "y"), ("z", "core"), None)
    return jax.shard_map(
        body,
        mesh=grid,
        in_specs=(split, split, split, P(), split, split),
        out_specs=(split, split, P(("x", "y"), None, None)),
        check_vma=False,
    )
```

```python
import functools
import math

import jax
import jax.numpy as jnp
from jax import lax
from jax.experimental import pallas as pl
from jax.experimental.pallas import tpu as pltpu
from jax.sharding import Mesh, PartitionSpec as P

coef_a = 3.4445
coef_b = -4.775
coef_c = 2.0315
beta_mom = 0.95
learn_rate = 0.02
norm_eps = 1e-07

NZ, NC, NX, NY = 8, 2, 4, 4
COPY_ORDER = (4, 3, -3, 2, -2, 1, -1, 0)
BF = jnp.bfloat16
F32 = jnp.float32


def swap(value):
    return lax.ppermute(value, "core", [(0, 1), (1, 0)])


def up(value):
    return lax.ppermute(value, "z", [(i, (i + 1) % NZ) for i in range(NZ)])


def down(value):
    return lax.ppermute(value, "z", [((i + 1) % NZ, i) for i in range(NZ)])


def shift(value, axis, offset):
    return lax.ppermute(value, axis, [(i, (i + offset) % 4) for i in range(4)])


def add_bf(left, right):
    return (left.astype(F32) + right.astype(F32)).astype(BF)


SMEM = pl.BlockSpec(memory_space=pltpu.SMEM)
VMEM = pl.BlockSpec(memory_space=pltpu.VMEM)
ANY = pl.BlockSpec(memory_space=pl.ANY)
HBM = pl.BlockSpec(memory_space=pltpu.HBM)


def small(limit=8):
    return pltpu.CompilerParams(vmem_limit_bytes=limit * 1024 * 1024)


def place_kernel(offsets, aliased, here_ref, *refs):
    if aliased:
        refs = refs[1:]
    own, other, out_ref, sems = refs
    rows = own.shape[0] // len(offsets)
    z, core = here_ref[0], here_ref[1]
    copies = []
    for index, offset in enumerate(offsets):
        there = NC * lax.rem(z + NZ + offset, NZ)
        for side, stack in enumerate((own, other)):
            row = pl.multiple_of((there + (1 - core if side else core)) * rows, rows)
            copies.append(
                pltpu.make_async_copy(
                    stack.at[pl.ds(index * rows, rows), :],
                    out_ref.at[pl.ds(row, rows), :],
                    sems.at[2 * index + side],
                )
            )
    for copy in copies:
        copy.start()
    for copy in copies:
        copy.wait()


def place(here, offsets, own, other, shape, before=None):
    aliased = before is not None
    return pl.pallas_call(
        functools.partial(place_kernel, offsets, aliased),
        out_shape=jax.ShapeDtypeStruct(shape, own.dtype),
        in_specs=[SMEM] + ([ANY] if aliased else []) + [VMEM] * 2,
        out_specs=ANY,
        scratch_shapes=[pltpu.SemaphoreType.DMA((2 * len(offsets),))],
        input_output_aliases={1: 0} if aliased else {},
        compiler_params=small(),
        name="place",
    )(here, *([before] if aliased else []), own, other)


def bucket_kernel(here_ref, list_ref, *refs):
    pieces, outs = refs[:NY], refs[NY:]
    x, y = here_ref[2], here_ref[3]
    totals = [jnp.zeros(outs[0].shape, F32) for _ in range(NX)]
    for offset, piece in enumerate(pieces):
        target = list_ref[x * NY + lax.rem(y + NY - offset, NY)]
        value = piece[...].astype(F32)
        for ahead in range(NX):
            fits = target == lax.rem(x + ahead, NX) * NY + y
            totals[ahead] = totals[ahead] + jnp.where(fits, value, 0.0)
    for out, total in zip(outs, totals, strict=True):
        out[...] = total.astype(out.dtype)


def buckets(here, copy_list, pieces):
    shape = pieces[0].shape
    return pl.pallas_call(
        bucket_kernel,
        out_shape=tuple(jax.ShapeDtypeStruct(shape, BF if k else F32) for k in range(NX)),
        in_specs=[SMEM, SMEM] + [VMEM] * NY,
        out_specs=(VMEM,) * NX,
        compiler_params=small(),
        name="buckets",
    )(here, copy_list, *pieces)


def wanted_kernel(here_ref, list_ref, *refs):
    pieces, outs = refs[:NX], refs[NX:]
    x, y = here_ref[2], here_ref[3]
    for offset, out in enumerate(outs):
        source = list_ref[x * NY + lax.rem(y + offset, NY)]
        behind = lax.rem(x + NX - lax.div(source, NY), NX)
        for k, piece in enumerate(pieces):

            @pl.when(behind == k)
            def _():
                out[...] = piece[...]


def wanted(here, copy_list, pieces):
    shape = pieces[0].shape
    return pl.pallas_call(
        wanted_kernel,
        out_shape=(jax.ShapeDtypeStruct(shape, BF),) * NY,
        in_specs=[SMEM, SMEM] + [VMEM] * NX,
        out_specs=(VMEM,) * NY,
        compiler_params=small(),
        name="wanted",
    )(here, copy_list, *pieces)


def pick_kernel(here_ref, list_ref, *refs):
    pieces, out = refs[:NY], refs[NY]
    x, y = here_ref[2], here_ref[3]
    behind = lax.rem(y + NY - lax.rem(list_ref[x * NY + y], NY), NY)
    for k, piece in enumerate(pieces):

        @pl.when(behind == k)
        def _():
            out[...] = piece[...]


def pick(here, copy_list, pieces):
    return pl.pallas_call(
        pick_kernel,
        out_shape=jax.ShapeDtypeStruct(pieces[0].shape, BF),
        in_specs=[SMEM, SMEM] + [VMEM] * NY,
        out_specs=VMEM,
        compiler_params=small(),
        name="pick",
    )(here, copy_list, *pieces)


PAD = 16


def give_kernel(here_ref, counts_ref, acts_ref, grads_ref, out_ref, sems):
    tok_rows, width = grads_ref.shape
    rows = acts_ref.shape[1] // (NZ * NC)
    core = here_ref[1]
    copies = [
        pltpu.make_async_copy(grads_ref, out_ref.at[pl.ds(0, tok_rows), pl.ds(0, width)], sems.at[NZ])
    ]
    for there in range(NZ):
        start = pl.multiple_of((NC * there + 1 - core) * rows, rows)
        copies.append(
            pltpu.make_async_copy(
                acts_ref.at[:, pl.ds(start, rows)],
                out_ref.at[pl.ds(0, tok_rows), pl.ds(width + there * rows, rows)],
                sems.at[there],
            )
        )
    for copy in copies:
        copy.start()
    for index in range(2):
        count = jnp.full((PAD, width), counts_ref[0, index], jnp.int32)
        start = tok_rows + index * PAD
        out_ref[start : start + PAD, :width] = count.astype(F32).astype(BF)
    for copy in copies:
        copy.wait()


def give(here, counts, acts, grads):
    tok_rows, width = grads.shape
    return pl.pallas_call(
        give_kernel,
        out_shape=jax.ShapeDtypeStruct((tok_rows + 2 * PAD, width + acts.shape[1] // NC), BF),
        in_specs=[SMEM, SMEM, HBM, HBM],
        out_specs=VMEM,
        scratch_shapes=[pltpu.SemaphoreType.DMA((NZ + 1,))],
        compiler_params=small(56),
        name="give",
    )(here, counts, acts, grads)


def terms_kernel(which, here_ref, counts_ref, acts_ref, got_ref, grads_ref, *out_refs):
    tok_rows, width = grads_ref.shape
    rows = acts_ref.shape[1] // (NZ * NC)
    z, core = here_ref[0], here_ref[1]
    if which:
        order = [lax.rem(z + NZ + offset, NZ) for offset in COPY_ORDER]
    else:
        order = list(range(NZ))

    def columns(ref, start):
        return ref[:tok_rows, pl.ds(pl.multiple_of(start, rows), rows)]

    slot = lax.broadcasted_iota(jnp.int32, (tok_rows, width), 0)
    home, copy = counts_ref[0, 0], counts_ref[0, 1]
    low, high = (home, home + copy) if which else (0, home)
    right = jnp.where((slot >= low) & (slot < high), grads_ref[...].astype(F32), 0.0).astype(BF)
    left = jnp.concatenate(
        [columns(acts_ref, (NC * there + core) * rows) for there in order], axis=1
    )
    contract = (((0,), (0,)), ((), ()))
    total = lax.dot_general(left, right, contract, preferred_element_type=F32)
    place = slot.astype(F32)
    home = got_ref[tok_rows : tok_rows + 1, :width].astype(F32)
    copy = got_ref[tok_rows + PAD : tok_rows + PAD + 1, :width].astype(F32)
    mask = (place >= home) & (place < home + copy) if which else place < home
    right = jnp.where(mask, got_ref[:tok_rows, :width].astype(F32), 0.0).astype(BF)
    left = jnp.concatenate(
        [columns(got_ref, width + there * rows) for there in order], axis=1
    )
    total = total + lax.dot_general(left, right, contract, preferred_element_type=F32)
    for index, out_ref in enumerate(out_refs):
        size = out_ref.shape[0]
        out_ref[...] = total[index * size : (index + 1) * size].astype(BF)


def terms(here, counts, acts, got, grads, which):
    tok_rows, width = grads.shape
    rows = acts.shape[1] // (NZ * NC)
    sizes = [rows] * NZ if which else [rows * NZ]
    return pl.pallas_call(
        functools.partial(terms_kernel, which),
        out_shape=tuple(jax.ShapeDtypeStruct((size, width), BF) for size in sizes),
        in_specs=[SMEM, SMEM] + [VMEM] * 3,
        out_specs=(VMEM,) * len(sizes),
        compiler_params=small(20),
        cost_estimate=pl.CostEstimate(
            flops=4 * tok_rows * rows * NZ * width,
            bytes_accessed=4 * tok_rows * rows * NZ,
            transcendentals=0,
        ),
        name="copy_terms" if which else "home_terms",
    )(here, counts, acts, got, grads)


def halves(value):
    high = value.astype(BF)
    return high, (value - high.astype(F32)).astype(BF)


def dot(left, right):
    return jnp.dot(left, right, preferred_element_type=F32)


def newton_kernel(
    factor,
    gram_ref,
    mine_ref,
    other_ref,
    mom_ref,
    weight_ref,
    update_ref,
    fresh_ref,
    s_hi,
    s_lo,
    k_hi,
    k_lo,
    t_hi,
    t_lo,
    iterate_ref,
):
    width = gram_ref.shape[0]
    tile = width // 3
    spans = [slice(i * tile, (i + 1) * tile) for i in range(3)]
    pairs = [(i, j) for i in range(3) for j in range(i, 3)]

    def store(hi, lo, i, j, value):
        hi[spans[i], spans[j]], lo[spans[i], spans[j]] = halves(value)
        if i != j:
            hi[spans[j], spans[i]], lo[spans[j], spans[i]] = halves(value.T)

    def load(hi, lo, i, j):
        return hi[spans[i], spans[j]].astype(F32) + lo[spans[i], spans[j]].astype(F32)

    def product(left, right, i, j):
        (l_hi, l_lo), (r_hi, r_lo) = left, right
        rows, cols = spans[i], spans[j]
        out = dot(l_hi[rows, :], r_lo[:, cols]) + dot(l_lo[rows, :], r_hi[:, cols])
        return out + dot(l_hi[rows, :], r_hi[:, cols])

    def times(value, right):
        hi, lo = halves(value)
        r_hi, r_lo = right
        both = dot(jnp.concatenate([hi, lo], axis=0), r_hi[...])
        rows = value.shape[0]
        return both[:rows] + (both[rows:] + dot(hi, r_lo[...]))

    same = lax.broadcasted_iota(jnp.int32, (tile, tile), 0) == lax.broadcasted_iota(
        jnp.int32, (tile, tile), 1
    )
    last = jnp.concatenate([mine_ref[...], other_ref[...]], axis=0)
    gram = gram_ref[...] + lax.dot_general(
        last, last, (((0,), (0,)), ((), ())), preferred_element_type=F32
    )
    total = jnp.zeros((1, 1), F32)
    for span in spans:
        on = jnp.where(same, gram[span, span], 0.0)
        total = total + jnp.sum(jnp.sum(on, axis=1, keepdims=True), axis=0, keepdims=True)
    scale = 1.0 / (jnp.sqrt(total) + norm_eps)
    for span in spans:
        s_hi[span, :], s_lo[span, :] = halves(gram[span, :] * scale * scale)
    iterate_ref[...] = mom_ref[...] * scale
    s, k, t = (s_hi, s_lo), (k_hi, k_lo), (t_hi, t_lo)

    @pl.loop(0, 2)
    def _(step):
        for i, j in pairs:
            store(*k, i, j, coef_b * load(*s, i, j) + coef_c * product(s, s, i, j))
        iterate_ref[...] = coef_a * iterate_ref[...] + times(iterate_ref[...], k)
        for i, j in pairs:
            store(*t, i, j, coef_a * load(*s, i, j) + product(s, k, i, j))
        for i, j in pairs:
            store(*s, i, j, coef_a * load(*t, i, j) + product(t, k, i, j))

    iterate = iterate_ref[...]
    side = times(iterate, s)
    iterate = coef_a * iterate + (coef_b * side + coef_c * times(side, s))
    update = factor * iterate
    update_ref[...] = update
    fresh_ref[...] = (weight_ref[...].astype(F32) - learn_rate * update).astype(BF)


def newton_schulz(gram, mine, other, mom, weight, longest):
    rows, width = mom.shape
    vmem = pl.BlockSpec(memory_space=pltpu.VMEM)
    return pl.pallas_call(
        functools.partial(newton_kernel, 0.2 * math.sqrt(longest)),
        out_shape=(
            jax.ShapeDtypeStruct((rows, width), F32),
            jax.ShapeDtypeStruct((rows, width), BF),
        ),
        in_specs=[vmem] * 5,
        out_specs=(vmem, vmem),
        scratch_shapes=[pltpu.VMEM((width, width), BF)] * 6 + [pltpu.VMEM((rows, width), F32)],
        compiler_params=small(20),
        cost_estimate=pl.CostEstimate(
            flops=28 * width**3, bytes_accessed=8 * width * width, transcendentals=0
        ),
        name="newton_schulz",
    )(gram, mine, other, mom, weight)


def after(value, *others):
    return lax.optimization_barrier((value, *others))


def ring(block, work):
    up1 = up(block)
    other = swap(block)
    block1, _ = after(block, other)
    down1 = down(block1)
    up2, down2 = up(up1), down(down1)
    stack = jnp.concatenate([block, up1, down1], axis=0)
    other = jnp.concatenate([other, swap(stack[block.shape[0]:])], axis=0)
    state = work((0, -1, 1), stack, other, None)
    up3, down3 = up(up2), down(down2)
    up3, state = after(up3, state)
    far = up(up3)
    stack = jnp.concatenate([up2, down2, up3, down3], axis=0)
    state = work((-2, 2, -3, 3), stack, swap(stack), state)
    far, state = after(far, state)
    return far, swap(far), state


def body(tokens_in, out_grads, counts, copy_list, weights, momentum):
    acts = tokens_in[0]
    grads = out_grads[0]
    model_width = acts.shape[1]
    width = grads.shape[1]
    here = jnp.stack([lax.axis_index(name) for name in ("z", "core", "x", "y")]).astype(jnp.int32)

    got = swap(give(here, counts[0], acts, grads))
    far, up3, down3, up2, down2, up1, down1, mine = terms(here, counts[0], acts, got, grads, 1)
    (home_terms,) = terms(here, counts[0], acts, got, grads, 0)

    down3, home_terms = after(down3, home_terms)
    going_up = add_bf(up3, up(far))
    going_up, going_down = add_bf(up2, up(going_up)), add_bf(down2, down(down3))
    going_up, going_down, home_terms = after(going_up, going_down, home_terms)
    home_sum = lax.psum_scatter(home_terms, "z", scatter_dimension=0, tiled=True)
    going_up, going_down = add_bf(up1, up(going_up)), add_bf(down1, down(going_down))
    going_up, going_down = up(going_up), down(going_down)
    copy_sum = (mine.astype(F32) + going_up.astype(F32) + going_down.astype(F32)).astype(BF)

    pieces = [copy_sum] + [shift(copy_sum, "y", offset) for offset in range(1, NY)]
    copies, *sent = buckets(here, copy_list, pieces)
    for ahead in range(1, NX):
        copies = copies + shift(sent[ahead - 1], "x", ahead).astype(F32)
    fresh_mom = beta_mom * momentum[0] + (home_sum.astype(F32) + copies)

    def add_gram(offsets, own, other, gram):
        for stack in (own, other):
            part = lax.dot_general(
                stack, stack, (((0,), (0,)), ((), ())), preferred_element_type=F32
            )
            gram = part if gram is None else gram + part
        return gram

    own, other, gram = ring(fresh_mom.astype(BF), add_gram)
    update, fresh = newton_schulz(
        gram, own, other, fresh_mom, weights[0], max(model_width, width)
    )

    pieces = [fresh] + [shift(fresh, "x", offset) for offset in range(1, NX)]
    kept, *sent = wanted(here, copy_list, pieces)
    pieces = [kept] + [shift(sent[offset - 1], "y", offset) for offset in range(1, NY)]
    replica = pick(here, copy_list, pieces)

    shape = (model_width, width)

    def put(offsets, own, other, full):
        return place(here, offsets, own, other, shape, full)

    own, other, full = ring(replica, put)
    full = put((4,), own, other, full)
    return (fresh_mom[None], update[None], full[None])


def solution(mesh):
    grid = Mesh(mesh.devices.reshape(NZ, NC, NX, NY), ("z", "core", "x", "y"))
    split = P(("x", "y"), ("z", "core"), None)
    return jax.shard_map(
        body,
        mesh=grid,
        in_specs=(split, split, split, P(), split, split),
        out_specs=(split, split, P(("x", "y"), None, None)),
        check_vma=False,
    )
```

```python
import functools
import math

import jax
import jax.numpy as jnp
from jax import lax
from jax.experimental import pallas as pl
from jax.experimental.pallas import tpu as pltpu
from jax.sharding import Mesh, PartitionSpec as P

coef_a = 3.4445
coef_b = -4.775
coef_c = 2.0315
beta_mom = 0.95
learn_rate = 0.02
norm_eps = 1e-07

NZ, NC, NX, NY = 8, 2, 4, 4
COPY_ORDER = (4, 3, -3, 2, -2, 1, -1, 0)
BF = jnp.bfloat16
F32 = jnp.float32


def swap(value):
    return lax.ppermute(value, "core", [(0, 1), (1, 0)])


def up(value):
    return lax.ppermute(value, "z", [(i, (i + 1) % NZ) for i in range(NZ)])


def down(value):
    return lax.ppermute(value, "z", [((i + 1) % NZ, i) for i in range(NZ)])


def add_bf(left, right):
    return (left.astype(F32) + right.astype(F32)).astype(BF)


SMEM = pl.BlockSpec(memory_space=pltpu.SMEM)
VMEM = pl.BlockSpec(memory_space=pltpu.VMEM)
ANY = pl.BlockSpec(memory_space=pl.ANY)
HBM = pl.BlockSpec(memory_space=pltpu.HBM)


def small(limit=8):
    return pltpu.CompilerParams(vmem_limit_bytes=limit * 1024 * 1024)


def place_kernel(step_ref, here_ref, own, other, before, out_ref, sems):
    del before
    rows = own.shape[0] // 2
    z, core, step = here_ref[0], here_ref[1], step_ref[0]
    copies = []
    for index, there in enumerate((lax.rem(z + NZ - step, NZ), lax.rem(z + step, NZ))):
        for side, stack in enumerate((own, other)):
            row = pl.multiple_of((NC * there + (1 - core if side else core)) * rows, rows)
            copies.append(
                pltpu.make_async_copy(
                    stack.at[pl.ds(index * rows, rows), :],
                    out_ref.at[pl.ds(row, rows), :],
                    sems.at[2 * index + side],
                )
            )
    twice = lax.rem(step, 4) != 0
    for copy in copies[:2]:
        copy.start()

    @pl.when(twice)
    def _():
        for copy in copies[2:]:
            copy.start()
        for copy in copies[2:]:
            copy.wait()

    for copy in copies[:2]:
        copy.wait()


def place(here, step, own, other, before):
    return pl.pallas_call(
        place_kernel,
        out_shape=jax.ShapeDtypeStruct(before.shape, before.dtype),
        in_specs=[SMEM, SMEM, VMEM, VMEM, ANY],
        out_specs=ANY,
        scratch_shapes=[pltpu.SemaphoreType.DMA((4,))],
        input_output_aliases={4: 0},
        compiler_params=small(),
        name="place",
    )(jnp.reshape(step, (1,)).astype(jnp.int32), here, own, other, before)


def empty_kernel(out_ref):
    del out_ref


def empty(shape, dtype):
    return pl.pallas_call(
        empty_kernel, out_shape=jax.ShapeDtypeStruct(shape, dtype), out_specs=ANY, name="empty"
    )()


def bucket_kernel(here_ref, list_ref, pieces, out):
    x, y = here_ref[2], here_ref[3]
    targets = [list_ref[x * NY + k] for k in range(NY)]
    values = [pieces[k].astype(F32) for k in range(NY)]
    for there in range(NX):
        total = jnp.zeros(out.shape[1:], F32)
        for target, value in zip(targets, values, strict=True):
            total = total + jnp.where(target == there * NY + y, value, 0.0)
        out[there] = total.astype(BF)


def wanted_kernel(here_ref, list_ref, pieces, out):
    x = here_ref[2]
    for there in range(NY):
        out[there] = pieces[lax.div(list_ref[x * NY + there], NY)]


def pick_kernel(here_ref, list_ref, pieces, out):
    x, y = here_ref[2], here_ref[3]
    out[...] = pieces[lax.rem(list_ref[x * NY + y], NY)]


def by_list(kernel, here, copy_list, pieces, shape):
    return pl.pallas_call(
        kernel,
        out_shape=jax.ShapeDtypeStruct(shape, BF),
        in_specs=[SMEM, SMEM, VMEM],
        out_specs=VMEM,
        compiler_params=small(),
        name=kernel.__name__,
    )(here, copy_list, pieces)


def gather4(value, axis):
    return exchange4(jnp.broadcast_to(value[None], (4, *value.shape)), axis)


def exchange4(values, axis):
    return lax.all_to_all(values, axis, 0, 0, tiled=True)


PAD = 16


def give_kernel(here_ref, counts_ref, acts_ref, grads_ref, out_ref, sems):
    tok_rows, width = grads_ref.shape
    rows = acts_ref.shape[1] // (NZ * NC)
    core = here_ref[1]
    copies = [
        pltpu.make_async_copy(grads_ref, out_ref.at[pl.ds(0, tok_rows), pl.ds(0, width)], sems.at[NZ])
    ]
    for there in range(NZ):
        start = pl.multiple_of((NC * there + 1 - core) * rows, rows)
        copies.append(
            pltpu.make_async_copy(
                acts_ref.at[:, pl.ds(start, rows)],
                out_ref.at[pl.ds(0, tok_rows), pl.ds(width + there * rows, rows)],
                sems.at[there],
            )
        )
    for copy in copies:
        copy.start()
    for index in range(2):
        count = jnp.full((PAD, width), counts_ref[0, index], jnp.int32)
        start = tok_rows + index * PAD
        out_ref[start : start + PAD, :width] = count.astype(F32).astype(BF)
    for copy in copies:
        copy.wait()


def give(here, counts, acts, grads):
    tok_rows, width = grads.shape
    return pl.pallas_call(
        give_kernel,
        out_shape=jax.ShapeDtypeStruct((tok_rows + 2 * PAD, width + acts.shape[1] // NC), BF),
        in_specs=[SMEM, SMEM, HBM, HBM],
        out_specs=VMEM,
        scratch_shapes=[pltpu.SemaphoreType.DMA((NZ + 1,))],
        compiler_params=small(56),
        name="give",
    )(here, counts, acts, grads)


def terms_kernel(which, here_ref, counts_ref, acts_ref, got_ref, grads_ref, *out_refs):
    tok_rows, width = grads_ref.shape
    rows = acts_ref.shape[1] // (NZ * NC)
    z, core = here_ref[0], here_ref[1]
    if which:
        order = [lax.rem(z + NZ + offset, NZ) for offset in COPY_ORDER]
    else:
        order = list(range(NZ))

    def columns(ref, start):
        return ref[:tok_rows, pl.ds(pl.multiple_of(start, rows), rows)]

    slot = lax.broadcasted_iota(jnp.int32, (tok_rows, width), 0)
    home, copy = counts_ref[0, 0], counts_ref[0, 1]
    low, high = (home, home + copy) if which else (0, home)
    right = jnp.where((slot >= low) & (slot < high), grads_ref[...].astype(F32), 0.0).astype(BF)
    left = jnp.concatenate(
        [columns(acts_ref, (NC * there + core) * rows) for there in order], axis=1
    )
    contract = (((0,), (0,)), ((), ()))
    total = lax.dot_general(left, right, contract, preferred_element_type=F32)
    place = slot.astype(F32)
    home = got_ref[tok_rows : tok_rows + 1, :width].astype(F32)
    copy = got_ref[tok_rows + PAD : tok_rows + PAD + 1, :width].astype(F32)
    mask = (place >= home) & (place < home + copy) if which else place < home
    right = jnp.where(mask, got_ref[:tok_rows, :width].astype(F32), 0.0).astype(BF)
    left = jnp.concatenate(
        [columns(got_ref, width + there * rows) for there in order], axis=1
    )
    total = total + lax.dot_general(left, right, contract, preferred_element_type=F32)
    for index, out_ref in enumerate(out_refs):
        size = out_ref.shape[0]
        out_ref[...] = total[index * size : (index + 1) * size].astype(BF)


def terms(here, counts, acts, got, grads, which):
    tok_rows, width = grads.shape
    rows = acts.shape[1] // (NZ * NC)
    sizes = [rows] * NZ if which else [rows * NZ]
    return pl.pallas_call(
        functools.partial(terms_kernel, which),
        out_shape=tuple(jax.ShapeDtypeStruct((size, width), BF) for size in sizes),
        in_specs=[SMEM, SMEM] + [VMEM] * 3,
        out_specs=(VMEM,) * len(sizes),
        compiler_params=small(20),
        cost_estimate=pl.CostEstimate(
            flops=4 * tok_rows * rows * NZ * width,
            bytes_accessed=4 * tok_rows * rows * NZ,
            transcendentals=0,
        ),
        name="copy_terms" if which else "home_terms",
    )(here, counts, acts, got, grads)


def halves(value):
    high = value.astype(BF)
    return high, (value - high.astype(F32)).astype(BF)


def dot(left, right):
    return jnp.dot(left, right, preferred_element_type=F32)


def newton_kernel(
    factor, gram_ref, mine_ref, other_ref, mom_ref, weight_ref, update_ref, fresh_ref, hi, lo, iterate_ref
):
    width = gram_ref.shape[0]
    tile = width // 3
    spans = [slice(i * tile, (i + 1) * tile) for i in range(3)]
    pairs = [(i, j) for i in range(3) for j in range(i, 3)]

    def store(to, i, j, value):
        hi[to, spans[i], spans[j]], lo[to, spans[i], spans[j]] = halves(value)
        if i != j:
            hi[to, spans[j], spans[i]], lo[to, spans[j], spans[i]] = halves(value.T)

    def load(at, i, j):
        return hi[at, spans[i], spans[j]].astype(F32) + lo[at, spans[i], spans[j]].astype(F32)

    def product(left, right, i, j):
        rows, cols = spans[i], spans[j]
        out = dot(hi[left, rows, :], lo[right, :, cols]) + dot(lo[left, rows, :], hi[right, :, cols])
        return out + dot(hi[left, rows, :], hi[right, :, cols])

    def times(value, right):
        high, low = halves(value)
        both = dot(jnp.concatenate([high, low], axis=0), hi[right])
        rows = value.shape[0]
        return both[:rows] + (both[rows:] + dot(high, lo[right]))

    same = lax.broadcasted_iota(jnp.int32, (tile, tile), 0) == lax.broadcasted_iota(
        jnp.int32, (tile, tile), 1
    )
    last = jnp.concatenate([mine_ref[...], other_ref[...]], axis=0)
    gram = gram_ref[...] + lax.dot_general(
        last, last, (((0,), (0,)), ((), ())), preferred_element_type=F32
    )
    total = jnp.zeros((1, 1), F32)
    for span in spans:
        on = jnp.where(same, gram[span, span], 0.0)
        total = total + jnp.sum(jnp.sum(on, axis=1, keepdims=True), axis=0, keepdims=True)
    scale = 1.0 / (jnp.sqrt(total) + norm_eps)
    for span in spans:
        hi[0, span, :], lo[0, span, :] = halves(gram[span, :] * scale * scale)
    iterate_ref[...] = mom_ref[...] * scale

    @pl.loop(0, 6)
    def _(index):
        stage = lax.rem(index, 3)
        left = jnp.where(stage == 2, 2, 0)
        right = jnp.where(stage == 0, 0, 1)
        to = lax.rem(stage + 1, 3)
        keep = jnp.where(stage == 0, coef_b, coef_a)
        gain = jnp.where(stage == 0, coef_c, 1.0)
        for i, j in pairs:
            store(to, i, j, keep * load(left, i, j) + gain * product(left, right, i, j))

        @pl.when(stage == 0)
        def _():
            iterate_ref[...] = coef_a * iterate_ref[...] + times(iterate_ref[...], 1)

    iterate = iterate_ref[...]
    side = times(iterate, 0)
    iterate = coef_a * iterate + (coef_b * side + coef_c * times(side, 0))
    update = factor * iterate
    update_ref[...] = update
    fresh_ref[...] = (weight_ref[...].astype(F32) - learn_rate * update).astype(BF)


def newton_schulz(gram, mine, other, mom, weight, longest):
    rows, width = mom.shape
    vmem = pl.BlockSpec(memory_space=pltpu.VMEM)
    return pl.pallas_call(
        functools.partial(newton_kernel, 0.2 * math.sqrt(longest)),
        out_shape=(
            jax.ShapeDtypeStruct((rows, width), F32),
            jax.ShapeDtypeStruct((rows, width), BF),
        ),
        in_specs=[vmem] * 5,
        out_specs=(vmem, vmem),
        scratch_shapes=[pltpu.VMEM((3, width, width), BF)] * 2 + [pltpu.VMEM((rows, width), F32)],
        compiler_params=small(20),
        cost_estimate=pl.CostEstimate(
            flops=28 * width**3, bytes_accessed=8 * width * width, transcendentals=0
        ),
        name="newton_schulz",
    )(gram, mine, other, mom, weight)


def after(value, *others):
    return lax.optimization_barrier((value, *others))


def ring(block, work, state):
    def one(step, carry):
        below, above, state = carry
        stack = jnp.concatenate([below, above], axis=0)
        below, above = up(below), down(above)
        return below, above, work(step, stack, swap(stack), state)

    far, _, state = lax.fori_loop(0, 4, one, (block, block, state))
    return far, swap(far), state


def body(tokens_in, out_grads, counts, copy_list, weights, momentum):
    acts = tokens_in[0]
    grads = out_grads[0]
    model_width = acts.shape[1]
    width = grads.shape[1]
    here = jnp.stack([lax.axis_index(name) for name in ("z", "core", "x", "y")]).astype(jnp.int32)

    got = swap(give(here, counts[0], acts, grads))
    far, up3, down3, up2, down2, up1, down1, mine = terms(here, counts[0], acts, got, grads, 1)
    (home_terms,) = terms(here, counts[0], acts, got, grads, 0)

    down3, home_terms = after(down3, home_terms)
    going_up = add_bf(up3, up(far))
    going_up, home_terms = after(going_up, home_terms)
    going_up, going_down = add_bf(up2, up(going_up)), add_bf(down2, down(down3))
    home_sum = lax.psum_scatter(home_terms, "z", scatter_dimension=0, tiled=True)
    going_up, going_down = add_bf(up1, up(going_up)), add_bf(down1, down(going_down))
    going_up, going_down = up(going_up), down(going_down)
    copy_sum = (mine.astype(F32) + going_up.astype(F32) + going_down.astype(F32)).astype(BF)

    four = (NX, *copy_sum.shape)
    sent = by_list(bucket_kernel, here, copy_list, gather4(copy_sum, "y"), four)
    sent, home_sum = after(sent, home_sum)
    copies = jnp.sum(exchange4(sent, "x").astype(F32), axis=0)
    fresh_mom = beta_mom * momentum[0] + (home_sum.astype(F32) + copies)

    def add_gram(step, own, other, gram):
        stack = jnp.concatenate([own, other], axis=0)
        part = lax.dot_general(
            stack, stack, (((0,), (0,)), ((), ())), preferred_element_type=F32
        )
        return gram + jnp.where(step == 0, 0.5, 1.0) * part

    own, other, gram = ring(fresh_mom.astype(BF), add_gram, jnp.zeros((width, width), F32))
    update, fresh = newton_schulz(
        gram, own, other, fresh_mom, weights[0], max(model_width, width)
    )

    sent = by_list(wanted_kernel, here, copy_list, gather4(fresh, "x"), four)
    replica = by_list(pick_kernel, here, copy_list, exchange4(sent, "y"), fresh.shape)

    def put(step, own, other, full):
        return place(here, step, own, other, full)

    own, other, full = ring(replica, put, empty((model_width, width), BF))
    full = put(4, jnp.concatenate([own, own], axis=0), jnp.concatenate([other, other], axis=0), full)
    return (fresh_mom[None], update[None], full[None])


def solution(mesh):
    grid = Mesh(mesh.devices.reshape(NZ, NC, NX, NY), ("z", "core", "x", "y"))
    split = P(("x", "y"), ("z", "core"), None)
    return jax.shard_map(
        body,
        mesh=grid,
        in_specs=(split, split, split, P(), split, split),
        out_specs=(split, split, P(("x", "y"), None, None)),
        check_vma=False,
    )
```

```python
import functools
import math

import jax
import jax.numpy as jnp
from jax import lax
from jax.experimental import pallas as pl
from jax.experimental.pallas import tpu as pltpu
from jax.sharding import Mesh, PartitionSpec as P

coef_a = 3.4445
coef_b = -4.775
coef_c = 2.0315
beta_mom = 0.95
learn_rate = 0.02
norm_eps = 1e-07

NZ, NC, NX, NY = 8, 2, 4, 4
COPY_ORDER = (4, 3, -3, 2, -2, 1, -1, 0)
BF = jnp.bfloat16
F32 = jnp.float32


def swap(value):
    return lax.ppermute(value, "core", [(0, 1), (1, 0)])


def up(value):
    return lax.ppermute(value, "z", [(i, (i + 1) % NZ) for i in range(NZ)])


def down(value):
    return lax.ppermute(value, "z", [((i + 1) % NZ, i) for i in range(NZ)])


def shift(value, axis, offset):
    return lax.ppermute(value, axis, [(i, (i + offset) % 4) for i in range(4)])


def add_bf(left, right):
    return (left.astype(F32) + right.astype(F32)).astype(BF)


SMEM = pl.BlockSpec(memory_space=pltpu.SMEM)
VMEM = pl.BlockSpec(memory_space=pltpu.VMEM)
ANY = pl.BlockSpec(memory_space=pl.ANY)
HBM = pl.BlockSpec(memory_space=pltpu.HBM)


def small(limit=8):
    return pltpu.CompilerParams(vmem_limit_bytes=limit * 1024 * 1024)


def place_kernel(step_ref, here_ref, own, other, before, out_ref, sems):
    del before
    rows = own.shape[0] // 2
    z, core, step = here_ref[0], here_ref[1], step_ref[0]
    copies = []
    for index, there in enumerate((lax.rem(z + NZ - step, NZ), lax.rem(z + step, NZ))):
        for side, stack in enumerate((own, other)):
            row = pl.multiple_of((NC * there + (1 - core if side else core)) * rows, rows)
            copies.append(
                pltpu.make_async_copy(
                    stack.at[pl.ds(index * rows, rows), :],
                    out_ref.at[pl.ds(row, rows), :],
                    sems.at[2 * index + side],
                )
            )
    twice = lax.rem(step, 4) != 0
    for copy in copies[:2]:
        copy.start()

    @pl.when(twice)
    def _():
        for copy in copies[2:]:
            copy.start()
        for copy in copies[2:]:
            copy.wait()

    for copy in copies[:2]:
        copy.wait()


def place(here, step, own, other, before):
    return pl.pallas_call(
        place_kernel,
        out_shape=jax.ShapeDtypeStruct(before.shape, before.dtype),
        in_specs=[SMEM, SMEM, VMEM, VMEM, ANY],
        out_specs=ANY,
        scratch_shapes=[pltpu.SemaphoreType.DMA((4,))],
        input_output_aliases={4: 0},
        compiler_params=small(),
        name="place",
    )(jnp.reshape(step, (1,)).astype(jnp.int32), here, own, other, before)


def empty_kernel(out_ref):
    del out_ref


def empty(shape, dtype):
    return pl.pallas_call(
        empty_kernel, out_shape=jax.ShapeDtypeStruct(shape, dtype), out_specs=ANY, name="empty"
    )()


def bucket_kernel(here_ref, list_ref, *refs):
    pieces, outs = refs[:NY], refs[NY:]
    x, y = here_ref[2], here_ref[3]
    totals = [jnp.zeros(outs[0].shape, F32) for _ in range(NX)]
    for offset, piece in enumerate(pieces):
        target = list_ref[x * NY + lax.rem(y + NY - offset, NY)]
        value = piece[...].astype(F32)
        for ahead in range(NX):
            fits = target == lax.rem(x + ahead, NX) * NY + y
            totals[ahead] = totals[ahead] + jnp.where(fits, value, 0.0)
    for out, total in zip(outs, totals, strict=True):
        out[...] = total.astype(out.dtype)


def buckets(here, copy_list, pieces):
    shape = pieces[0].shape
    return pl.pallas_call(
        bucket_kernel,
        out_shape=tuple(jax.ShapeDtypeStruct(shape, BF if k else F32) for k in range(NX)),
        in_specs=[SMEM, SMEM] + [VMEM] * NY,
        out_specs=(VMEM,) * NX,
        compiler_params=small(),
        name="buckets",
    )(here, copy_list, *pieces)


def wanted_kernel(here_ref, list_ref, *refs):
    pieces, outs = refs[:NX], refs[NX:]
    x, y = here_ref[2], here_ref[3]
    for offset, out in enumerate(outs):
        source = list_ref[x * NY + lax.rem(y + offset, NY)]
        behind = lax.rem(x + NX - lax.div(source, NY), NX)
        for k, piece in enumerate(pieces):

            @pl.when(behind == k)
            def _():
                out[...] = piece[...]


def wanted(here, copy_list, pieces):
    shape = pieces[0].shape
    return pl.pallas_call(
        wanted_kernel,
        out_shape=(jax.ShapeDtypeStruct(shape, BF),) * NY,
        in_specs=[SMEM, SMEM] + [VMEM] * NX,
        out_specs=(VMEM,) * NY,
        compiler_params=small(),
        name="wanted",
    )(here, copy_list, *pieces)


def pick_kernel(here_ref, list_ref, *refs):
    pieces, out = refs[:NY], refs[NY]
    x, y = here_ref[2], here_ref[3]
    behind = lax.rem(y + NY - lax.rem(list_ref[x * NY + y], NY), NY)
    for k, piece in enumerate(pieces):

        @pl.when(behind == k)
        def _():
            out[...] = piece[...]


def pick(here, copy_list, pieces):
    return pl.pallas_call(
        pick_kernel,
        out_shape=jax.ShapeDtypeStruct(pieces[0].shape, BF),
        in_specs=[SMEM, SMEM] + [VMEM] * NY,
        out_specs=VMEM,
        compiler_params=small(),
        name="pick",
    )(here, copy_list, *pieces)


PAD = 16


def give_kernel(here_ref, counts_ref, acts_ref, grads_ref, out_ref, sems):
    tok_rows, width = grads_ref.shape
    rows = acts_ref.shape[1] // (NZ * NC)
    core = here_ref[1]
    copies = [
        pltpu.make_async_copy(grads_ref, out_ref.at[pl.ds(0, tok_rows), pl.ds(0, width)], sems.at[NZ])
    ]
    for there in range(NZ):
        start = pl.multiple_of((NC * there + 1 - core) * rows, rows)
        copies.append(
            pltpu.make_async_copy(
                acts_ref.at[:, pl.ds(start, rows)],
                out_ref.at[pl.ds(0, tok_rows), pl.ds(width + there * rows, rows)],
                sems.at[there],
            )
        )
    for copy in copies:
        copy.start()
    for index in range(2):
        count = jnp.full((PAD, width), counts_ref[0, index], jnp.int32)
        start = tok_rows + index * PAD
        out_ref[start : start + PAD, :width] = count.astype(F32).astype(BF)
    for copy in copies:
        copy.wait()


def give(here, counts, acts, grads):
    tok_rows, width = grads.shape
    return pl.pallas_call(
        give_kernel,
        out_shape=jax.ShapeDtypeStruct((tok_rows + 2 * PAD, width + acts.shape[1] // NC), BF),
        in_specs=[SMEM, SMEM, HBM, HBM],
        out_specs=VMEM,
        scratch_shapes=[pltpu.SemaphoreType.DMA((NZ + 1,))],
        compiler_params=small(56),
        name="give",
    )(here, counts, acts, grads)


def terms_kernel(which, here_ref, counts_ref, acts_ref, got_ref, grads_ref, *out_refs):
    tok_rows, width = grads_ref.shape
    rows = acts_ref.shape[1] // (NZ * NC)
    z, core = here_ref[0], here_ref[1]
    if which:
        order = [lax.rem(z + NZ + offset, NZ) for offset in COPY_ORDER]
    else:
        order = list(range(NZ))

    def columns(ref, start):
        return ref[:tok_rows, pl.ds(pl.multiple_of(start, rows), rows)]

    slot = lax.broadcasted_iota(jnp.int32, (tok_rows, width), 0)
    home, copy = counts_ref[0, 0], counts_ref[0, 1]
    low, high = (home, home + copy) if which else (0, home)
    right = jnp.where((slot >= low) & (slot < high), grads_ref[...].astype(F32), 0.0).astype(BF)
    left = jnp.concatenate(
        [columns(acts_ref, (NC * there + core) * rows) for there in order], axis=1
    )
    contract = (((0,), (0,)), ((), ()))
    total = lax.dot_general(left, right, contract, preferred_element_type=F32)
    place = slot.astype(F32)
    home = got_ref[tok_rows : tok_rows + 1, :width].astype(F32)
    copy = got_ref[tok_rows + PAD : tok_rows + PAD + 1, :width].astype(F32)
    mask = (place >= home) & (place < home + copy) if which else place < home
    right = jnp.where(mask, got_ref[:tok_rows, :width].astype(F32), 0.0).astype(BF)
    left = jnp.concatenate(
        [columns(got_ref, width + there * rows) for there in order], axis=1
    )
    total = total + lax.dot_general(left, right, contract, preferred_element_type=F32)
    for index, out_ref in enumerate(out_refs):
        size = out_ref.shape[0]
        out_ref[...] = total[index * size : (index + 1) * size].astype(BF)


def terms(here, counts, acts, got, grads, which):
    tok_rows, width = grads.shape
    rows = acts.shape[1] // (NZ * NC)
    sizes = [rows] * NZ if which else [rows * NZ]
    return pl.pallas_call(
        functools.partial(terms_kernel, which),
        out_shape=tuple(jax.ShapeDtypeStruct((size, width), BF) for size in sizes),
        in_specs=[SMEM, SMEM] + [VMEM] * 3,
        out_specs=(VMEM,) * len(sizes),
        compiler_params=small(20),
        cost_estimate=pl.CostEstimate(
            flops=4 * tok_rows * rows * NZ * width,
            bytes_accessed=4 * tok_rows * rows * NZ,
            transcendentals=0,
        ),
        name="copy_terms" if which else "home_terms",
    )(here, counts, acts, got, grads)


def halves(value):
    high = value.astype(BF)
    return high, (value - high.astype(F32)).astype(BF)


def dot(left, right):
    return jnp.dot(left, right, preferred_element_type=F32)


def newton_kernel(
    factor,
    gram_ref,
    mine_ref,
    other_ref,
    mom_ref,
    weight_ref,
    update_ref,
    fresh_ref,
    s_hi,
    s_lo,
    k_hi,
    k_lo,
    t_hi,
    t_lo,
    iterate_ref,
):
    width = gram_ref.shape[0]
    tile = width // 3
    spans = [slice(i * tile, (i + 1) * tile) for i in range(3)]
    pairs = [(i, j) for i in range(3) for j in range(i, 3)]

    def store(hi, lo, i, j, value):
        hi[spans[i], spans[j]], lo[spans[i], spans[j]] = halves(value)
        if i != j:
            hi[spans[j], spans[i]], lo[spans[j], spans[i]] = halves(value.T)

    def load(hi, lo, i, j):
        return hi[spans[i], spans[j]].astype(F32) + lo[spans[i], spans[j]].astype(F32)

    def product(left, right, i, j):
        (l_hi, l_lo), (r_hi, r_lo) = left, right
        rows, cols = spans[i], spans[j]
        out = dot(l_hi[rows, :], r_lo[:, cols]) + dot(l_lo[rows, :], r_hi[:, cols])
        return out + dot(l_hi[rows, :], r_hi[:, cols])

    def times(value, right):
        hi, lo = halves(value)
        r_hi, r_lo = right
        both = dot(jnp.concatenate([hi, lo], axis=0), r_hi[...])
        rows = value.shape[0]
        return both[:rows] + (both[rows:] + dot(hi, r_lo[...]))

    same = lax.broadcasted_iota(jnp.int32, (tile, tile), 0) == lax.broadcasted_iota(
        jnp.int32, (tile, tile), 1
    )
    last = jnp.concatenate([mine_ref[...], other_ref[...]], axis=0)
    gram = gram_ref[...] + lax.dot_general(
        last, last, (((0,), (0,)), ((), ())), preferred_element_type=F32
    )
    total = jnp.zeros((1, 1), F32)
    for span in spans:
        on = jnp.where(same, gram[span, span], 0.0)
        total = total + jnp.sum(jnp.sum(on, axis=1, keepdims=True), axis=0, keepdims=True)
    scale = 1.0 / (jnp.sqrt(total) + norm_eps)
    for span in spans:
        s_hi[span, :], s_lo[span, :] = halves(gram[span, :] * scale * scale)
    iterate_ref[...] = mom_ref[...] * scale
    s, k, t = (s_hi, s_lo), (k_hi, k_lo), (t_hi, t_lo)

    @pl.loop(0, 2)
    def _(step):
        for i, j in pairs:
            store(*k, i, j, coef_b * load(*s, i, j) + coef_c * product(s, s, i, j))
        iterate_ref[...] = coef_a * iterate_ref[...] + times(iterate_ref[...], k)
        for i, j in pairs:
            store(*t, i, j, coef_a * load(*s, i, j) + product(s, k, i, j))
        for i, j in pairs:
            store(*s, i, j, coef_a * load(*t, i, j) + product(t, k, i, j))

    iterate = iterate_ref[...]
    side = times(iterate, s)
    iterate = coef_a * iterate + (coef_b * side + coef_c * times(side, s))
    update = factor * iterate
    update_ref[...] = update
    fresh_ref[...] = (weight_ref[...].astype(F32) - learn_rate * update).astype(BF)


def newton_schulz(gram, mine, other, mom, weight, longest):
    rows, width = mom.shape
    vmem = pl.BlockSpec(memory_space=pltpu.VMEM)
    return pl.pallas_call(
        functools.partial(newton_kernel, 0.2 * math.sqrt(longest)),
        out_shape=(
            jax.ShapeDtypeStruct((rows, width), F32),
            jax.ShapeDtypeStruct((rows, width), BF),
        ),
        in_specs=[vmem] * 5,
        out_specs=(vmem, vmem),
        scratch_shapes=[pltpu.VMEM((width, width), BF)] * 6 + [pltpu.VMEM((rows, width), F32)],
        compiler_params=small(20),
        cost_estimate=pl.CostEstimate(
            flops=28 * width**3, bytes_accessed=8 * width * width, transcendentals=0
        ),
        name="newton_schulz",
    )(gram, mine, other, mom, weight)


def after(value, *others):
    return lax.optimization_barrier((value, *others))


def ring(block, work, state):
    def one(step, carry):
        below, above, state = carry
        stack = jnp.concatenate([below, above], axis=0)
        below, above = up(below), down(above)
        return below, above, work(step, stack, swap(stack), state)

    far, _, state = lax.fori_loop(0, 4, one, (block, block, state))
    return far, swap(far), state


def body(tokens_in, out_grads, counts, copy_list, weights, momentum):
    acts = tokens_in[0]
    grads = out_grads[0]
    model_width = acts.shape[1]
    width = grads.shape[1]
    here = jnp.stack([lax.axis_index(name) for name in ("z", "core", "x", "y")]).astype(jnp.int32)

    got = swap(give(here, counts[0], acts, grads))
    far, up3, down3, up2, down2, up1, down1, mine = terms(here, counts[0], acts, got, grads, 1)
    (home_terms,) = terms(here, counts[0], acts, got, grads, 0)

    down3, home_terms = after(down3, home_terms)
    going_up = add_bf(up3, up(far))
    going_up, going_down = add_bf(up2, up(going_up)), add_bf(down2, down(down3))
    going_up, going_down, home_terms = after(going_up, going_down, home_terms)
    home_sum = lax.psum_scatter(home_terms, "z", scatter_dimension=0, tiled=True)
    going_up, going_down = add_bf(up1, up(going_up)), add_bf(down1, down(going_down))
    going_up, going_down = up(going_up), down(going_down)
    copy_sum = (mine.astype(F32) + going_up.astype(F32) + going_down.astype(F32)).astype(BF)

    pieces = [copy_sum] + [shift(copy_sum, "y", offset) for offset in range(1, NY)]
    copies, *sent = buckets(here, copy_list, pieces)
    for ahead in range(1, NX):
        copies = copies + shift(sent[ahead - 1], "x", ahead).astype(F32)
    fresh_mom = beta_mom * momentum[0] + (home_sum.astype(F32) + copies)

    def add_gram(step, own, other, gram):
        stack = jnp.concatenate([own, other], axis=0)
        part = lax.dot_general(
            stack, stack, (((0,), (0,)), ((), ())), preferred_element_type=F32
        )
        return gram + jnp.where(step == 0, 0.5, 1.0) * part

    own, other, gram = ring(fresh_mom.astype(BF), add_gram, jnp.zeros((width, width), F32))
    update, fresh = newton_schulz(
        gram, own, other, fresh_mom, weights[0], max(model_width, width)
    )

    pieces = [fresh] + [shift(fresh, "x", offset) for offset in range(1, NX)]
    kept, *sent = wanted(here, copy_list, pieces)
    pieces = [kept] + [shift(sent[offset - 1], "y", offset) for offset in range(1, NY)]
    replica = pick(here, copy_list, pieces)

    def put(step, own, other, full):
        return place(here, step, own, other, full)

    own, other, full = ring(replica, put, empty((model_width, width), BF))
    full = put(4, jnp.concatenate([own, own], axis=0), jnp.concatenate([other, other], axis=0), full)
    return (fresh_mom[None], update[None], full[None])


def solution(mesh):
    grid = Mesh(mesh.devices.reshape(NZ, NC, NX, NY), ("z", "core", "x", "y"))
    split = P(("x", "y"), ("z", "core"), None)
    return jax.shard_map(
        body,
        mesh=grid,
        in_specs=(split, split, split, P(), split, split),
        out_specs=(split, split, P(("x", "y"), None, None)),
        check_vma=False,
    )
```

```python
import functools
import math

import jax
import jax.numpy as jnp
from jax import lax
from jax.experimental import pallas as pl
from jax.experimental.pallas import tpu as pltpu
from jax.sharding import Mesh, PartitionSpec as P

coef_a = 3.4445
coef_b = -4.775
coef_c = 2.0315
beta_mom = 0.95
learn_rate = 0.02
norm_eps = 1e-07

NZ, NC, NX, NY = 8, 2, 4, 4
TERM_ORDER = (4, 3, -3, 2, -2, 1, -1, 0)
BF = jnp.bfloat16
F32 = jnp.float32


def swap(value):
    return lax.ppermute(value, "core", [(0, 1), (1, 0)])


def up(value):
    return lax.ppermute(value, "z", [(i, (i + 1) % NZ) for i in range(NZ)])


def down(value):
    return lax.ppermute(value, "z", [((i + 1) % NZ, i) for i in range(NZ)])


def shift(value, axis, offset):
    return lax.ppermute(value, axis, [(i, (i + offset) % 4) for i in range(4)])


def add_bf(left, right):
    return (left.astype(F32) + right.astype(F32)).astype(BF)


SMEM = pl.BlockSpec(memory_space=pltpu.SMEM)
VMEM = pl.BlockSpec(memory_space=pltpu.VMEM)
ANY = pl.BlockSpec(memory_space=pl.ANY)
HBM = pl.BlockSpec(memory_space=pltpu.HBM)


def small(limit=8):
    return pltpu.CompilerParams(vmem_limit_bytes=limit * 1024 * 1024)


def place_kernel(step_ref, here_ref, own, other, before, out_ref, sems):
    del before
    rows = own.shape[0] // 2
    z, core, step = here_ref[0], here_ref[1], step_ref[0]
    copies = []
    for index, there in enumerate((lax.rem(z + NZ - step, NZ), lax.rem(z + step, NZ))):
        for side, stack in enumerate((own, other)):
            row = pl.multiple_of((NC * there + (1 - core if side else core)) * rows, rows)
            copies.append(
                pltpu.make_async_copy(
                    stack.at[pl.ds(index * rows, rows), :],
                    out_ref.at[pl.ds(row, rows), :],
                    sems.at[2 * index + side],
                )
            )
    twice = lax.rem(step, 4) != 0
    for copy in copies[:2]:
        copy.start()

    @pl.when(twice)
    def _():
        for copy in copies[2:]:
            copy.start()
        for copy in copies[2:]:
            copy.wait()

    for copy in copies[:2]:
        copy.wait()


def place(here, step, own, other, before):
    return pl.pallas_call(
        place_kernel,
        out_shape=jax.ShapeDtypeStruct(before.shape, before.dtype),
        in_specs=[SMEM, SMEM, VMEM, VMEM, ANY],
        out_specs=ANY,
        scratch_shapes=[pltpu.SemaphoreType.DMA((4,))],
        input_output_aliases={4: 0},
        compiler_params=small(),
        name="place",
    )(jnp.reshape(step, (1,)).astype(jnp.int32), here, own, other, before)


def empty_kernel(out_ref):
    del out_ref


def empty(shape, dtype):
    return pl.pallas_call(
        empty_kernel, out_shape=jax.ShapeDtypeStruct(shape, dtype), out_specs=ANY, name="empty"
    )()


def bucket_kernel(here_ref, list_ref, *refs):
    pieces, outs = refs[:NY], refs[NY:]
    x, y = here_ref[2], here_ref[3]
    totals = [jnp.zeros(outs[0].shape, F32) for _ in range(NX)]
    for offset, piece in enumerate(pieces):
        target = list_ref[x * NY + lax.rem(y + NY - offset, NY)]
        value = piece[...].astype(F32)
        for ahead in range(NX):
            fits = target == lax.rem(x + ahead, NX) * NY + y
            totals[ahead] = totals[ahead] + jnp.where(fits, value, 0.0)
    for out, total in zip(outs, totals, strict=True):
        out[...] = total.astype(out.dtype)


def buckets(here, copy_list, pieces):
    shape = pieces[0].shape
    return pl.pallas_call(
        bucket_kernel,
        out_shape=tuple(jax.ShapeDtypeStruct(shape, BF if k else F32) for k in range(NX)),
        in_specs=[SMEM, SMEM] + [VMEM] * NY,
        out_specs=(VMEM,) * NX,
        compiler_params=small(),
        name="buckets",
    )(here, copy_list, *pieces)


def wanted_kernel(here_ref, list_ref, *refs):
    pieces, outs = refs[:NX], refs[NX:]
    x, y = here_ref[2], here_ref[3]
    for offset, out in enumerate(outs):
        source = list_ref[x * NY + lax.rem(y + offset, NY)]
        behind = lax.rem(x + NX - lax.div(source, NY), NX)
        for k, piece in enumerate(pieces):

            @pl.when(behind == k)
            def _():
                out[...] = piece[...]


def wanted(here, copy_list, pieces):
    shape = pieces[0].shape
    return pl.pallas_call(
        wanted_kernel,
        out_shape=(jax.ShapeDtypeStruct(shape, BF),) * NY,
        in_specs=[SMEM, SMEM] + [VMEM] * NX,
        out_specs=(VMEM,) * NY,
        compiler_params=small(),
        name="wanted",
    )(here, copy_list, *pieces)


def pick_kernel(here_ref, list_ref, *refs):
    pieces, out = refs[:NY], refs[NY]
    x, y = here_ref[2], here_ref[3]
    behind = lax.rem(y + NY - lax.rem(list_ref[x * NY + y], NY), NY)
    for k, piece in enumerate(pieces):

        @pl.when(behind == k)
        def _():
            out[...] = piece[...]


def pick(here, copy_list, pieces):
    return pl.pallas_call(
        pick_kernel,
        out_shape=jax.ShapeDtypeStruct(pieces[0].shape, BF),
        in_specs=[SMEM, SMEM] + [VMEM] * NY,
        out_specs=VMEM,
        compiler_params=small(),
        name="pick",
    )(here, copy_list, *pieces)


PAD = 16
CHUNK = 64


def give_kernel(here_ref, counts_ref, acts_ref, grads_ref, out_ref, sems):
    tok_rows, width = grads_ref.shape
    rows = acts_ref.shape[1] // (NZ * NC)
    core = here_ref[1]
    copies = [
        pltpu.make_async_copy(grads_ref, out_ref.at[pl.ds(0, tok_rows), pl.ds(0, width)], sems.at[NZ])
    ]
    for there in range(NZ):
        start = pl.multiple_of((NC * there + 1 - core) * rows, rows)
        copies.append(
            pltpu.make_async_copy(
                acts_ref.at[:, pl.ds(start, rows)],
                out_ref.at[pl.ds(0, tok_rows), pl.ds(width + there * rows, rows)],
                sems.at[there],
            )
        )
    for copy in copies:
        copy.start()
    for index in range(2):
        count = jnp.full((PAD, width), counts_ref[0, index], jnp.int32)
        start = tok_rows + index * PAD
        out_ref[start : start + PAD, :width] = count.astype(F32).astype(BF)
    for copy in copies:
        copy.wait()


def give(here, counts, acts, grads):
    tok_rows, width = grads.shape
    return pl.pallas_call(
        give_kernel,
        out_shape=jax.ShapeDtypeStruct((tok_rows + 2 * PAD, width + acts.shape[1] // NC), BF),
        in_specs=[SMEM, SMEM, HBM, HBM],
        out_specs=VMEM,
        scratch_shapes=[pltpu.SemaphoreType.DMA((NZ + 1,))],
        compiler_params=small(56),
        name="give",
    )(here, counts, acts, grads)


def terms_kernel(which, here_ref, counts_ref, acts_ref, got_ref, grads_ref, *out_refs):
    tok_rows, width = grads_ref.shape
    rows = acts_ref.shape[1] // (NZ * NC)
    z, core = here_ref[0], here_ref[1]
    order = [lax.rem(z + NZ + offset, NZ) for offset in TERM_ORDER]

    def columns(ref, start):
        return ref[:tok_rows, pl.ds(pl.multiple_of(start, rows), rows)]

    slot = lax.broadcasted_iota(jnp.int32, (tok_rows, width), 0)
    home, copy = counts_ref[0, 0], counts_ref[0, 1]
    low, high = (home, home + copy) if which else (0, home)
    right = jnp.where((slot >= low) & (slot < high), grads_ref[...].astype(F32), 0.0).astype(BF)
    left = jnp.concatenate(
        [columns(acts_ref, (NC * there + core) * rows) for there in order], axis=1
    )
    contract = (((0,), (0,)), ((), ()))
    total = lax.dot_general(left, right, contract, preferred_element_type=F32)
    place = slot.astype(F32)
    home = got_ref[tok_rows : tok_rows + 1, :width].astype(F32)
    copy = got_ref[tok_rows + PAD : tok_rows + PAD + 1, :width].astype(F32)
    mask = (place >= home) & (place < home + copy) if which else place < home
    right = jnp.where(mask, got_ref[:tok_rows, :width].astype(F32), 0.0).astype(BF)
    left = jnp.concatenate(
        [columns(got_ref, width + there * rows) for there in order], axis=1
    )
    total = total + lax.dot_general(left, right, contract, preferred_element_type=F32)
    for index, out_ref in enumerate(out_refs):
        size = out_ref.shape[0]
        out_ref[...] = total[index * size : (index + 1) * size].astype(BF)


def terms(here, counts, acts, got, grads, which):
    tok_rows, width = grads.shape
    rows = acts.shape[1] // (NZ * NC)
    return pl.pallas_call(
        functools.partial(terms_kernel, which),
        out_shape=(jax.ShapeDtypeStruct((rows, width), BF),) * NZ,
        in_specs=[SMEM, SMEM] + [VMEM] * 3,
        out_specs=(VMEM,) * NZ,
        compiler_params=small(20),
        cost_estimate=pl.CostEstimate(
            flops=4 * tok_rows * rows * NZ * width,
            bytes_accessed=4 * tok_rows * rows * NZ,
            transcendentals=0,
        ),
        name="copy_terms" if which else "home_terms",
    )(here, counts, acts, got, grads)


def halves(value):
    high = value.astype(BF)
    return high, (value - high.astype(F32)).astype(BF)


def dot(left, right):
    return jnp.dot(left, right, preferred_element_type=F32)


def newton_kernel(
    factor,
    gram_ref,
    mine_ref,
    other_ref,
    mom_ref,
    weight_ref,
    update_ref,
    fresh_ref,
    s_hi,
    s_lo,
    k_hi,
    k_lo,
    t_hi,
    t_lo,
    iterate_ref,
    full_ref,
):
    width = gram_ref.shape[0]
    tile = width // 3
    spans = [slice(i * tile, (i + 1) * tile) for i in range(3)]
    pairs = [(i, j) for i in range(3) for j in range(i, 3)]

    def store(hi, lo, i, j, value):
        hi[spans[i], spans[j]], lo[spans[i], spans[j]] = halves(value)
        if i != j:
            hi[spans[j], spans[i]], lo[spans[j], spans[i]] = halves(value.T)

    def load(hi, lo, i, j):
        return hi[spans[i], spans[j]].astype(F32) + lo[spans[i], spans[j]].astype(F32)

    def product(left, right, i, j):
        (l_hi, l_lo), (r_hi, r_lo) = left, right
        rows, cols = spans[i], spans[j]
        out = dot(l_hi[rows, :], r_lo[:, cols]) + dot(l_lo[rows, :], r_hi[:, cols])
        return out + dot(l_hi[rows, :], r_hi[:, cols])

    def times(value, right):
        hi, lo = halves(value)
        r_hi, r_lo = right
        both = dot(jnp.concatenate([hi, lo], axis=0), r_hi[...])
        rows = value.shape[0]
        return both[:rows] + (both[rows:] + dot(hi, r_lo[...]))

    same = lax.broadcasted_iota(jnp.int32, (tile, tile), 0) == lax.broadcasted_iota(
        jnp.int32, (tile, tile), 1
    )
    last = jnp.concatenate([mine_ref[...], other_ref[...]], axis=0)
    total = jnp.zeros((1, 1), F32)
    for span in spans:
        value = gram_ref[span, :] + lax.dot_general(
            last[:, span], last, (((0,), (0,)), ((), ())), preferred_element_type=F32
        )
        full_ref[span, :] = value
        on = jnp.where(same, value[:, span], 0.0)
        total = total + jnp.sum(jnp.sum(on, axis=1, keepdims=True), axis=0, keepdims=True)
    scale = 1.0 / (jnp.sqrt(total) + norm_eps)

    @pl.loop(0, width // CHUNK)
    def _(index):
        chunk = pl.ds(pl.multiple_of(index * CHUNK, CHUNK), CHUNK)
        s_hi[chunk, :], s_lo[chunk, :] = halves(full_ref[chunk, :] * scale * scale)

    iterate_ref[...] = mom_ref[...] * scale
    s, k, t = (s_hi, s_lo), (k_hi, k_lo), (t_hi, t_lo)

    @pl.loop(0, 2)
    def _(step):
        for i, j in pairs:
            store(*k, i, j, coef_b * load(*s, i, j) + coef_c * product(s, s, i, j))
        iterate_ref[...] = coef_a * iterate_ref[...] + times(iterate_ref[...], k)
        for i, j in pairs:
            store(*t, i, j, coef_a * load(*s, i, j) + product(s, k, i, j))
        for i, j in pairs:
            store(*s, i, j, coef_a * load(*t, i, j) + product(t, k, i, j))

    iterate = iterate_ref[...]
    side = times(iterate, s)
    iterate = coef_a * iterate + (coef_b * side + coef_c * times(side, s))
    update = factor * iterate
    update_ref[...] = update
    fresh_ref[...] = (weight_ref[...].astype(F32) - learn_rate * update).astype(BF)


def newton_schulz(gram, mine, other, mom, weight, longest):
    rows, width = mom.shape
    vmem = pl.BlockSpec(memory_space=pltpu.VMEM)
    return pl.pallas_call(
        functools.partial(newton_kernel, 0.2 * math.sqrt(longest)),
        out_shape=(
            jax.ShapeDtypeStruct((rows, width), F32),
            jax.ShapeDtypeStruct((rows, width), BF),
        ),
        in_specs=[vmem] * 5,
        out_specs=(vmem, vmem),
        scratch_shapes=[pltpu.VMEM((width, width), BF)] * 6
        + [pltpu.VMEM((rows, width), F32), pltpu.VMEM((width, width), F32)],
        compiler_params=small(20),
        cost_estimate=pl.CostEstimate(
            flops=28 * width**3, bytes_accessed=8 * width * width, transcendentals=0
        ),
        name="newton_schulz",
    )(gram, mine, other, mom, weight)


def after(value, *others):
    return lax.optimization_barrier((value, *others))


def hold(value, other):
    return lax.optimization_barrier((value, other))


def sum_step(blocks, step, state):
    far, up3, down3, up2, down2, up1, down1, mine = blocks
    if step == 0:
        return add_bf(up3, up(far)), down3
    below, above = up(state[0]), down(state[1])
    if step == 3:
        return mine, below, above
    return add_bf((up2, up1)[step - 1], below), add_bf((down2, down1)[step - 1], above)


def ring(block, work, state):
    def one(step, carry):
        below, above, state = carry
        stack = jnp.concatenate([below, above], axis=0)
        below, above = up(below), down(above)
        return below, above, work(step, stack, swap(stack), state)

    far, _, state = lax.fori_loop(0, 4, one, (block, block, state))
    return far, swap(far), state


def body(tokens_in, out_grads, counts, copy_list, weights, momentum):
    acts = tokens_in[0]
    grads = out_grads[0]
    model_width = acts.shape[1]
    width = grads.shape[1]
    here = jnp.stack([lax.axis_index(name) for name in ("z", "core", "x", "y")]).astype(jnp.int32)

    got = swap(give(here, counts[0], acts, grads))
    copy = terms(here, counts[0], acts, got, grads, 1)
    home = terms(here, counts[0], acts, got, grads, 0)

    copy_state = sum_step(copy, 0, None)
    home, copy_state = hold(home, copy_state)
    copy_state = sum_step(copy, 1, copy_state)
    home_state = sum_step(home, 0, None)
    for step in (2, 3):
        home_state, copy_state = hold(home_state, copy_state)
        copy_state = sum_step(copy, step, copy_state)
        home_state = sum_step(home, step - 1, home_state)
    copy_sum = sum(value.astype(F32) for value in copy_state).astype(BF)
    home_state, copy_sum = hold(home_state, copy_sum)
    home_sum = sum(value.astype(F32) for value in sum_step(home, 3, home_state))

    pieces = {offset: shift(copy_sum, "y", offset) for offset in (2, 1, 3)}
    pieces = [copy_sum] + [pieces[offset] for offset in range(1, NY)]
    copies, *sent = buckets(here, copy_list, pieces)
    for ahead in (2, 1, 3):
        copies = copies + shift(sent[ahead - 1], "x", ahead).astype(F32)
    fresh_mom = beta_mom * momentum[0] + (home_sum + copies)

    def add_gram(step, own, other, gram):
        stack = jnp.concatenate([own, other], axis=0)
        part = lax.dot_general(
            stack, stack, (((0,), (0,)), ((), ())), preferred_element_type=F32
        )
        return gram + jnp.where(step == 0, 0.5, 1.0) * part

    own, other, gram = ring(fresh_mom.astype(BF), add_gram, jnp.zeros((width, width), F32))
    update, fresh = newton_schulz(
        gram, own, other, fresh_mom, weights[0], max(model_width, width)
    )

    pieces = {offset: shift(fresh, "x", offset) for offset in (2, 1, 3)}
    pieces = [fresh] + [pieces[offset] for offset in range(1, NX)]
    kept, *sent = wanted(here, copy_list, pieces)
    pieces = {offset: shift(sent[offset - 1], "y", offset) for offset in (2, 1, 3)}
    pieces = [kept] + [pieces[offset] for offset in range(1, NY)]
    replica = pick(here, copy_list, pieces)

    def put(step, own, other, full):
        return place(here, step, own, other, full)

    own, other, full = ring(replica, put, empty((model_width, width), BF))
    full = put(4, jnp.concatenate([own, own], axis=0), jnp.concatenate([other, other], axis=0), full)
    return (fresh_mom[None], update[None], full[None])


def solution(mesh):
    grid = Mesh(mesh.devices.reshape(NZ, NC, NX, NY), ("z", "core", "x", "y"))
    split = P(("x", "y"), ("z", "core"), None)
    return jax.shard_map(
        body,
        mesh=grid,
        in_specs=(split, split, split, P(), split, split),
        out_specs=(split, split, P(("x", "y"), None, None)),
        check_vma=False,
    )
```

```python
import functools
import math

import jax
import jax.numpy as jnp
from jax import lax
from jax.experimental import pallas as pl
from jax.experimental.pallas import tpu as pltpu
from jax.sharding import Mesh, PartitionSpec as P

coef_a = 3.4445
coef_b = -4.775
coef_c = 2.0315
beta_mom = 0.95
learn_rate = 0.02
norm_eps = 1e-07

NZ, NC, NX, NY = 8, 2, 4, 4
BF = jnp.bfloat16
F32 = jnp.float32


def swap(value):
    return lax.ppermute(value, "core", [(0, 1), (1, 0)])


def up(value):
    return lax.ppermute(value, "z", [(i, (i + 1) % NZ) for i in range(NZ)])


def down(value):
    return lax.ppermute(value, "z", [((i + 1) % NZ, i) for i in range(NZ)])


def shift(value, axis, offset):
    return lax.ppermute(value, axis, [(i, (i + offset) % 4) for i in range(4)])


def add_bf(left, right):
    return (left.astype(F32) + right.astype(F32)).astype(BF)


SMEM = pl.BlockSpec(memory_space=pltpu.SMEM)
VMEM = pl.BlockSpec(memory_space=pltpu.VMEM)
ANY = pl.BlockSpec(memory_space=pl.ANY)
HBM = pl.BlockSpec(memory_space=pltpu.HBM)


def small(limit=8):
    return pltpu.CompilerParams(vmem_limit_bytes=limit * 1024 * 1024)


def place_kernel(side, here_ref, blocks_ref, *refs):
    out_ref, sems = refs[-2:]
    rows = blocks_ref.shape[0] // NZ
    z, core = here_ref[0], here_ref[1]
    parity = 1 - core if side else core
    copies = []
    for index in range(NZ):
        there = NC * lax.rem(z + index + NZ // 2, NZ) + parity
        copies.append(
            pltpu.make_async_copy(
                blocks_ref.at[pl.ds(index * rows, rows), :],
                out_ref.at[pl.ds(pl.multiple_of(there * rows, rows), rows), :],
                sems.at[index],
            )
        )
    for copy in copies:
        copy.start()
    for copy in copies:
        copy.wait()


def place(side, here, blocks, before=None):
    return pl.pallas_call(
        functools.partial(place_kernel, side),
        out_shape=jax.ShapeDtypeStruct((NC * blocks.shape[0], blocks.shape[1]), blocks.dtype),
        in_specs=[SMEM, VMEM] + ([] if before is None else [ANY]),
        out_specs=ANY,
        scratch_shapes=[pltpu.SemaphoreType.DMA((NZ,))],
        input_output_aliases={} if before is None else {2: 0},
        compiler_params=small(),
        name="place",
    )(here, blocks, *([] if before is None else [before]))


def bucket_kernel(here_ref, list_ref, *refs):
    pieces, outs = refs[:NY], refs[NY:]
    x, y = here_ref[2], here_ref[3]
    totals = [jnp.zeros(outs[0].shape, F32) for _ in range(NX)]
    for offset, piece in enumerate(pieces):
        target = list_ref[x * NY + lax.rem(y + NY - offset, NY)]
        value = piece[...].astype(F32)
        for ahead in range(NX):
            fits = target == lax.rem(x + ahead, NX) * NY + y
            totals[ahead] = totals[ahead] + jnp.where(fits, value, 0.0)
    for out, total in zip(outs, totals, strict=True):
        out[...] = total.astype(out.dtype)


def buckets(here, copy_list, pieces):
    shape = pieces[0].shape
    return pl.pallas_call(
        bucket_kernel,
        out_shape=tuple(jax.ShapeDtypeStruct(shape, BF if k else F32) for k in range(NX)),
        in_specs=[SMEM, SMEM] + [VMEM] * NY,
        out_specs=(VMEM,) * NX,
        compiler_params=small(),
        name="buckets",
    )(here, copy_list, *pieces)


def wanted_kernel(here_ref, list_ref, *refs):
    pieces, outs = refs[:NX], refs[NX:]
    x, y = here_ref[2], here_ref[3]
    for offset, out in enumerate(outs):
        source = list_ref[x * NY + lax.rem(y + offset, NY)]
        behind = lax.rem(x + NX - lax.div(source, NY), NX)
        for k, piece in enumerate(pieces):

            @pl.when(behind == k)
            def _():
                out[...] = piece[...]


def wanted(here, copy_list, pieces):
    shape = pieces[0].shape
    return pl.pallas_call(
        wanted_kernel,
        out_shape=(jax.ShapeDtypeStruct(shape, BF),) * NY,
        in_specs=[SMEM, SMEM] + [VMEM] * NX,
        out_specs=(VMEM,) * NY,
        compiler_params=small(),
        name="wanted",
    )(here, copy_list, *pieces)


def pick_kernel(here_ref, list_ref, *refs):
    pieces, out = refs[:NY], refs[NY]
    x, y = here_ref[2], here_ref[3]
    behind = lax.rem(y + NY - lax.rem(list_ref[x * NY + y], NY), NY)
    for k, piece in enumerate(pieces):

        @pl.when(behind == k)
        def _():
            out[...] = piece[...]


def pick(here, copy_list, pieces):
    return pl.pallas_call(
        pick_kernel,
        out_shape=jax.ShapeDtypeStruct(pieces[0].shape, BF),
        in_specs=[SMEM, SMEM] + [VMEM] * NY,
        out_specs=VMEM,
        compiler_params=small(),
        name="pick",
    )(here, copy_list, *pieces)


CHUNK = 64


def terms_kernel(
    offsets, here_ref, counts_ref, got_counts_ref, acts_ref, got_ref, grads_ref, got_grads_ref, *out_refs
):
    tok_rows, width = grads_ref.shape
    rows = acts_ref.shape[1] // (NZ * NC)
    z, core = here_ref[0], here_ref[1]
    starts = [
        pl.multiple_of((NC * lax.rem(z + NZ + offset, NZ) + core) * rows, rows) for offset in offsets
    ]
    slot = lax.broadcasted_iota(jnp.int32, (tok_rows, width), 0)
    totals = [None, None]
    for acts, grads, counts in (
        (acts_ref, grads_ref, counts_ref),
        (got_ref, got_grads_ref, got_counts_ref),
    ):
        home, copy = counts[0, 0], counts[0, 1]
        left = jnp.concatenate([acts[:, pl.ds(start, rows)] for start in starts], axis=1)
        value = grads[...].astype(F32)
        for which, (low, high) in enumerate(((home, home + copy), (0, home))):
            right = jnp.where((slot >= low) & (slot < high), value, 0.0).astype(BF)
            part = lax.dot_general(
                left, right, (((0,), (0,)), ((), ())), preferred_element_type=F32
            )
            totals[which] = part if totals[which] is None else totals[which] + part
    for index, out_ref in enumerate(out_refs):
        span = slice(index * rows, (index + 1) * rows)
        out_ref[:rows] = totals[0][span].astype(BF)
        out_ref[rows:] = totals[1][span].astype(BF)


def terms(here, counts, got_counts, acts, got, grads, got_grads, offsets):
    tok_rows, width = grads.shape
    rows = acts.shape[1] // (NZ * NC)
    return pl.pallas_call(
        functools.partial(terms_kernel, offsets),
        out_shape=(jax.ShapeDtypeStruct((2 * rows, width), BF),) * len(offsets),
        in_specs=[SMEM] * 3 + [VMEM] * 4,
        out_specs=(VMEM,) * len(offsets),
        compiler_params=small(20),
        cost_estimate=pl.CostEstimate(
            flops=8 * tok_rows * rows * len(offsets) * width,
            bytes_accessed=4 * tok_rows * rows * NZ,
            transcendentals=0,
        ),
        name="terms",
    )(here, counts, got_counts, acts, got, grads, got_grads)


def halves(value):
    high = value.astype(BF)
    return high, (value - high.astype(F32)).astype(BF)


def dot(left, right):
    return jnp.dot(left, right, preferred_element_type=F32)


def newton_kernel(
    factor,
    gram_ref,
    other_ref,
    mom_ref,
    weight_ref,
    update_ref,
    fresh_ref,
    s_hi,
    s_lo,
    k_hi,
    k_lo,
    t_hi,
    t_lo,
    iterate_ref,
    full_ref,
):
    width = gram_ref.shape[0]
    tile = width // 3
    spans = [slice(i * tile, (i + 1) * tile) for i in range(3)]
    pairs = [(i, j) for i in range(3) for j in range(i, 3)]

    def store(hi, lo, i, j, value):
        hi[spans[i], spans[j]], lo[spans[i], spans[j]] = halves(value)
        if i != j:
            hi[spans[j], spans[i]], lo[spans[j], spans[i]] = halves(value.T)

    def load(hi, lo, i, j):
        return hi[spans[i], spans[j]].astype(F32) + lo[spans[i], spans[j]].astype(F32)

    def product(left, right, i, j):
        (l_hi, l_lo), (r_hi, r_lo) = left, right
        rows, cols = spans[i], spans[j]
        out = dot(l_hi[rows, :], r_lo[:, cols]) + dot(l_lo[rows, :], r_hi[:, cols])
        return out + dot(l_hi[rows, :], r_hi[:, cols])

    def times(value, right):
        hi, lo = halves(value)
        r_hi, r_lo = right
        both = dot(jnp.concatenate([hi, lo], axis=0), r_hi[...])
        rows = value.shape[0]
        return both[:rows] + (both[rows:] + dot(hi, r_lo[...]))

    same = lax.broadcasted_iota(jnp.int32, (tile, tile), 0) == lax.broadcasted_iota(
        jnp.int32, (tile, tile), 1
    )
    total = jnp.zeros((1, 1), F32)
    for span in spans:
        value = gram_ref[span, :] + lax.dot_general(
            other_ref[:, span],
            other_ref[...],
            (((0,), (0,)), ((), ())),
            preferred_element_type=F32,
        )
        full_ref[span, :] = value
        on = jnp.where(same, value[:, span], 0.0)
        total = total + jnp.sum(jnp.sum(on, axis=1, keepdims=True), axis=0, keepdims=True)
    scale = 1.0 / (jnp.sqrt(total) + norm_eps)

    @pl.loop(0, width // CHUNK)
    def _(index):
        chunk = pl.ds(pl.multiple_of(index * CHUNK, CHUNK), CHUNK)
        s_hi[chunk, :], s_lo[chunk, :] = halves(full_ref[chunk, :] * scale * scale)

    iterate_ref[...] = mom_ref[...] * scale
    s, k, t = (s_hi, s_lo), (k_hi, k_lo), (t_hi, t_lo)

    @pl.loop(0, 2)
    def _(step):
        for i, j in pairs:
            store(*k, i, j, coef_b * load(*s, i, j) + coef_c * product(s, s, i, j))
        iterate_ref[...] = coef_a * iterate_ref[...] + times(iterate_ref[...], k)
        for i, j in pairs:
            store(*t, i, j, coef_a * load(*s, i, j) + product(s, k, i, j))
        for i, j in pairs:
            store(*s, i, j, coef_a * load(*t, i, j) + product(t, k, i, j))

    iterate = iterate_ref[...]
    side = times(iterate, s)
    iterate = coef_a * iterate + (coef_b * side + coef_c * times(side, s))
    update = factor * iterate
    update_ref[...] = update
    fresh_ref[...] = (weight_ref[...].astype(F32) - learn_rate * update).astype(BF)


def newton_schulz(gram, other, mom, weight, longest):
    rows, width = mom.shape
    vmem = pl.BlockSpec(memory_space=pltpu.VMEM)
    return pl.pallas_call(
        functools.partial(newton_kernel, 0.2 * math.sqrt(longest)),
        out_shape=(
            jax.ShapeDtypeStruct((rows, width), F32),
            jax.ShapeDtypeStruct((rows, width), BF),
        ),
        in_specs=[vmem] * 4,
        out_specs=(vmem, vmem),
        scratch_shapes=[pltpu.VMEM((width, width), BF)] * 6
        + [pltpu.VMEM((rows, width), F32), pltpu.VMEM((width, width), F32)],
        compiler_params=small(20),
        cost_estimate=pl.CostEstimate(
            flops=28 * width**3, bytes_accessed=8 * width * width, transcendentals=0
        ),
        name="newton_schulz",
    )(gram, other, mom, weight)


def after(value, *others):
    return lax.optimization_barrier((value, *others))


def ring_sum(far, near):
    rows = far.shape[0] // 2
    up3, up2, up1, mine, down1, down2, down3 = near
    copies, homes = up(far[:rows]), down(far[rows:])
    below = jnp.concatenate([add_bf(up3[:rows], copies), up3[rows:]], axis=0)
    above = jnp.concatenate([down3[:rows], add_bf(down3[rows:], homes)], axis=0)
    on_up = jnp.stack([up2, up1, mine])
    on_down = jnp.stack([down2, down1, jnp.zeros_like(mine)])

    def one(step, carry):
        below, above = carry
        below, above = up(below), down(above)
        return add_bf(below, on_up[step]), add_bf(above, on_down[step])

    return lax.fori_loop(0, 3, one, (below, above))


def ring(block):
    rows, width = block.shape

    def one(step, carry):
        below, above, got = carry
        got = lax.dynamic_update_slice(got, below, ((4 - step) * rows, 0))
        got = lax.dynamic_update_slice(got, above, ((4 + step) * rows, 0))
        return up(below), down(above), got

    got = jnp.zeros((NZ * rows, width), block.dtype)
    far, _, got = lax.fori_loop(0, 4, one, (block, block, got))
    return lax.dynamic_update_slice(got, far, (0, 0))


def body(tokens_in, out_grads, counts, copy_list, weights, momentum):
    acts = tokens_in[0]
    grads = out_grads[0]
    model_width = acts.shape[1]
    width = grads.shape[1]
    here = jnp.stack([lax.axis_index(name) for name in ("z", "core", "x", "y")]).astype(jnp.int32)

    tokens = (counts[0], swap(counts[0]), acts, swap(acts), grads, swap(grads))
    (far,) = terms(here, *tokens, (4,))
    near = terms(here, *tokens, (3, 2, 1, 0, -1, -2, -3))
    below, above = ring_sum(far, near)
    rows = below.shape[0] // 2
    total = below.astype(F32) + above.astype(F32)
    copy_sum, home_sum = total[:rows].astype(BF), total[rows:]

    pieces = {offset: shift(copy_sum, "y", offset) for offset in (2, 1, 3)}
    pieces = [copy_sum] + [pieces[offset] for offset in range(1, NY)]
    copies, *sent = buckets(here, copy_list, pieces)
    for ahead in (2, 1, 3):
        copies = copies + shift(sent[ahead - 1], "x", ahead).astype(F32)
    fresh_mom = beta_mom * momentum[0] + (home_sum + copies)

    own = ring(fresh_mom.astype(BF))
    gram = lax.dot_general(own, own, (((0,), (0,)), ((), ())), preferred_element_type=F32)
    update, fresh = newton_schulz(
        gram, swap(own), fresh_mom, weights[0], max(model_width, width)
    )

    pieces = {offset: shift(fresh, "x", offset) for offset in (2, 1, 3)}
    pieces = [fresh] + [pieces[offset] for offset in range(1, NX)]
    kept, *sent = wanted(here, copy_list, pieces)
    pieces = {offset: shift(sent[offset - 1], "y", offset) for offset in (2, 1, 3)}
    pieces = [kept] + [pieces[offset] for offset in range(1, NY)]
    replica = pick(here, copy_list, pieces)

    own = ring(replica)
    full = place(1, here, swap(own), place(0, here, own))
    return (fresh_mom[None], update[None], full[None])


def solution(mesh):
    grid = Mesh(mesh.devices.reshape(NZ, NC, NX, NY), ("z", "core", "x", "y"))
    split = P(("x", "y"), ("z", "core"), None)
    return jax.shard_map(
        body,
        mesh=grid,
        in_specs=(split, split, split, P(), split, split),
        out_specs=(split, split, P(("x", "y"), None, None)),
        check_vma=False,
    )
```

```python
import functools
import math

import jax
import jax.numpy as jnp
from jax import lax
from jax.experimental import pallas as pl
from jax.experimental.pallas import tpu as pltpu
from jax.sharding import Mesh, PartitionSpec as P

coef_a = 3.4445
coef_b = -4.775
coef_c = 2.0315
beta_mom = 0.95
learn_rate = 0.02
norm_eps = 1e-07

NZ, NC, NX, NY = 8, 2, 4, 4
BF = jnp.bfloat16
F32 = jnp.float32


def swap(value):
    return lax.ppermute(value, "core", [(0, 1), (1, 0)])


def up(value):
    return lax.ppermute(value, "z", [(i, (i + 1) % NZ) for i in range(NZ)])


def down(value):
    return lax.ppermute(value, "z", [((i + 1) % NZ, i) for i in range(NZ)])


def shift(value, axis, offset):
    return lax.ppermute(value, axis, [(i, (i + offset) % 4) for i in range(4)])


def add_bf(left, right):
    return (left.astype(F32) + right.astype(F32)).astype(BF)


SMEM = pl.BlockSpec(memory_space=pltpu.SMEM)
VMEM = pl.BlockSpec(memory_space=pltpu.VMEM)
ANY = pl.BlockSpec(memory_space=pl.ANY)
HBM = pl.BlockSpec(memory_space=pltpu.HBM)


def small(limit=8):
    return pltpu.CompilerParams(vmem_limit_bytes=limit * 1024 * 1024)


def place_kernel(side, here_ref, blocks_ref, *refs):
    out_ref, sems = refs[-2:]
    rows = blocks_ref.shape[0] // NZ
    z, core = here_ref[0], here_ref[1]
    parity = 1 - core if side else core
    copies = []
    for index in range(NZ):
        there = NC * lax.rem(z + index + NZ // 2, NZ) + parity
        copies.append(
            pltpu.make_async_copy(
                blocks_ref.at[pl.ds(index * rows, rows), :],
                out_ref.at[pl.ds(pl.multiple_of(there * rows, rows), rows), :],
                sems.at[index],
            )
        )
    for copy in copies:
        copy.start()
    for copy in copies:
        copy.wait()


def place(side, here, blocks, before=None):
    return pl.pallas_call(
        functools.partial(place_kernel, side),
        out_shape=jax.ShapeDtypeStruct((NC * blocks.shape[0], blocks.shape[1]), blocks.dtype),
        in_specs=[SMEM, VMEM] + ([] if before is None else [ANY]),
        out_specs=ANY,
        scratch_shapes=[pltpu.SemaphoreType.DMA((NZ,))],
        input_output_aliases={} if before is None else {2: 0},
        compiler_params=small(),
        name="place",
    )(here, blocks, *([] if before is None else [before]))


def bucket_kernel(here_ref, list_ref, *refs):
    pieces, outs = refs[:NY], refs[NY:]
    x, y = here_ref[2], here_ref[3]
    totals = [jnp.zeros(outs[0].shape, F32) for _ in range(NX)]
    for offset, piece in enumerate(pieces):
        target = list_ref[x * NY + lax.rem(y + NY - offset, NY)]
        value = piece[...].astype(F32)
        for ahead in range(NX):
            fits = target == lax.rem(x + ahead, NX) * NY + y
            totals[ahead] = totals[ahead] + jnp.where(fits, value, 0.0)
    for out, total in zip(outs, totals, strict=True):
        out[...] = total.astype(out.dtype)


def buckets(here, copy_list, pieces):
    shape = pieces[0].shape
    return pl.pallas_call(
        bucket_kernel,
        out_shape=tuple(jax.ShapeDtypeStruct(shape, BF if k else F32) for k in range(NX)),
        in_specs=[SMEM, SMEM] + [VMEM] * NY,
        out_specs=(VMEM,) * NX,
        compiler_params=small(),
        name="buckets",
    )(here, copy_list, *pieces)


def wanted_kernel(here_ref, list_ref, *refs):
    pieces, outs = refs[:NX], refs[NX:]
    x, y = here_ref[2], here_ref[3]
    for offset, out in enumerate(outs):
        source = list_ref[x * NY + lax.rem(y + offset, NY)]
        behind = lax.rem(x + NX - lax.div(source, NY), NX)
        for k, piece in enumerate(pieces):

            @pl.when(behind == k)
            def _():
                out[...] = piece[...]


def wanted(here, copy_list, pieces):
    shape = pieces[0].shape
    return pl.pallas_call(
        wanted_kernel,
        out_shape=(jax.ShapeDtypeStruct(shape, BF),) * NY,
        in_specs=[SMEM, SMEM] + [VMEM] * NX,
        out_specs=(VMEM,) * NY,
        compiler_params=small(),
        name="wanted",
    )(here, copy_list, *pieces)


def pick_kernel(here_ref, list_ref, *refs):
    pieces, out = refs[:NY], refs[NY]
    x, y = here_ref[2], here_ref[3]
    behind = lax.rem(y + NY - lax.rem(list_ref[x * NY + y], NY), NY)
    for k, piece in enumerate(pieces):

        @pl.when(behind == k)
        def _():
            out[...] = piece[...]


def pick(here, copy_list, pieces):
    return pl.pallas_call(
        pick_kernel,
        out_shape=jax.ShapeDtypeStruct(pieces[0].shape, BF),
        in_specs=[SMEM, SMEM] + [VMEM] * NY,
        out_specs=VMEM,
        compiler_params=small(),
        name="pick",
    )(here, copy_list, *pieces)


CHUNK = 64


def terms_kernel(
    offsets, here_ref, counts_ref, got_counts_ref, acts_ref, got_ref, grads_ref, got_grads_ref, *out_refs
):
    tok_rows, width = grads_ref.shape
    rows = acts_ref.shape[1] // (NZ * NC)
    z, core = here_ref[0], here_ref[1]
    starts = [
        pl.multiple_of((NC * lax.rem(z + NZ + offset, NZ) + core) * rows, rows) for offset in offsets
    ]
    slot = lax.broadcasted_iota(jnp.int32, (tok_rows, width), 0)
    totals = [None, None]
    for acts, grads, counts in (
        (acts_ref, grads_ref, counts_ref),
        (got_ref, got_grads_ref, got_counts_ref),
    ):
        home, copy = counts[0, 0], counts[0, 1]
        left = jnp.concatenate([acts[:, pl.ds(start, rows)] for start in starts], axis=1)
        value = grads[...].astype(F32)
        for which, (low, high) in enumerate(((home, home + copy), (0, home))):
            right = jnp.where((slot >= low) & (slot < high), value, 0.0).astype(BF)
            part = lax.dot_general(
                left, right, (((0,), (0,)), ((), ())), preferred_element_type=F32
            )
            totals[which] = part if totals[which] is None else totals[which] + part
    for index, out_ref in enumerate(out_refs):
        span = slice(index * rows, (index + 1) * rows)
        out_ref[:rows] = totals[0][span].astype(BF)
        out_ref[rows:] = totals[1][span].astype(BF)


def terms(here, counts, got_counts, acts, got, grads, got_grads, offsets):
    tok_rows, width = grads.shape
    rows = acts.shape[1] // (NZ * NC)
    return pl.pallas_call(
        functools.partial(terms_kernel, offsets),
        out_shape=(jax.ShapeDtypeStruct((2 * rows, width), BF),) * len(offsets),
        in_specs=[SMEM] * 3 + [VMEM] * 4,
        out_specs=(VMEM,) * len(offsets),
        compiler_params=small(56 if len(offsets) == 1 else 20),
        cost_estimate=pl.CostEstimate(
            flops=8 * tok_rows * rows * len(offsets) * width,
            bytes_accessed=4 * tok_rows * rows * NZ,
            transcendentals=0,
        ),
        name="terms",
    )(here, counts, got_counts, acts, got, grads, got_grads)


def halves(value):
    high = value.astype(BF)
    return high, (value - high.astype(F32)).astype(BF)


def dot(left, right):
    return jnp.dot(left, right, preferred_element_type=F32)


def newton_kernel(
    factor,
    gram_ref,
    other_ref,
    mom_ref,
    weight_ref,
    update_ref,
    fresh_ref,
    s_hi,
    s_lo,
    k_hi,
    k_lo,
    t_hi,
    t_lo,
    iterate_ref,
    full_ref,
):
    width = gram_ref.shape[0]
    tile = width // 3
    spans = [slice(i * tile, (i + 1) * tile) for i in range(3)]
    pairs = [(i, j) for i in range(3) for j in range(i, 3)]

    def store(hi, lo, i, j, value):
        hi[spans[i], spans[j]], lo[spans[i], spans[j]] = halves(value)
        if i != j:
            hi[spans[j], spans[i]], lo[spans[j], spans[i]] = halves(value.T)

    def load(hi, lo, i, j):
        return hi[spans[i], spans[j]].astype(F32) + lo[spans[i], spans[j]].astype(F32)

    def product(left, right, i, j):
        (l_hi, l_lo), (r_hi, r_lo) = left, right
        rows, cols = spans[i], spans[j]
        out = dot(l_hi[rows, :], r_lo[:, cols]) + dot(l_lo[rows, :], r_hi[:, cols])
        return out + dot(l_hi[rows, :], r_hi[:, cols])

    def times(value, right):
        hi, lo = halves(value)
        r_hi, r_lo = right
        both = dot(jnp.concatenate([hi, lo], axis=0), r_hi[...])
        rows = value.shape[0]
        return both[:rows] + (both[rows:] + dot(hi, r_lo[...]))

    same = lax.broadcasted_iota(jnp.int32, (tile, tile), 0) == lax.broadcasted_iota(
        jnp.int32, (tile, tile), 1
    )
    total = jnp.zeros((1, 1), F32)
    for span in spans:
        value = gram_ref[span, :] + lax.dot_general(
            other_ref[:, span],
            other_ref[...],
            (((0,), (0,)), ((), ())),
            preferred_element_type=F32,
        )
        full_ref[span, :] = value
        on = jnp.where(same, value[:, span], 0.0)
        total = total + jnp.sum(jnp.sum(on, axis=1, keepdims=True), axis=0, keepdims=True)
    scale = 1.0 / (jnp.sqrt(total) + norm_eps)

    @pl.loop(0, width // CHUNK)
    def _(index):
        chunk = pl.ds(pl.multiple_of(index * CHUNK, CHUNK), CHUNK)
        s_hi[chunk, :], s_lo[chunk, :] = halves(full_ref[chunk, :] * scale * scale)

    iterate_ref[...] = mom_ref[...] * scale
    s, k, t = (s_hi, s_lo), (k_hi, k_lo), (t_hi, t_lo)

    @pl.loop(0, 2)
    def _(step):
        for i, j in pairs:
            store(*k, i, j, coef_b * load(*s, i, j) + coef_c * product(s, s, i, j))
        iterate_ref[...] = coef_a * iterate_ref[...] + times(iterate_ref[...], k)
        for i, j in pairs:
            store(*t, i, j, coef_a * load(*s, i, j) + product(s, k, i, j))
        for i, j in pairs:
            store(*s, i, j, coef_a * load(*t, i, j) + product(t, k, i, j))

    iterate = iterate_ref[...]
    side = times(iterate, s)
    iterate = coef_a * iterate + (coef_b * side + coef_c * times(side, s))
    update = factor * iterate
    update_ref[...] = update
    fresh_ref[...] = (weight_ref[...].astype(F32) - learn_rate * update).astype(BF)


def newton_schulz(gram, other, mom, weight, longest):
    rows, width = mom.shape
    vmem = pl.BlockSpec(memory_space=pltpu.VMEM)
    return pl.pallas_call(
        functools.partial(newton_kernel, 0.2 * math.sqrt(longest)),
        out_shape=(
            jax.ShapeDtypeStruct((rows, width), F32),
            jax.ShapeDtypeStruct((rows, width), BF),
        ),
        in_specs=[vmem] * 4,
        out_specs=(vmem, vmem),
        scratch_shapes=[pltpu.VMEM((width, width), BF)] * 6
        + [pltpu.VMEM((rows, width), F32), pltpu.VMEM((width, width), F32)],
        compiler_params=small(20),
        cost_estimate=pl.CostEstimate(
            flops=28 * width**3, bytes_accessed=8 * width * width, transcendentals=0
        ),
        name="newton_schulz",
    )(gram, other, mom, weight)


def after(value, *others):
    return lax.optimization_barrier((value, *others))


def ring_sum(far, near):
    rows = far.shape[0] // 2
    up3, up2, up1, mine, down1, down2, down3 = near
    copies, homes = up(far[:rows]), down(far[rows:])
    below = jnp.concatenate([add_bf(up3[:rows], copies), up3[rows:]], axis=0)
    above = jnp.concatenate([down3[:rows], add_bf(down3[rows:], homes)], axis=0)
    for near_up, near_down in ((up2, down2), (up1, down1)):
        below, above = add_bf(near_up, up(below)), add_bf(near_down, down(above))
    return mine.astype(F32) + up(below).astype(F32) + down(above).astype(F32)


def ring(block):
    rows, width = block.shape

    def one(step, carry):
        below, above, got = carry
        got = lax.dynamic_update_slice(got, below, ((4 - step) * rows, 0))
        got = lax.dynamic_update_slice(got, above, ((4 + step) * rows, 0))
        return up(below), down(above), got

    got = jnp.zeros((NZ * rows, width), block.dtype)
    far, _, got = lax.fori_loop(0, 4, one, (block, block, got))
    return lax.dynamic_update_slice(got, far, (0, 0))


def body(tokens_in, out_grads, counts, copy_list, weights, momentum):
    acts = tokens_in[0]
    grads = out_grads[0]
    model_width = acts.shape[1]
    width = grads.shape[1]
    here = jnp.stack([lax.axis_index(name) for name in ("z", "core", "x", "y")]).astype(jnp.int32)

    tokens = (counts[0], swap(counts[0]), acts, swap(acts), grads, swap(grads))
    (far,) = terms(here, *tokens, (4,))
    near = terms(here, *tokens, (3, 2, 1, 0, -1, -2, -3))
    total = ring_sum(far, near)
    rows = total.shape[0] // 2
    copy_sum, home_sum = total[:rows].astype(BF), total[rows:]

    pieces = {offset: shift(copy_sum, "y", offset) for offset in (3, 1, 2)}
    pieces = [copy_sum] + [pieces[offset] for offset in range(1, NY)]
    copies, *sent = buckets(here, copy_list, pieces)
    for ahead in (2, 1, 3):
        copies = copies + shift(sent[ahead - 1], "x", ahead).astype(F32)
    fresh_mom = beta_mom * momentum[0] + (home_sum + copies)

    own = ring(fresh_mom.astype(BF))
    gram = lax.dot_general(own, own, (((0,), (0,)), ((), ())), preferred_element_type=F32)
    update, fresh = newton_schulz(
        gram, swap(own), fresh_mom, weights[0], max(model_width, width)
    )

    pieces = {offset: shift(fresh, "x", offset) for offset in (3, 1, 2)}
    pieces = [fresh] + [pieces[offset] for offset in range(1, NX)]
    kept, *sent = wanted(here, copy_list, pieces)
    pieces = {offset: shift(sent[offset - 1], "y", offset) for offset in (2, 1, 3)}
    pieces = [kept] + [pieces[offset] for offset in range(1, NY)]
    replica = pick(here, copy_list, pieces)

    own = ring(replica)
    full = place(1, here, swap(own), place(0, here, own))
    return (fresh_mom[None], update[None], full[None])


def solution(mesh):
    grid = Mesh(mesh.devices.reshape(NZ, NC, NX, NY), ("z", "core", "x", "y"))
    split = P(("x", "y"), ("z", "core"), None)
    return jax.shard_map(
        body,
        mesh=grid,
        in_specs=(split, split, split, P(), split, split),
        out_specs=(split, split, P(("x", "y"), None, None)),
        check_vma=False,
    )
```

```python
import functools
import math

import jax
import jax.numpy as jnp
from jax import lax
from jax.experimental import pallas as pl
from jax.experimental.pallas import tpu as pltpu
from jax.sharding import Mesh, PartitionSpec as P

coef_a = 3.4445
coef_b = -4.775
coef_c = 2.0315
beta_mom = 0.95
learn_rate = 0.02
norm_eps = 1e-07

NZ, NC, NX, NY = 8, 2, 4, 4
FAR_LAST, FAR_FIRST = (0, 1, 3, 2), (0, 2, 1, 3)
BF = jnp.bfloat16
F32 = jnp.float32


def swap(value):
    return lax.ppermute(value, "core", [(0, 1), (1, 0)])


def up(value):
    return lax.ppermute(value, "z", [(i, (i + 1) % NZ) for i in range(NZ)])


def down(value):
    return lax.ppermute(value, "z", [((i + 1) % NZ, i) for i in range(NZ)])


def shift(value, axis, offset):
    return lax.ppermute(value, axis, [(i, (i + offset) % 4) for i in range(4)])


def add_bf(left, right):
    return (left.astype(F32) + right.astype(F32)).astype(BF)


SMEM = pl.BlockSpec(memory_space=pltpu.SMEM)
VMEM = pl.BlockSpec(memory_space=pltpu.VMEM)
ANY = pl.BlockSpec(memory_space=pl.ANY)
HBM = pl.BlockSpec(memory_space=pltpu.HBM)


def small(limit=8):
    return pltpu.CompilerParams(vmem_limit_bytes=limit * 1024 * 1024)


def place_kernel(side, here_ref, blocks_ref, *refs):
    out_ref, sems = refs[-2:]
    rows = blocks_ref.shape[0] // NZ
    z, core = here_ref[0], here_ref[1]
    parity = 1 - core if side else core
    copies = []
    for index in range(NZ):
        there = NC * lax.rem(z + index + NZ // 2, NZ) + parity
        copies.append(
            pltpu.make_async_copy(
                blocks_ref.at[pl.ds(index * rows, rows), :],
                out_ref.at[pl.ds(pl.multiple_of(there * rows, rows), rows), :],
                sems.at[index],
            )
        )
    for copy in copies:
        copy.start()
    for copy in copies:
        copy.wait()


def place(side, here, blocks, before=None):
    return pl.pallas_call(
        functools.partial(place_kernel, side),
        out_shape=jax.ShapeDtypeStruct((NC * blocks.shape[0], blocks.shape[1]), blocks.dtype),
        in_specs=[SMEM, VMEM] + ([] if before is None else [ANY]),
        out_specs=ANY,
        scratch_shapes=[pltpu.SemaphoreType.DMA((NZ,))],
        input_output_aliases={} if before is None else {2: 0},
        compiler_params=small(),
        name="place",
    )(here, blocks, *([] if before is None else [before]))


def bucket_kernel(here_ref, list_ref, *refs):
    pieces, outs = refs[:NY], refs[NY:]
    x, y = here_ref[2], here_ref[3]
    totals = [jnp.zeros(outs[0].shape, F32) for _ in range(NX)]
    for offset, piece in zip(FAR_LAST, pieces, strict=True):
        target = list_ref[x * NY + lax.rem(y + NY - offset, NY)]
        value = piece[...].astype(F32)
        for ahead in range(NX):
            fits = target == lax.rem(x + ahead, NX) * NY + y
            totals[ahead] = totals[ahead] + jnp.where(fits, value, 0.0)
    for out, total in zip(outs, totals, strict=True):
        out[...] = total.astype(out.dtype)


def buckets(here, copy_list, pieces):
    shape = pieces[0].shape
    return pl.pallas_call(
        bucket_kernel,
        out_shape=tuple(jax.ShapeDtypeStruct(shape, BF if k else F32) for k in range(NX)),
        in_specs=[SMEM, SMEM] + [VMEM] * NY,
        out_specs=(VMEM,) * NX,
        compiler_params=small(),
        name="buckets",
    )(here, copy_list, *pieces)


def wanted_kernel(here_ref, list_ref, *refs):
    pieces, outs = refs[:NX], refs[NX:]
    x, y = here_ref[2], here_ref[3]
    for offset, out in enumerate(outs):
        source = list_ref[x * NY + lax.rem(y + offset, NY)]
        behind = lax.rem(x + NX - lax.div(source, NY), NX)
        for k, piece in zip(FAR_LAST, pieces, strict=True):

            @pl.when(behind == k)
            def _():
                out[...] = piece[...]


def wanted(here, copy_list, pieces):
    shape = pieces[0].shape
    return pl.pallas_call(
        wanted_kernel,
        out_shape=(jax.ShapeDtypeStruct(shape, BF),) * NY,
        in_specs=[SMEM, SMEM] + [VMEM] * NX,
        out_specs=(VMEM,) * NY,
        compiler_params=small(),
        name="wanted",
    )(here, copy_list, *pieces)


def pick_kernel(here_ref, list_ref, *refs):
    pieces, out = refs[:NY], refs[NY]
    x, y = here_ref[2], here_ref[3]
    behind = lax.rem(y + NY - lax.rem(list_ref[x * NY + y], NY), NY)
    for k, piece in zip(FAR_FIRST, pieces, strict=True):

        @pl.when(behind == k)
        def _():
            out[...] = piece[...]


def pick(here, copy_list, pieces):
    return pl.pallas_call(
        pick_kernel,
        out_shape=jax.ShapeDtypeStruct(pieces[0].shape, BF),
        in_specs=[SMEM, SMEM] + [VMEM] * NY,
        out_specs=VMEM,
        compiler_params=small(),
        name="pick",
    )(here, copy_list, *pieces)


CHUNK = 64


def terms_kernel(
    offsets, here_ref, counts_ref, got_counts_ref, acts_ref, got_ref, grads_ref, got_grads_ref, *out_refs
):
    tok_rows, width = grads_ref.shape
    rows = acts_ref.shape[1] // (NZ * NC)
    z, core = here_ref[0], here_ref[1]
    starts = [
        pl.multiple_of((NC * lax.rem(z + NZ + offset, NZ) + core) * rows, rows) for offset in offsets
    ]
    slot = lax.broadcasted_iota(jnp.int32, (tok_rows, width), 0)
    totals = [None, None]
    for acts, grads, counts in (
        (acts_ref, grads_ref, counts_ref),
        (got_ref, got_grads_ref, got_counts_ref),
    ):
        home, copy = counts[0, 0], counts[0, 1]
        left = jnp.concatenate([acts[:, pl.ds(start, rows)] for start in starts], axis=1)
        value = grads[...].astype(F32)
        for which, (low, high) in enumerate(((home, home + copy), (0, home))):
            right = jnp.where((slot >= low) & (slot < high), value, 0.0).astype(BF)
            part = lax.dot_general(
                left, right, (((0,), (0,)), ((), ())), preferred_element_type=F32
            )
            totals[which] = part if totals[which] is None else totals[which] + part
    for index, out_ref in enumerate(out_refs):
        span = slice(index * rows, (index + 1) * rows)
        out_ref[:rows] = totals[0][span].astype(BF)
        out_ref[rows:] = totals[1][span].astype(BF)


def far_kernel(
    here_ref, counts_ref, got_counts_ref, acts_ref, got_ref, grads_ref, got_grads_ref, out_ref, *scratch
):
    *held, sems = scratch
    rows = out_ref.shape[0] // 2
    z, core = here_ref[0], here_ref[1]
    start = pl.multiple_of((NC * lax.rem(z + NZ // 2, NZ) + core) * rows, rows)
    sources = (
        acts_ref.at[:, pl.ds(start, rows)],
        got_ref.at[:, pl.ds(start, rows)],
        grads_ref,
        got_grads_ref,
    )
    copies = [
        pltpu.make_async_copy(source, target, sems.at[index])
        for index, (source, target) in enumerate(zip(sources, held, strict=True))
    ]
    for copy in copies:
        copy.start()
    for copy in copies:
        copy.wait()
    acts, got, grads, got_grads = held
    tok_rows, width = grads.shape
    slot = lax.broadcasted_iota(jnp.int32, (tok_rows, width), 0)
    for which in range(2):
        total = jnp.zeros((rows, width), F32)
        for left, value, counts in ((acts, grads, counts_ref), (got, got_grads, got_counts_ref)):
            home, copy = counts[0, 0], counts[0, 1]
            low, high = (0, home) if which else (home, home + copy)
            right = jnp.where((slot >= low) & (slot < high), value[...].astype(F32), 0.0).astype(BF)
            total = total + lax.dot_general(
                left[...], right, (((0,), (0,)), ((), ())), preferred_element_type=F32
            )
        out_ref[which * rows : (which + 1) * rows] = total.astype(BF)


def far_terms(here, counts, got_counts, acts, got, grads, got_grads):
    tok_rows, width = grads.shape
    rows = acts.shape[1] // (NZ * NC)
    return pl.pallas_call(
        far_kernel,
        out_shape=jax.ShapeDtypeStruct((2 * rows, width), BF),
        in_specs=[SMEM] * 3 + [HBM] * 4,
        out_specs=VMEM,
        scratch_shapes=[pltpu.VMEM((tok_rows, rows), BF)] * 2
        + [pltpu.VMEM((tok_rows, width), BF)] * 2
        + [pltpu.SemaphoreType.DMA((4,))],
        compiler_params=small(56),
        name="far_terms",
    )(here, counts, got_counts, acts, got, grads, got_grads)


def terms(here, counts, got_counts, acts, got, grads, got_grads, offsets):
    tok_rows, width = grads.shape
    rows = acts.shape[1] // (NZ * NC)
    return pl.pallas_call(
        functools.partial(terms_kernel, offsets),
        out_shape=(jax.ShapeDtypeStruct((2 * rows, width), BF),) * len(offsets),
        in_specs=[SMEM] * 3 + [VMEM] * 4,
        out_specs=(VMEM,) * len(offsets),
        compiler_params=small(20),
        cost_estimate=pl.CostEstimate(
            flops=8 * tok_rows * rows * len(offsets) * width,
            bytes_accessed=4 * tok_rows * rows * NZ,
            transcendentals=0,
        ),
        name="terms",
    )(here, counts, got_counts, acts, got, grads, got_grads)


def halves(value):
    high = value.astype(BF)
    return high, (value - high.astype(F32)).astype(BF)


def dot(left, right):
    return jnp.dot(left, right, preferred_element_type=F32)


def newton_kernel(
    factor,
    gram_ref,
    other_ref,
    mom_ref,
    weight_ref,
    update_ref,
    fresh_ref,
    s_hi,
    s_lo,
    k_hi,
    k_lo,
    t_hi,
    t_lo,
    iterate_ref,
    full_ref,
):
    width = gram_ref.shape[0]
    tile = width // 3
    spans = [slice(i * tile, (i + 1) * tile) for i in range(3)]
    pairs = [(i, j) for i in range(3) for j in range(i, 3)]

    def store(hi, lo, i, j, value):
        hi[spans[i], spans[j]], lo[spans[i], spans[j]] = halves(value)
        if i != j:
            hi[spans[j], spans[i]], lo[spans[j], spans[i]] = halves(value.T)

    def load(hi, lo, i, j):
        return hi[spans[i], spans[j]].astype(F32) + lo[spans[i], spans[j]].astype(F32)

    def product(left, right, i, j):
        (l_hi, l_lo), (r_hi, r_lo) = left, right
        rows, cols = spans[i], spans[j]
        out = dot(l_hi[rows, :], r_lo[:, cols]) + dot(l_lo[rows, :], r_hi[:, cols])
        return out + dot(l_hi[rows, :], r_hi[:, cols])

    def times(value, right):
        hi, lo = halves(value)
        r_hi, r_lo = right
        both = dot(jnp.concatenate([hi, lo], axis=0), r_hi[...])
        rows = value.shape[0]
        return both[:rows] + (both[rows:] + dot(hi, r_lo[...]))

    same = lax.broadcasted_iota(jnp.int32, (tile, tile), 0) == lax.broadcasted_iota(
        jnp.int32, (tile, tile), 1
    )

    def add_other(index, total):
        span = pl.ds(pl.multiple_of(index * tile, tile), tile)
        full_ref[span, :] = gram_ref[span, :] + lax.dot_general(
            other_ref[:, span],
            other_ref[...],
            (((0,), (0,)), ((), ())),
            preferred_element_type=F32,
        )
        on = jnp.where(same, full_ref[span, span], 0.0)
        return total + jnp.sum(jnp.sum(on, axis=1, keepdims=True), axis=0, keepdims=True)

    total = lax.fori_loop(0, 3, add_other, jnp.zeros((1, 1), F32))
    scale = 1.0 / (jnp.sqrt(total) + norm_eps)

    @pl.loop(0, width // CHUNK)
    def _(index):
        chunk = pl.ds(pl.multiple_of(index * CHUNK, CHUNK), CHUNK)
        s_hi[chunk, :], s_lo[chunk, :] = halves(full_ref[chunk, :] * scale * scale)

    iterate_ref[...] = mom_ref[...] * scale
    s, k, t = (s_hi, s_lo), (k_hi, k_lo), (t_hi, t_lo)

    @pl.loop(0, 2)
    def _(step):
        for i, j in pairs:
            store(*k, i, j, coef_b * load(*s, i, j) + coef_c * product(s, s, i, j))
        iterate_ref[...] = coef_a * iterate_ref[...] + times(iterate_ref[...], k)
        for i, j in pairs:
            store(*t, i, j, coef_a * load(*s, i, j) + product(s, k, i, j))
        for i, j in pairs:
            store(*s, i, j, coef_a * load(*t, i, j) + product(t, k, i, j))

    iterate = iterate_ref[...]
    side = times(iterate, s)
    iterate = coef_a * iterate + (coef_b * side + coef_c * times(side, s))
    update = factor * iterate
    update_ref[...] = update
    fresh_ref[...] = (weight_ref[...].astype(F32) - learn_rate * update).astype(BF)


def newton_schulz(gram, other, mom, weight, longest):
    rows, width = mom.shape
    vmem = pl.BlockSpec(memory_space=pltpu.VMEM)
    return pl.pallas_call(
        functools.partial(newton_kernel, 0.2 * math.sqrt(longest)),
        out_shape=(
            jax.ShapeDtypeStruct((rows, width), F32),
            jax.ShapeDtypeStruct((rows, width), BF),
        ),
        in_specs=[vmem] * 4,
        out_specs=(vmem, vmem),
        scratch_shapes=[pltpu.VMEM((width, width), BF)] * 6
        + [pltpu.VMEM((rows, width), F32), pltpu.VMEM((width, width), F32)],
        compiler_params=small(20),
        cost_estimate=pl.CostEstimate(
            flops=28 * width**3, bytes_accessed=8 * width * width, transcendentals=0
        ),
        name="newton_schulz",
    )(gram, other, mom, weight)


def after(value, *others):
    return lax.optimization_barrier((value, *others))


def ring_sum(far, near):
    rows = far.shape[0] // 2
    up3, up2, up1, mine, down1, down2, down3 = near
    copies, homes = up(far[:rows]), down(far[rows:])
    below = jnp.concatenate([add_bf(up3[:rows], copies), up3[rows:]], axis=0)
    above = jnp.concatenate([down3[:rows], add_bf(down3[rows:], homes)], axis=0)
    on_up = jnp.stack([up2, up1, mine])
    on_down = jnp.stack([down2, down1, jnp.zeros_like(mine)])

    def one(step, carry):
        below, above = carry
        below, above = up(below), down(above)
        return add_bf(below, on_up[step]), add_bf(above, on_down[step])

    below, above = lax.fori_loop(0, 3, one, (below, above))
    return below.astype(F32) + above.astype(F32)


def ring(block):
    rows, width = block.shape

    def one(step, carry):
        below, above, got = carry
        got = lax.dynamic_update_slice(got, below, ((4 - step) * rows, 0))
        got = lax.dynamic_update_slice(got, above, ((4 + step) * rows, 0))
        return up(below), down(above), got

    got = jnp.zeros((NZ * rows, width), block.dtype)
    far, _, got = lax.fori_loop(0, 4, one, (block, block, got))
    return lax.dynamic_update_slice(got, far, (0, 0))


def free_ring(block):
    below, above = [block], [block]
    for _ in range(3):
        below.append(up(below[-1]))
        above.append(down(above[-1]))
    far = up(below[-1])
    return jnp.concatenate([far, *below[:0:-1], *above], axis=0)


def body(tokens_in, out_grads, counts, copy_list, weights, momentum):
    acts = tokens_in[0]
    grads = out_grads[0]
    model_width = acts.shape[1]
    width = grads.shape[1]
    here = jnp.stack([lax.axis_index(name) for name in ("z", "core", "x", "y")]).astype(jnp.int32)

    tokens = (counts[0], swap(counts[0]), acts, swap(acts), grads, swap(grads))
    far = far_terms(here, *tokens)
    near = terms(here, *tokens, (3, 2, 1, 0, -1, -2, -3))
    total = ring_sum(far, near)
    rows = total.shape[0] // 2
    copy_sum, home_sum = total[:rows].astype(BF), total[rows:]

    pieces = [copy_sum] + [shift(copy_sum, "y", offset) for offset in FAR_LAST[1:]]
    copies, *sent = buckets(here, copy_list, pieces)
    for ahead in (2, 1, 3):
        copies = copies + shift(sent[ahead - 1], "x", ahead).astype(F32)
    fresh_mom = beta_mom * momentum[0] + (home_sum + copies)

    own = ring(fresh_mom.astype(BF))
    gram = lax.dot_general(own, own, (((0,), (0,)), ((), ())), preferred_element_type=F32)
    update, fresh = newton_schulz(
        gram, swap(own), fresh_mom, weights[0], max(model_width, width)
    )

    pieces = [fresh] + [shift(fresh, "x", offset) for offset in FAR_LAST[1:]]
    kept, *sent = wanted(here, copy_list, pieces)
    pieces = [kept] + [shift(sent[offset - 1], "y", offset) for offset in FAR_FIRST[1:]]
    replica = pick(here, copy_list, pieces)

    own = free_ring(replica)
    full = place(1, here, swap(own), place(0, here, own))
    return (fresh_mom[None], update[None], full[None])


def solution(mesh):
    grid = Mesh(mesh.devices.reshape(NZ, NC, NX, NY), ("z", "core", "x", "y"))
    split = P(("x", "y"), ("z", "core"), None)
    return jax.shard_map(
        body,
        mesh=grid,
        in_specs=(split, split, split, P(), split, split),
        out_specs=(split, split, P(("x", "y"), None, None)),
        check_vma=False,
    )
```

```python
import functools
import math

import jax
import jax.numpy as jnp
from jax import lax
from jax.experimental import pallas as pl
from jax.experimental.pallas import tpu as pltpu
from jax.sharding import Mesh, PartitionSpec as P

coef_a = 3.4445
coef_b = -4.775
coef_c = 2.0315
beta_mom = 0.95
learn_rate = 0.02
norm_eps = 1e-07

NZ, NC, NX, NY = 8, 2, 4, 4
FAR_LAST, FAR_FIRST = (0, 1, 3, 2), (0, 2, 1, 3)
BF = jnp.bfloat16
F32 = jnp.float32


def swap(value):
    return lax.ppermute(value, "core", [(0, 1), (1, 0)])


def up(value):
    return lax.ppermute(value, "z", [(i, (i + 1) % NZ) for i in range(NZ)])


def down(value):
    return lax.ppermute(value, "z", [((i + 1) % NZ, i) for i in range(NZ)])


def shift(value, axis, offset):
    return lax.ppermute(value, axis, [(i, (i + offset) % 4) for i in range(4)])


def add_bf(left, right):
    return (left.astype(F32) + right.astype(F32)).astype(BF)


SMEM = pl.BlockSpec(memory_space=pltpu.SMEM)
VMEM = pl.BlockSpec(memory_space=pltpu.VMEM)
ANY = pl.BlockSpec(memory_space=pl.ANY)


def small(limit=8):
    return pltpu.CompilerParams(vmem_limit_bytes=limit * 1024 * 1024)


def place_kernel(side, here_ref, blocks_ref, *refs):
    out_ref, sems = refs[-2:]
    rows = blocks_ref.shape[0] // NZ
    z, core = here_ref[0], here_ref[1]
    parity = 1 - core if side else core
    copies = []
    for index in range(NZ):
        there = NC * lax.rem(z + index + NZ // 2, NZ) + parity
        copies.append(
            pltpu.make_async_copy(
                blocks_ref.at[pl.ds(index * rows, rows), :],
                out_ref.at[pl.ds(pl.multiple_of(there * rows, rows), rows), :],
                sems.at[index],
            )
        )
    for copy in copies:
        copy.start()
    for copy in copies:
        copy.wait()


def place(side, here, blocks, before=None):
    return pl.pallas_call(
        functools.partial(place_kernel, side),
        out_shape=jax.ShapeDtypeStruct((NC * blocks.shape[0], blocks.shape[1]), blocks.dtype),
        in_specs=[SMEM, VMEM] + ([] if before is None else [ANY]),
        out_specs=ANY,
        scratch_shapes=[pltpu.SemaphoreType.DMA((NZ,))],
        input_output_aliases={} if before is None else {2: 0},
        compiler_params=small(),
        name="place",
    )(here, blocks, *([] if before is None else [before]))


def bucket_kernel(here_ref, list_ref, *refs):
    pieces, outs = refs[:NY], refs[NY:]
    x, y = here_ref[2], here_ref[3]
    totals = [jnp.zeros(outs[0].shape, F32) for _ in range(NX)]
    for offset, piece in zip(FAR_LAST, pieces, strict=True):
        target = list_ref[x * NY + lax.rem(y + NY - offset, NY)]
        value = piece[...].astype(F32)
        for ahead in range(NX):
            fits = target == lax.rem(x + ahead, NX) * NY + y
            totals[ahead] = totals[ahead] + jnp.where(fits, value, 0.0)
    for out, total in zip(outs, totals, strict=True):
        out[...] = total.astype(out.dtype)


def buckets(here, copy_list, pieces):
    shape = pieces[0].shape
    return pl.pallas_call(
        bucket_kernel,
        out_shape=tuple(jax.ShapeDtypeStruct(shape, BF if k else F32) for k in range(NX)),
        in_specs=[SMEM, SMEM] + [VMEM] * NY,
        out_specs=(VMEM,) * NX,
        compiler_params=small(),
        name="buckets",
    )(here, copy_list, *pieces)


def wanted_kernel(here_ref, list_ref, *refs):
    pieces, outs = refs[:NX], refs[NX:]
    x, y = here_ref[2], here_ref[3]
    for offset, out in enumerate(outs):
        source = list_ref[x * NY + lax.rem(y + offset, NY)]
        behind = lax.rem(x + NX - lax.div(source, NY), NX)
        for k, piece in zip(FAR_LAST, pieces, strict=True):

            @pl.when(behind == k)
            def _():
                out[...] = piece[...]


def wanted(here, copy_list, pieces):
    shape = pieces[0].shape
    return pl.pallas_call(
        wanted_kernel,
        out_shape=(jax.ShapeDtypeStruct(shape, BF),) * NY,
        in_specs=[SMEM, SMEM] + [VMEM] * NX,
        out_specs=(VMEM,) * NY,
        compiler_params=small(),
        name="wanted",
    )(here, copy_list, *pieces)


def pick_kernel(here_ref, list_ref, *refs):
    pieces, out = refs[:NY], refs[NY]
    x, y = here_ref[2], here_ref[3]
    behind = lax.rem(y + NY - lax.rem(list_ref[x * NY + y], NY), NY)
    for k, piece in zip(FAR_FIRST, pieces, strict=True):

        @pl.when(behind == k)
        def _():
            out[...] = piece[...]


def pick(here, copy_list, pieces):
    return pl.pallas_call(
        pick_kernel,
        out_shape=jax.ShapeDtypeStruct(pieces[0].shape, BF),
        in_specs=[SMEM, SMEM] + [VMEM] * NY,
        out_specs=VMEM,
        compiler_params=small(),
        name="pick",
    )(here, copy_list, *pieces)


CHUNK = 64


def terms_kernel(
    offsets, here_ref, counts_ref, got_counts_ref, acts_ref, got_ref, grads_ref, got_grads_ref, *out_refs
):
    tok_rows, width = grads_ref.shape
    rows = acts_ref.shape[1] // (NZ * NC)
    z, core = here_ref[0], here_ref[1]
    starts = [
        pl.multiple_of((NC * lax.rem(z + NZ + offset, NZ) + core) * rows, rows) for offset in offsets
    ]
    slot = lax.broadcasted_iota(jnp.int32, (tok_rows, width), 0)
    totals = [None, None]
    for acts, grads, counts in (
        (acts_ref, grads_ref, counts_ref),
        (got_ref, got_grads_ref, got_counts_ref),
    ):
        home, copy = counts[0, 0], counts[0, 1]
        left = jnp.concatenate([acts[:, pl.ds(start, rows)] for start in starts], axis=1)
        value = grads[...].astype(F32)
        for which, (low, high) in enumerate(((home, home + copy), (0, home))):
            right = jnp.where((slot >= low) & (slot < high), value, 0.0).astype(BF)
            part = lax.dot_general(
                left, right, (((0,), (0,)), ((), ())), preferred_element_type=F32
            )
            totals[which] = part if totals[which] is None else totals[which] + part
    for index, out_ref in enumerate(out_refs):
        span = slice(index * rows, (index + 1) * rows)
        out_ref[:rows] = totals[0][span].astype(BF)
        out_ref[rows:] = totals[1][span].astype(BF)


def far_kernel(here_ref, counts_ref, acts_ref, grads_ref, *refs):
    *before, copy_ref, home_ref = refs
    rows = copy_ref.shape[0]
    tok_rows, width = grads_ref.shape
    z, core = here_ref[0], here_ref[1]
    start = pl.multiple_of((NC * lax.rem(z + NZ // 2, NZ) + core) * rows, rows)
    left = acts_ref[:, pl.ds(start, rows)]
    slot = lax.broadcasted_iota(jnp.int32, (tok_rows, width), 0)
    home, copy = counts_ref[0, 0], counts_ref[0, 1]
    value = grads_ref[...].astype(F32)
    for which, (low, high, out_ref) in enumerate(
        ((home, home + copy, copy_ref), (0, home, home_ref))
    ):
        right = jnp.where((slot >= low) & (slot < high), value, 0.0).astype(BF)
        total = lax.dot_general(
            left, right, (((0,), (0,)), ((), ())), preferred_element_type=F32
        )
        if before:
            total = total + before[which][...]
        out_ref[...] = total.astype(out_ref.dtype)


def far_terms(here, counts, acts, grads, before=()):
    tok_rows, width = grads.shape
    rows = acts.shape[1] // (NZ * NC)
    return pl.pallas_call(
        far_kernel,
        out_shape=(jax.ShapeDtypeStruct((rows, width), BF if before else F32),) * 2,
        in_specs=[SMEM] * 2 + [VMEM] * (2 + len(before)),
        out_specs=(VMEM, VMEM),
        compiler_params=small(),
        cost_estimate=pl.CostEstimate(
            flops=4 * tok_rows * rows * width, bytes_accessed=4 * tok_rows * width, transcendentals=0
        ),
        name="far_terms",
    )(here, counts, acts, grads, *before)


def terms(here, counts, got_counts, acts, got, grads, got_grads, offsets):
    tok_rows, width = grads.shape
    rows = acts.shape[1] // (NZ * NC)
    return pl.pallas_call(
        functools.partial(terms_kernel, offsets),
        out_shape=(jax.ShapeDtypeStruct((2 * rows, width), BF),) * len(offsets),
        in_specs=[SMEM] * 3 + [VMEM] * 4,
        out_specs=(VMEM,) * len(offsets),
        compiler_params=small(20),
        cost_estimate=pl.CostEstimate(
            flops=8 * tok_rows * rows * len(offsets) * width,
            bytes_accessed=4 * tok_rows * rows * NZ,
            transcendentals=0,
        ),
        name="terms",
    )(here, counts, got_counts, acts, got, grads, got_grads)


def halves(value):
    high = value.astype(BF)
    return high, (value - high.astype(F32)).astype(BF)


def dot(left, right):
    return jnp.dot(left, right, preferred_element_type=F32)


def newton_kernel(
    factor,
    gram_ref,
    other_ref,
    mom_ref,
    weight_ref,
    update_ref,
    fresh_ref,
    s_hi,
    s_lo,
    k_hi,
    k_lo,
    t_hi,
    t_lo,
    iterate_ref,
    full_ref,
):
    width = gram_ref.shape[0]
    tile = width // 3
    spans = [slice(i * tile, (i + 1) * tile) for i in range(3)]
    pairs = [(i, j) for i in range(3) for j in range(i, 3)]

    def store(hi, lo, i, j, value):
        hi[spans[i], spans[j]], lo[spans[i], spans[j]] = halves(value)
        if i != j:
            hi[spans[j], spans[i]], lo[spans[j], spans[i]] = halves(value.T)

    def load(hi, lo, i, j):
        return hi[spans[i], spans[j]].astype(F32) + lo[spans[i], spans[j]].astype(F32)

    def product(left, right, i, j):
        (l_hi, l_lo), (r_hi, r_lo) = left, right
        rows, cols = spans[i], spans[j]
        out = dot(l_hi[rows, :], r_lo[:, cols]) + dot(l_lo[rows, :], r_hi[:, cols])
        return out + dot(l_hi[rows, :], r_hi[:, cols])

    def times(value, right):
        hi, lo = halves(value)
        r_hi, r_lo = right
        both = dot(jnp.concatenate([hi, lo], axis=0), r_hi[...])
        rows = value.shape[0]
        return both[:rows] + (both[rows:] + dot(hi, r_lo[...]))

    same = lax.broadcasted_iota(jnp.int32, (tile, tile), 0) == lax.broadcasted_iota(
        jnp.int32, (tile, tile), 1
    )
    total = jnp.zeros((1, 1), F32)
    for span in spans:
        value = gram_ref[span, :] + lax.dot_general(
            other_ref[:, span],
            other_ref[...],
            (((0,), (0,)), ((), ())),
            preferred_element_type=F32,
        )
        full_ref[span, :] = value
        on = jnp.where(same, value[:, span], 0.0)
        total = total + jnp.sum(jnp.sum(on, axis=1, keepdims=True), axis=0, keepdims=True)
    scale = 1.0 / (jnp.sqrt(total) + norm_eps)

    @pl.loop(0, width // CHUNK)
    def _(index):
        chunk = pl.ds(pl.multiple_of(index * CHUNK, CHUNK), CHUNK)
        s_hi[chunk, :], s_lo[chunk, :] = halves(full_ref[chunk, :] * scale * scale)

    iterate_ref[...] = mom_ref[...] * scale
    s, k, t = (s_hi, s_lo), (k_hi, k_lo), (t_hi, t_lo)

    @pl.loop(0, 2)
    def _(step):
        for i, j in pairs:
            store(*k, i, j, coef_b * load(*s, i, j) + coef_c * product(s, s, i, j))
        iterate_ref[...] = coef_a * iterate_ref[...] + times(iterate_ref[...], k)
        for i, j in pairs:
            store(*t, i, j, coef_a * load(*s, i, j) + product(s, k, i, j))
        for i, j in pairs:
            store(*s, i, j, coef_a * load(*t, i, j) + product(t, k, i, j))

    iterate = iterate_ref[...]
    side = times(iterate, s)
    iterate = coef_a * iterate + (coef_b * side + coef_c * times(side, s))
    update = factor * iterate
    update_ref[...] = update
    fresh_ref[...] = (weight_ref[...].astype(F32) - learn_rate * update).astype(BF)


def newton_schulz(gram, other, mom, weight, longest):
    rows, width = mom.shape
    vmem = pl.BlockSpec(memory_space=pltpu.VMEM)
    return pl.pallas_call(
        functools.partial(newton_kernel, 0.2 * math.sqrt(longest)),
        out_shape=(
            jax.ShapeDtypeStruct((rows, width), F32),
            jax.ShapeDtypeStruct((rows, width), BF),
        ),
        in_specs=[vmem] * 4,
        out_specs=(vmem, vmem),
        scratch_shapes=[pltpu.VMEM((width, width), BF)] * 6
        + [pltpu.VMEM((rows, width), F32), pltpu.VMEM((width, width), F32)],
        compiler_params=small(20),
        cost_estimate=pl.CostEstimate(
            flops=28 * width**3, bytes_accessed=8 * width * width, transcendentals=0
        ),
        name="newton_schulz",
    )(gram, other, mom, weight)


def after(value, *others):
    return lax.optimization_barrier((value, *others))


def ring_sum(far, near):
    rows = far[0].shape[0]
    up3, up2, up1, mine, down1, down2, down3 = near
    copies, homes = up(far[0]), down(far[1])
    below = jnp.concatenate([add_bf(up3[:rows], copies), up3[rows:]], axis=0)
    above = jnp.concatenate([down3[:rows], add_bf(down3[rows:], homes)], axis=0)
    for near_up, near_down in ((up2, down2), (up1, down1)):
        below, above = add_bf(near_up, up(below)), add_bf(near_down, down(above))
    return mine.astype(F32) + up(below).astype(F32) + down(above).astype(F32)


def ring(block):
    rows, width = block.shape

    def one(step, carry):
        below, above, got = carry
        got = lax.dynamic_update_slice(got, below, ((4 - step) * rows, 0))
        got = lax.dynamic_update_slice(got, above, ((4 + step) * rows, 0))
        return up(below), down(above), got

    got = jnp.zeros((NZ * rows, width), block.dtype)
    far, _, got = lax.fori_loop(0, 4, one, (block, block, got))
    return lax.dynamic_update_slice(got, far, (0, 0))


def body(tokens_in, out_grads, counts, copy_list, weights, momentum):
    acts = tokens_in[0]
    grads = out_grads[0]
    model_width = acts.shape[1]
    width = grads.shape[1]
    here = jnp.stack([lax.axis_index(name) for name in ("z", "core", "x", "y")]).astype(jnp.int32)

    tokens = (counts[0], swap(counts[0]), acts, swap(acts), grads, swap(grads))
    got_counts, got, got_grads = tokens[1::2]
    far = far_terms(here, counts[0], acts, grads)
    far = far_terms(here, got_counts, got, got_grads, far)
    near = terms(here, *tokens, (3, 2, 1, 0, -1, -2, -3))
    total = ring_sum(far, near)
    rows = total.shape[0] // 2
    copy_sum, home_sum = total[:rows].astype(BF), total[rows:]

    pieces = [copy_sum] + [shift(copy_sum, "y", offset) for offset in FAR_LAST[1:]]
    copies, *sent = buckets(here, copy_list, pieces)
    for ahead in (2, 1, 3):
        copies = copies + shift(sent[ahead - 1], "x", ahead).astype(F32)
    fresh_mom = beta_mom * momentum[0] + (home_sum + copies)

    own = ring(fresh_mom.astype(BF))
    gram = lax.dot_general(own, own, (((0,), (0,)), ((), ())), preferred_element_type=F32)
    update, fresh = newton_schulz(
        gram, swap(own), fresh_mom, weights[0], max(model_width, width)
    )

    pieces = [fresh] + [shift(fresh, "x", offset) for offset in FAR_LAST[1:]]
    kept, *sent = wanted(here, copy_list, pieces)
    pieces = [kept] + [shift(sent[offset - 1], "y", offset) for offset in FAR_FIRST[1:]]
    replica = pick(here, copy_list, pieces)

    own = ring(replica)
    full = place(1, here, swap(own), place(0, here, own))
    return (fresh_mom[None], update[None], full[None])


def solution(mesh):
    grid = Mesh(mesh.devices.reshape(NZ, NC, NX, NY), ("z", "core", "x", "y"))
    split = P(("x", "y"), ("z", "core"), None)
    return jax.shard_map(
        body,
        mesh=grid,
        in_specs=(split, split, split, P(), split, split),
        out_specs=(split, split, P(("x", "y"), None, None)),
        check_vma=False,
    )
```

```python
import functools
import math

import jax
import jax.numpy as jnp
from jax import lax
from jax.experimental import pallas as pl
from jax.experimental.pallas import tpu as pltpu
from jax.sharding import Mesh, PartitionSpec as P

coef_a = 3.4445
coef_b = -4.775
coef_c = 2.0315
beta_mom = 0.95
learn_rate = 0.02
norm_eps = 1e-07

NZ, NC, NX, NY = 8, 2, 4, 4
FAR_LAST, FAR_FIRST = (0, 1, 3, 2), (0, 2, 1, 3)
BF = jnp.bfloat16
F32 = jnp.float32


def swap(value):
    return lax.ppermute(value, "core", [(0, 1), (1, 0)])


def up(value):
    return lax.ppermute(value, "z", [(i, (i + 1) % NZ) for i in range(NZ)])


def down(value):
    return lax.ppermute(value, "z", [((i + 1) % NZ, i) for i in range(NZ)])


def shift(value, axis, offset):
    return lax.ppermute(value, axis, [(i, (i + offset) % 4) for i in range(4)])


def add_bf(left, right):
    return (left.astype(F32) + right.astype(F32)).astype(BF)


SMEM = pl.BlockSpec(memory_space=pltpu.SMEM)
VMEM = pl.BlockSpec(memory_space=pltpu.VMEM)
ANY = pl.BlockSpec(memory_space=pl.ANY)


def small(limit=8):
    return pltpu.CompilerParams(vmem_limit_bytes=limit * 1024 * 1024)


def place_kernel(side, here_ref, blocks_ref, *refs):
    out_ref, sems = refs[-2:]
    rows = blocks_ref.shape[0] // NZ
    z, core = here_ref[0], here_ref[1]
    parity = 1 - core if side else core
    copies = []
    for index in range(NZ):
        there = NC * lax.rem(z + index + NZ // 2, NZ) + parity
        copies.append(
            pltpu.make_async_copy(
                blocks_ref.at[pl.ds(index * rows, rows), :],
                out_ref.at[pl.ds(pl.multiple_of(there * rows, rows), rows), :],
                sems.at[index],
            )
        )
    for copy in copies:
        copy.start()
    for copy in copies:
        copy.wait()


def place(side, here, blocks, before=None):
    return pl.pallas_call(
        functools.partial(place_kernel, side),
        out_shape=jax.ShapeDtypeStruct((NC * blocks.shape[0], blocks.shape[1]), blocks.dtype),
        in_specs=[SMEM, VMEM] + ([] if before is None else [ANY]),
        out_specs=ANY,
        scratch_shapes=[pltpu.SemaphoreType.DMA((NZ,))],
        input_output_aliases={} if before is None else {2: 0},
        compiler_params=small(),
        name="place",
    )(here, blocks, *([] if before is None else [before]))


def bucket_kernel(here_ref, list_ref, *refs):
    pieces, outs = refs[:NY], refs[NY:]
    x, y = here_ref[2], here_ref[3]
    totals = [jnp.zeros(outs[0].shape, F32) for _ in range(NX)]
    for offset, piece in zip(FAR_LAST, pieces, strict=True):
        target = list_ref[x * NY + lax.rem(y + NY - offset, NY)]
        value = piece[...].astype(F32)
        for ahead in range(NX):
            fits = target == lax.rem(x + ahead, NX) * NY + y
            totals[ahead] = totals[ahead] + jnp.where(fits, value, 0.0)
    for out, total in zip(outs, totals, strict=True):
        out[...] = total.astype(out.dtype)


def buckets(here, copy_list, pieces):
    shape = pieces[0].shape
    return pl.pallas_call(
        bucket_kernel,
        out_shape=tuple(jax.ShapeDtypeStruct(shape, BF if k else F32) for k in range(NX)),
        in_specs=[SMEM, SMEM] + [VMEM] * NY,
        out_specs=(VMEM,) * NX,
        compiler_params=small(),
        name="buckets",
    )(here, copy_list, *pieces)


def wanted_kernel(here_ref, list_ref, *refs):
    pieces, outs = refs[:NX], refs[NX:]
    x, y = here_ref[2], here_ref[3]
    for offset, out in enumerate(outs):
        source = list_ref[x * NY + lax.rem(y + offset, NY)]
        behind = lax.rem(x + NX - lax.div(source, NY), NX)
        for k, piece in zip(FAR_LAST, pieces, strict=True):

            @pl.when(behind == k)
            def _():
                out[...] = piece[...]


def wanted(here, copy_list, pieces):
    shape = pieces[0].shape
    return pl.pallas_call(
        wanted_kernel,
        out_shape=(jax.ShapeDtypeStruct(shape, BF),) * NY,
        in_specs=[SMEM, SMEM] + [VMEM] * NX,
        out_specs=(VMEM,) * NY,
        compiler_params=small(),
        name="wanted",
    )(here, copy_list, *pieces)


def pick_kernel(here_ref, list_ref, *refs):
    pieces, out = refs[:NY], refs[NY]
    x, y = here_ref[2], here_ref[3]
    behind = lax.rem(y + NY - lax.rem(list_ref[x * NY + y], NY), NY)
    for k, piece in zip(FAR_FIRST, pieces, strict=True):

        @pl.when(behind == k)
        def _():
            out[...] = piece[...]


def pick(here, copy_list, pieces):
    return pl.pallas_call(
        pick_kernel,
        out_shape=jax.ShapeDtypeStruct(pieces[0].shape, BF),
        in_specs=[SMEM, SMEM] + [VMEM] * NY,
        out_specs=VMEM,
        compiler_params=small(),
        name="pick",
    )(here, copy_list, *pieces)


CHUNK = 64


def terms_kernel(
    offsets, here_ref, counts_ref, got_counts_ref, acts_ref, got_ref, grads_ref, got_grads_ref, *out_refs
):
    tok_rows, width = grads_ref.shape
    rows = acts_ref.shape[1] // (NZ * NC)
    z, core = here_ref[0], here_ref[1]
    starts = [
        pl.multiple_of((NC * lax.rem(z + NZ + offset, NZ) + core) * rows, rows) for offset in offsets
    ]
    slot = lax.broadcasted_iota(jnp.int32, (tok_rows, width), 0)
    totals = [None, None]
    for acts, grads, counts in (
        (acts_ref, grads_ref, counts_ref),
        (got_ref, got_grads_ref, got_counts_ref),
    ):
        home, copy = counts[0, 0], counts[0, 1]
        left = jnp.concatenate([acts[:, pl.ds(start, rows)] for start in starts], axis=1)
        value = grads[...].astype(F32)
        for which, (low, high) in enumerate(((home, home + copy), (0, home))):
            right = jnp.where((slot >= low) & (slot < high), value, 0.0).astype(BF)
            part = lax.dot_general(
                left, right, (((0,), (0,)), ((), ())), preferred_element_type=F32
            )
            totals[which] = part if totals[which] is None else totals[which] + part
    for index, out_ref in enumerate(out_refs):
        span = slice(index * rows, (index + 1) * rows)
        out_ref[:rows] = totals[0][span].astype(BF)
        out_ref[rows:] = totals[1][span].astype(BF)


def far_kernel(here_ref, counts_ref, acts_ref, grads_ref, *refs):
    *before, copy_ref, home_ref = refs
    rows = copy_ref.shape[0]
    tok_rows, width = grads_ref.shape
    z, core = here_ref[0], here_ref[1]
    start = pl.multiple_of((NC * lax.rem(z + NZ // 2, NZ) + core) * rows, rows)
    left = acts_ref[:, pl.ds(start, rows)]
    slot = lax.broadcasted_iota(jnp.int32, (tok_rows, width), 0)
    home, copy = counts_ref[0, 0], counts_ref[0, 1]
    value = grads_ref[...].astype(F32)
    for which, (low, high, out_ref) in enumerate(
        ((home, home + copy, copy_ref), (0, home, home_ref))
    ):
        right = jnp.where((slot >= low) & (slot < high), value, 0.0).astype(BF)
        total = lax.dot_general(
            left, right, (((0,), (0,)), ((), ())), preferred_element_type=F32
        )
        if before:
            total = total + before[which][...]
        out_ref[...] = total.astype(out_ref.dtype)


def far_terms(here, counts, acts, grads, before=()):
    tok_rows, width = grads.shape
    rows = acts.shape[1] // (NZ * NC)
    return pl.pallas_call(
        far_kernel,
        out_shape=(jax.ShapeDtypeStruct((rows, width), BF if before else F32),) * 2,
        in_specs=[SMEM] * 2 + [VMEM] * (2 + len(before)),
        out_specs=(VMEM, VMEM),
        compiler_params=small(),
        cost_estimate=pl.CostEstimate(
            flops=4 * tok_rows * rows * width, bytes_accessed=4 * tok_rows * width, transcendentals=0
        ),
        name="far_terms",
    )(here, counts, acts, grads, *before)


def terms(here, counts, got_counts, acts, got, grads, got_grads, offsets):
    tok_rows, width = grads.shape
    rows = acts.shape[1] // (NZ * NC)
    return pl.pallas_call(
        functools.partial(terms_kernel, offsets),
        out_shape=(jax.ShapeDtypeStruct((2 * rows, width), BF),) * len(offsets),
        in_specs=[SMEM] * 3 + [VMEM] * 4,
        out_specs=(VMEM,) * len(offsets),
        compiler_params=small(20),
        cost_estimate=pl.CostEstimate(
            flops=8 * tok_rows * rows * len(offsets) * width,
            bytes_accessed=4 * tok_rows * rows * NZ,
            transcendentals=0,
        ),
        name="terms",
    )(here, counts, got_counts, acts, got, grads, got_grads)


def halves(value):
    high = value.astype(BF)
    return high, (value - high.astype(F32)).astype(BF)


def dot(left, right):
    return jnp.dot(left, right, preferred_element_type=F32)


def newton_kernel(
    factor,
    gram_ref,
    other_ref,
    mom_ref,
    weight_ref,
    update_ref,
    fresh_ref,
    s_hi,
    s_lo,
    k_hi,
    k_lo,
    t_hi,
    t_lo,
    iterate_ref,
    side_ref,
    full_ref,
):
    width = gram_ref.shape[0]
    tile = width // 3
    spans = [slice(i * tile, (i + 1) * tile) for i in range(3)]
    pairs = [(i, j) for i in range(3) for j in range(i, 3)]

    def store(hi, lo, i, j, value):
        hi[spans[i], spans[j]], lo[spans[i], spans[j]] = halves(value)
        if i != j:
            hi[spans[j], spans[i]], lo[spans[j], spans[i]] = halves(value.T)

    def load(hi, lo, i, j):
        return hi[spans[i], spans[j]].astype(F32) + lo[spans[i], spans[j]].astype(F32)

    def product(left, right, i, j):
        (l_hi, l_lo), (r_hi, r_lo) = left, right
        rows, cols = spans[i], spans[j]
        out = dot(l_hi[rows, :], r_lo[:, cols]) + dot(l_lo[rows, :], r_hi[:, cols])
        return out + dot(l_hi[rows, :], r_hi[:, cols])

    def times(value, right):
        hi, lo = halves(value)
        r_hi, r_lo = right
        both = dot(jnp.concatenate([hi, lo], axis=0), r_hi[...])
        rows = value.shape[0]
        return both[:rows] + (both[rows:] + dot(hi, r_lo[...]))

    same = lax.broadcasted_iota(jnp.int32, (tile, tile), 0) == lax.broadcasted_iota(
        jnp.int32, (tile, tile), 1
    )
    total = jnp.zeros((1, 1), F32)
    for span in spans:
        value = gram_ref[span, :] + lax.dot_general(
            other_ref[:, span],
            other_ref[...],
            (((0,), (0,)), ((), ())),
            preferred_element_type=F32,
        )
        full_ref[span, :] = value
        on = jnp.where(same, value[:, span], 0.0)
        total = total + jnp.sum(jnp.sum(on, axis=1, keepdims=True), axis=0, keepdims=True)
    scale = 1.0 / (jnp.sqrt(total) + norm_eps)

    @pl.loop(0, width // CHUNK)
    def _(index):
        chunk = pl.ds(pl.multiple_of(index * CHUNK, CHUNK), CHUNK)
        s_hi[chunk, :], s_lo[chunk, :] = halves(full_ref[chunk, :] * scale * scale)

    iterate_ref[...] = mom_ref[...] * scale
    s, k, t = (s_hi, s_lo), (k_hi, k_lo), (t_hi, t_lo)

    @pl.loop(0, 2)
    def _(step):
        for i, j in pairs:
            store(*k, i, j, coef_b * load(*s, i, j) + coef_c * product(s, s, i, j))
        iterate_ref[...] = coef_a * iterate_ref[...] + times(iterate_ref[...], k)

        @pl.when(step == 0)
        def _():
            for i, j in pairs:
                store(*t, i, j, coef_a * load(*s, i, j) + product(s, k, i, j))
            for i, j in pairs:
                store(*s, i, j, coef_a * load(*t, i, j) + product(t, k, i, j))

    side_ref[...] = iterate_ref[...]
    iterate_ref[...] = coef_a * iterate_ref[...]

    @pl.loop(0, 2)
    def _(index):
        side = side_ref[...]
        side = times(coef_a * side + times(side, k), s)
        side = coef_a * side + times(side, k)
        side_ref[...] = side
        iterate_ref[...] += jnp.where(index == 0, coef_b, coef_c) * side

    iterate = iterate_ref[...]
    update = factor * iterate
    update_ref[...] = update
    fresh_ref[...] = (weight_ref[...].astype(F32) - learn_rate * update).astype(BF)


def newton_schulz(gram, other, mom, weight, longest):
    rows, width = mom.shape
    vmem = pl.BlockSpec(memory_space=pltpu.VMEM)
    return pl.pallas_call(
        functools.partial(newton_kernel, 0.2 * math.sqrt(longest)),
        out_shape=(
            jax.ShapeDtypeStruct((rows, width), F32),
            jax.ShapeDtypeStruct((rows, width), BF),
        ),
        in_specs=[vmem] * 4,
        out_specs=(vmem, vmem),
        scratch_shapes=[pltpu.VMEM((width, width), BF)] * 6
        + [pltpu.VMEM((rows, width), F32)] * 2
        + [pltpu.VMEM((width, width), F32)],
        compiler_params=small(20),
        cost_estimate=pl.CostEstimate(
            flops=28 * width**3, bytes_accessed=8 * width * width, transcendentals=0
        ),
        name="newton_schulz",
    )(gram, other, mom, weight)


def after(value, *others):
    return lax.optimization_barrier((value, *others))


def ring_sum(far, near):
    rows = far[0].shape[0]
    up3, up2, up1, mine, down1, down2, down3 = near
    copies, homes = up(far[0]), down(far[1])
    below = jnp.concatenate([add_bf(up3[:rows], copies), up3[rows:]], axis=0)
    above = jnp.concatenate([down3[:rows], add_bf(down3[rows:], homes)], axis=0)
    for near_up, near_down in ((up2, down2), (up1, down1)):
        below, above = add_bf(near_up, up(below)), add_bf(near_down, down(above))
    return mine.astype(F32) + up(below).astype(F32) + down(above).astype(F32)


def ring(block):
    rows, width = block.shape

    def one(step, carry):
        below, above, got = carry
        got = lax.dynamic_update_slice(got, below, ((4 - step) * rows, 0))
        got = lax.dynamic_update_slice(got, above, ((4 + step) * rows, 0))
        return up(below), down(above), got

    got = jnp.zeros((NZ * rows, width), block.dtype)
    far, _, got = lax.fori_loop(0, 4, one, (block, block, got))
    return lax.dynamic_update_slice(got, far, (0, 0))


def body(tokens_in, out_grads, counts, copy_list, weights, momentum):
    acts = tokens_in[0]
    grads = out_grads[0]
    model_width = acts.shape[1]
    width = grads.shape[1]
    here = jnp.stack([lax.axis_index(name) for name in ("z", "core", "x", "y")]).astype(jnp.int32)

    tokens = (counts[0], swap(counts[0]), acts, swap(acts), grads, swap(grads))
    got_counts, got, got_grads = tokens[1::2]
    far = far_terms(here, counts[0], acts, grads)
    far = far_terms(here, got_counts, got, got_grads, far)
    near = terms(here, *tokens, (3, 2, 1, 0, -1, -2, -3))
    total = ring_sum(far, near)
    rows = total.shape[0] // 2
    copy_sum, home_sum = total[:rows].astype(BF), total[rows:]

    pieces = [copy_sum] + [shift(copy_sum, "y", offset) for offset in FAR_LAST[1:]]
    copies, *sent = buckets(here, copy_list, pieces)
    for ahead in (2, 1, 3):
        copies = copies + shift(sent[ahead - 1], "x", ahead).astype(F32)
    fresh_mom = beta_mom * momentum[0] + (home_sum + copies)

    own = ring(fresh_mom.astype(BF))
    gram = lax.dot_general(own, own, (((0,), (0,)), ((), ())), preferred_element_type=F32)
    update, fresh = newton_schulz(
        gram, swap(own), fresh_mom, weights[0], max(model_width, width)
    )

    pieces = [fresh] + [shift(fresh, "x", offset) for offset in FAR_LAST[1:]]
    kept, *sent = wanted(here, copy_list, pieces)
    pieces = [kept] + [shift(sent[offset - 1], "y", offset) for offset in FAR_FIRST[1:]]
    replica = pick(here, copy_list, pieces)

    own = ring(replica)
    full = place(1, here, swap(own), place(0, here, own))
    return (fresh_mom[None], update[None], full[None])


def solution(mesh):
    grid = Mesh(mesh.devices.reshape(NZ, NC, NX, NY), ("z", "core", "x", "y"))
    split = P(("x", "y"), ("z", "core"), None)
    return jax.shard_map(
        body,
        mesh=grid,
        in_specs=(split, split, split, P(), split, split),
        out_specs=(split, split, P(("x", "y"), None, None)),
        check_vma=False,
    )
```

```python
import functools
import math

import jax
import jax.numpy as jnp
from jax import lax
from jax.experimental import pallas as pl
from jax.experimental.pallas import tpu as pltpu
from jax.sharding import Mesh, PartitionSpec as P

coef_a = 3.4445
coef_b = -4.775
coef_c = 2.0315
beta_mom = 0.95
learn_rate = 0.02
norm_eps = 1e-07

NZ, NC, NX, NY = 8, 2, 4, 4
FAR_LAST, FAR_FIRST = (0, 1, 3, 2), (0, 2, 1, 3)
BF = jnp.bfloat16
F32 = jnp.float32


def swap(value):
    return lax.ppermute(value, "core", [(0, 1), (1, 0)])


def up(value):
    return lax.ppermute(value, "z", [(i, (i + 1) % NZ) for i in range(NZ)])


def down(value):
    return lax.ppermute(value, "z", [((i + 1) % NZ, i) for i in range(NZ)])


def shift(value, axis, offset):
    return lax.ppermute(value, axis, [(i, (i + offset) % 4) for i in range(4)])


def add_bf(left, right):
    return (left.astype(F32) + right.astype(F32)).astype(BF)


SMEM = pl.BlockSpec(memory_space=pltpu.SMEM)
VMEM = pl.BlockSpec(memory_space=pltpu.VMEM)
ANY = pl.BlockSpec(memory_space=pl.ANY)


def small(limit=8):
    return pltpu.CompilerParams(vmem_limit_bytes=limit * 1024 * 1024)


def place_kernel(side, here_ref, blocks_ref, *refs):
    out_ref, sems = refs[-2:]
    rows = blocks_ref.shape[0] // NZ
    z, core = here_ref[0], here_ref[1]
    parity = 1 - core if side else core
    copies = []
    for index in range(NZ):
        there = NC * lax.rem(z + index + NZ // 2, NZ) + parity
        copies.append(
            pltpu.make_async_copy(
                blocks_ref.at[pl.ds(index * rows, rows), :],
                out_ref.at[pl.ds(pl.multiple_of(there * rows, rows), rows), :],
                sems.at[index],
            )
        )
    for copy in copies:
        copy.start()
    for copy in copies:
        copy.wait()


def place(side, here, blocks, before=None):
    return pl.pallas_call(
        functools.partial(place_kernel, side),
        out_shape=jax.ShapeDtypeStruct((NC * blocks.shape[0], blocks.shape[1]), blocks.dtype),
        in_specs=[SMEM, VMEM] + ([] if before is None else [ANY]),
        out_specs=ANY,
        scratch_shapes=[pltpu.SemaphoreType.DMA((NZ,))],
        input_output_aliases={} if before is None else {2: 0},
        compiler_params=small(),
        name="place",
    )(here, blocks, *([] if before is None else [before]))


def bucket_kernel(here_ref, list_ref, *refs):
    pieces, outs = refs[:NY], refs[NY:]
    x, y = here_ref[2], here_ref[3]
    totals = [jnp.zeros(outs[0].shape, F32) for _ in range(NX)]
    for offset, piece in zip(FAR_LAST, pieces, strict=True):
        target = list_ref[x * NY + lax.rem(y + NY - offset, NY)]
        value = piece[...].astype(F32)
        for ahead in range(NX):
            fits = target == lax.rem(x + ahead, NX) * NY + y
            totals[ahead] = totals[ahead] + jnp.where(fits, value, 0.0)
    for out, total in zip(outs, totals, strict=True):
        out[...] = total.astype(out.dtype)


def buckets(here, copy_list, pieces):
    shape = pieces[0].shape
    return pl.pallas_call(
        bucket_kernel,
        out_shape=tuple(jax.ShapeDtypeStruct(shape, BF if k else F32) for k in range(NX)),
        in_specs=[SMEM, SMEM] + [VMEM] * NY,
        out_specs=(VMEM,) * NX,
        compiler_params=small(),
        name="buckets",
    )(here, copy_list, *pieces)


def wanted_kernel(here_ref, list_ref, *refs):
    pieces, outs = refs[:NX], refs[NX:]
    x, y = here_ref[2], here_ref[3]
    for offset, out in enumerate(outs):
        source = list_ref[x * NY + lax.rem(y + offset, NY)]
        behind = lax.rem(x + NX - lax.div(source, NY), NX)
        for k, piece in zip(FAR_LAST, pieces, strict=True):

            @pl.when(behind == k)
            def _():
                out[...] = piece[...]


def wanted(here, copy_list, pieces):
    shape = pieces[0].shape
    return pl.pallas_call(
        wanted_kernel,
        out_shape=(jax.ShapeDtypeStruct(shape, BF),) * NY,
        in_specs=[SMEM, SMEM] + [VMEM] * NX,
        out_specs=(VMEM,) * NY,
        compiler_params=small(),
        name="wanted",
    )(here, copy_list, *pieces)


def pick_kernel(here_ref, list_ref, *refs):
    pieces, out = refs[:NY], refs[NY]
    x, y = here_ref[2], here_ref[3]
    behind = lax.rem(y + NY - lax.rem(list_ref[x * NY + y], NY), NY)
    for k, piece in zip(FAR_FIRST, pieces, strict=True):

        @pl.when(behind == k)
        def _():
            out[...] = piece[...]


def pick(here, copy_list, pieces):
    return pl.pallas_call(
        pick_kernel,
        out_shape=jax.ShapeDtypeStruct(pieces[0].shape, BF),
        in_specs=[SMEM, SMEM] + [VMEM] * NY,
        out_specs=VMEM,
        compiler_params=small(),
        name="pick",
    )(here, copy_list, *pieces)


CHUNK = 64


def terms_kernel(
    offsets, here_ref, counts_ref, got_counts_ref, acts_ref, got_ref, grads_ref, got_grads_ref, *out_refs
):
    tok_rows, width = grads_ref.shape
    rows = acts_ref.shape[1] // (NZ * NC)
    z, core = here_ref[0], here_ref[1]
    starts = [
        pl.multiple_of((NC * lax.rem(z + NZ + offset, NZ) + core) * rows, rows) for offset in offsets
    ]
    slot = lax.broadcasted_iota(jnp.int32, (tok_rows, width), 0)
    totals = [None, None]
    for acts, grads, counts in (
        (acts_ref, grads_ref, counts_ref),
        (got_ref, got_grads_ref, got_counts_ref),
    ):
        home, copy = counts[0, 0], counts[0, 1]
        left = jnp.concatenate([acts[:, pl.ds(start, rows)] for start in starts], axis=1)
        value = grads[...].astype(F32)
        for which, (low, high) in enumerate(((home, home + copy), (0, home))):
            right = jnp.where((slot >= low) & (slot < high), value, 0.0).astype(BF)
            part = lax.dot_general(
                left, right, (((0,), (0,)), ((), ())), preferred_element_type=F32
            )
            totals[which] = part if totals[which] is None else totals[which] + part
    for index, out_ref in enumerate(out_refs):
        span = slice(index * rows, (index + 1) * rows)
        out_ref[:rows] = totals[0][span].astype(BF)
        out_ref[rows:] = totals[1][span].astype(BF)


def far_kernel(here_ref, counts_ref, acts_ref, grads_ref, *refs):
    *before, copy_ref, home_ref = refs
    rows = copy_ref.shape[0]
    tok_rows, width = grads_ref.shape
    z, core = here_ref[0], here_ref[1]
    start = pl.multiple_of((NC * lax.rem(z + NZ // 2, NZ) + core) * rows, rows)
    left = acts_ref[:, pl.ds(start, rows)]
    slot = lax.broadcasted_iota(jnp.int32, (tok_rows, width), 0)
    home, copy = counts_ref[0, 0], counts_ref[0, 1]
    value = grads_ref[...].astype(F32)
    for which, (low, high, out_ref) in enumerate(
        ((home, home + copy, copy_ref), (0, home, home_ref))
    ):
        right = jnp.where((slot >= low) & (slot < high), value, 0.0).astype(BF)
        total = lax.dot_general(
            left, right, (((0,), (0,)), ((), ())), preferred_element_type=F32
        )
        if before:
            total = total + before[which][...]
        out_ref[...] = total.astype(out_ref.dtype)


def far_terms(here, counts, acts, grads, before=()):
    tok_rows, width = grads.shape
    rows = acts.shape[1] // (NZ * NC)
    return pl.pallas_call(
        far_kernel,
        out_shape=(jax.ShapeDtypeStruct((rows, width), BF if before else F32),) * 2,
        in_specs=[SMEM] * 2 + [VMEM] * (2 + len(before)),
        out_specs=(VMEM, VMEM),
        compiler_params=small(),
        cost_estimate=pl.CostEstimate(
            flops=4 * tok_rows * rows * width, bytes_accessed=4 * tok_rows * width, transcendentals=0
        ),
        name="far_terms",
    )(here, counts, acts, grads, *before)


def terms(here, counts, got_counts, acts, got, grads, got_grads, offsets):
    tok_rows, width = grads.shape
    rows = acts.shape[1] // (NZ * NC)
    return pl.pallas_call(
        functools.partial(terms_kernel, offsets),
        out_shape=(jax.ShapeDtypeStruct((2 * rows, width), BF),) * len(offsets),
        in_specs=[SMEM] * 3 + [VMEM] * 4,
        out_specs=(VMEM,) * len(offsets),
        compiler_params=small(20),
        cost_estimate=pl.CostEstimate(
            flops=8 * tok_rows * rows * len(offsets) * width,
            bytes_accessed=4 * tok_rows * rows * NZ,
            transcendentals=0,
        ),
        name="terms",
    )(here, counts, got_counts, acts, got, grads, got_grads)


def halves(value):
    high = value.astype(BF)
    return high, (value - high.astype(F32)).astype(BF)


def dot(left, right):
    return jnp.dot(left, right, preferred_element_type=F32)


def newton_kernel(
    factor,
    gram_ref,
    other_ref,
    mom_ref,
    weight_ref,
    update_ref,
    fresh_ref,
    s_hi,
    s_lo,
    k_hi,
    k_lo,
    t_hi,
    t_lo,
    iterate_ref,
    side_ref,
    full_ref,
):
    width = gram_ref.shape[0]
    tile = width // 3
    spans = [slice(i * tile, (i + 1) * tile) for i in range(3)]
    pairs = [(i, j) for i in range(3) for j in range(i, 3)]

    def store(hi, lo, i, j, value):
        hi[spans[i], spans[j]], lo[spans[i], spans[j]] = halves(value)
        if i != j:
            hi[spans[j], spans[i]], lo[spans[j], spans[i]] = halves(value.T)

    def load(hi, lo, i, j):
        return hi[spans[i], spans[j]].astype(F32) + lo[spans[i], spans[j]].astype(F32)

    def product(left, right, i, j):
        (l_hi, l_lo), (r_hi, r_lo) = left, right
        rows, cols = spans[i], spans[j]
        out = dot(l_hi[rows, :], r_lo[:, cols]) + dot(l_lo[rows, :], r_hi[:, cols])
        return out + dot(l_hi[rows, :], r_hi[:, cols])

    def times(value, right):
        hi, lo = halves(value)
        r_hi, r_lo = right
        both = dot(jnp.concatenate([hi, lo], axis=0), r_hi[...])
        rows = value.shape[0]
        return both[:rows] + (both[rows:] + dot(hi, r_lo[...]))

    same = lax.broadcasted_iota(jnp.int32, (tile, tile), 0) == lax.broadcasted_iota(
        jnp.int32, (tile, tile), 1
    )
    total = jnp.zeros((1, 1), F32)
    for span in spans:
        value = gram_ref[span, :] + lax.dot_general(
            other_ref[:, span],
            other_ref[...],
            (((0,), (0,)), ((), ())),
            preferred_element_type=F32,
        )
        full_ref[span, :] = value
        on = jnp.where(same, value[:, span], 0.0)
        total = total + jnp.sum(jnp.sum(on, axis=1, keepdims=True), axis=0, keepdims=True)
    scale = 1.0 / (jnp.sqrt(total) + norm_eps)

    @pl.loop(0, width // CHUNK)
    def _(index):
        chunk = pl.ds(pl.multiple_of(index * CHUNK, CHUNK), CHUNK)
        s_hi[chunk, :], s_lo[chunk, :] = halves(full_ref[chunk, :] * scale * scale)

    iterate_ref[...] = mom_ref[...] * scale
    s, k, t = (s_hi, s_lo), (k_hi, k_lo), (t_hi, t_lo)

    @pl.loop(0, 2)
    def _(step):
        for i, j in pairs:
            store(*k, i, j, coef_b * load(*s, i, j) + coef_c * product(s, s, i, j))
        iterate_ref[...] = coef_a * iterate_ref[...] + times(iterate_ref[...], k)

        @pl.when(step == 0)
        def _():
            for i, j in pairs:
                store(*t, i, j, coef_a * load(*s, i, j) + product(s, k, i, j))
            for i, j in pairs:
                store(*s, i, j, coef_a * load(*t, i, j) + product(t, k, i, j))

    side_ref[...] = iterate_ref[...]
    iterate_ref[...] = coef_a * iterate_ref[...]

    @pl.loop(0, 2)
    def _(index):
        side = side_ref[...]
        side = times(coef_a * side + times(side, k), s)
        side = coef_a * side + times(side, k)
        side_ref[...] = side
        iterate_ref[...] += jnp.where(index == 0, coef_b, coef_c) * side

    iterate = iterate_ref[...]
    update = factor * iterate
    update_ref[...] = update
    fresh_ref[...] = (weight_ref[...].astype(F32) - learn_rate * update).astype(BF)


def newton_schulz(gram, other, mom, weight, longest):
    rows, width = mom.shape
    vmem = pl.BlockSpec(memory_space=pltpu.VMEM)
    return pl.pallas_call(
        functools.partial(newton_kernel, 0.2 * math.sqrt(longest)),
        out_shape=(
            jax.ShapeDtypeStruct((rows, width), F32),
            jax.ShapeDtypeStruct((rows, width), BF),
        ),
        in_specs=[vmem] * 4,
        out_specs=(vmem, vmem),
        scratch_shapes=[pltpu.VMEM((width, width), BF)] * 6
        + [pltpu.VMEM((rows, width), F32)] * 2
        + [pltpu.VMEM((width, width), F32)],
        compiler_params=small(20),
        cost_estimate=pl.CostEstimate(
            flops=28 * width**3, bytes_accessed=8 * width * width, transcendentals=0
        ),
        name="newton_schulz",
    )(gram, other, mom, weight)


def after(value, *others):
    return lax.optimization_barrier((value, *others))


def ring_sum(far, near):
    rows = far[0].shape[0]
    up3, up2, up1, mine, down1, down2, down3 = near
    copies, homes = up(far[0]), down(far[1])
    below = jnp.concatenate([add_bf(up3[:rows], copies), up3[rows:]], axis=0)
    above = jnp.concatenate([down3[:rows], add_bf(down3[rows:], homes)], axis=0)
    for near_up, near_down in ((up2, down2), (up1, down1)):
        below, above = add_bf(near_up, up(below)), add_bf(near_down, down(above))
    return mine.astype(F32) + up(below).astype(F32) + down(above).astype(F32)


def ring(block):
    rows, width = block.shape

    def one(step, carry):
        below, above, got = carry
        got = lax.dynamic_update_slice(got, below, ((4 - step) * rows, 0))
        got = lax.dynamic_update_slice(got, above, ((4 + step) * rows, 0))
        return up(below), down(above), got

    got = jnp.zeros((NZ * rows, width), block.dtype)
    far, _, got = lax.fori_loop(0, 4, one, (block, block, got))
    return lax.dynamic_update_slice(got, far, (0, 0))


def split_ring(block):
    rows, width = block.shape

    def one(step, carry):
        below, above, got = carry
        got = lax.dynamic_update_slice(got, below, ((4 - step) * rows, 0))
        got = lax.dynamic_update_slice(got, above, ((4 + step) * rows, 0))
        return up(below), down(above), got

    got = jnp.zeros((NZ * rows, width), block.dtype)
    below, above, got = lax.fori_loop(0, 3, one, (block, block, got))
    half = rows // 2
    far = (up(below[:half]), down(above[half:]))
    got = lax.dynamic_update_slice(got, below, (rows, 0))
    got = lax.dynamic_update_slice(got, above, (7 * rows, 0))
    got = lax.dynamic_update_slice(got, far[0], (0, 0))
    return lax.dynamic_update_slice(got, far[1], (half, 0))


def body(tokens_in, out_grads, counts, copy_list, weights, momentum):
    acts = tokens_in[0]
    grads = out_grads[0]
    model_width = acts.shape[1]
    width = grads.shape[1]
    here = jnp.stack([lax.axis_index(name) for name in ("z", "core", "x", "y")]).astype(jnp.int32)

    tokens = (counts[0], swap(counts[0]), acts, swap(acts), grads, swap(grads))
    got_counts, got, got_grads = tokens[1::2]
    far = far_terms(here, counts[0], acts, grads)
    far = far_terms(here, got_counts, got, got_grads, far)
    near = terms(here, *tokens, (3, 2, 1, 0, -1, -2, -3))
    total = ring_sum(far, near)
    rows = total.shape[0] // 2
    copy_sum, home_sum = total[:rows].astype(BF), total[rows:]

    pieces = [copy_sum] + [shift(copy_sum, "y", offset) for offset in FAR_LAST[1:]]
    copies, *sent = buckets(here, copy_list, pieces)
    for ahead in (2, 1, 3):
        copies = copies + shift(sent[ahead - 1], "x", ahead).astype(F32)
    fresh_mom = beta_mom * momentum[0] + (home_sum + copies)

    own = ring(fresh_mom.astype(BF))
    gram = lax.dot_general(own, own, (((0,), (0,)), ((), ())), preferred_element_type=F32)
    update, fresh = newton_schulz(
        gram, swap(own), fresh_mom, weights[0], max(model_width, width)
    )

    pieces = [fresh] + [shift(fresh, "x", offset) for offset in FAR_LAST[1:]]
    kept, *sent = wanted(here, copy_list, pieces)
    pieces = [kept] + [shift(sent[offset - 1], "y", offset) for offset in FAR_FIRST[1:]]
    replica = pick(here, copy_list, pieces)

    own = split_ring(replica)
    full = place(1, here, swap(own), place(0, here, own))
    return (fresh_mom[None], update[None], full[None])


def solution(mesh):
    grid = Mesh(mesh.devices.reshape(NZ, NC, NX, NY), ("z", "core", "x", "y"))
    split = P(("x", "y"), ("z", "core"), None)
    return jax.shard_map(
        body,
        mesh=grid,
        in_specs=(split, split, split, P(), split, split),
        out_specs=(split, split, P(("x", "y"), None, None)),
        check_vma=False,
    )
```

```python
import functools
import math

import jax
import jax.numpy as jnp
from jax import lax
from jax.experimental import pallas as pl
from jax.experimental.pallas import tpu as pltpu
from jax.sharding import Mesh, PartitionSpec as P

coef_a = 3.4445
coef_b = -4.775
coef_c = 2.0315
beta_mom = 0.95
learn_rate = 0.02
norm_eps = 1e-07

NZ, NC, NX, NY = 8, 2, 4, 4
FAR_LAST, FAR_FIRST = (0, 1, 3, 2), (0, 2, 1, 3)
BF = jnp.bfloat16
F32 = jnp.float32


def swap(value):
    return lax.ppermute(value, "core", [(0, 1), (1, 0)])


def up(value):
    return lax.ppermute(value, "z", [(i, (i + 1) % NZ) for i in range(NZ)])


def down(value):
    return lax.ppermute(value, "z", [((i + 1) % NZ, i) for i in range(NZ)])


def shift(value, axis, offset):
    return lax.ppermute(value, axis, [(i, (i + offset) % 4) for i in range(4)])


def add_bf(left, right):
    return (left.astype(F32) + right.astype(F32)).astype(BF)


SMEM = pl.BlockSpec(memory_space=pltpu.SMEM)
VMEM = pl.BlockSpec(memory_space=pltpu.VMEM)
ANY = pl.BlockSpec(memory_space=pl.ANY)


def small(limit=8):
    return pltpu.CompilerParams(vmem_limit_bytes=limit * 1024 * 1024)


def place_kernel(side, here_ref, blocks_ref, *refs):
    out_ref, sems = refs[-2:]
    rows = blocks_ref.shape[0] // NZ
    z, core = here_ref[0], here_ref[1]
    parity = 1 - core if side else core
    copies = []
    for index in range(NZ):
        there = NC * lax.rem(z + index + NZ // 2, NZ) + parity
        copies.append(
            pltpu.make_async_copy(
                blocks_ref.at[pl.ds(index * rows, rows), :],
                out_ref.at[pl.ds(pl.multiple_of(there * rows, rows), rows), :],
                sems.at[index],
            )
        )
    for copy in copies:
        copy.start()
    for copy in copies:
        copy.wait()


def place(side, here, blocks, before=None):
    return pl.pallas_call(
        functools.partial(place_kernel, side),
        out_shape=jax.ShapeDtypeStruct((NC * blocks.shape[0], blocks.shape[1]), blocks.dtype),
        in_specs=[SMEM, VMEM] + ([] if before is None else [ANY]),
        out_specs=ANY,
        scratch_shapes=[pltpu.SemaphoreType.DMA((NZ,))],
        input_output_aliases={} if before is None else {2: 0},
        compiler_params=small(),
        name="place",
    )(here, blocks, *([] if before is None else [before]))


def bucket_kernel(here_ref, list_ref, *refs):
    pieces, outs = refs[:NY], refs[NY:]
    x, y = here_ref[2], here_ref[3]
    totals = [jnp.zeros(outs[0].shape, F32) for _ in range(NX)]
    for offset, piece in zip(FAR_LAST, pieces, strict=True):
        target = list_ref[x * NY + lax.rem(y + NY - offset, NY)]
        value = piece[...].astype(F32)
        for ahead in range(NX):
            fits = target == lax.rem(x + ahead, NX) * NY + y
            totals[ahead] = totals[ahead] + jnp.where(fits, value, 0.0)
    for out, total in zip(outs, totals, strict=True):
        out[...] = total.astype(out.dtype)


def buckets(here, copy_list, pieces):
    shape = pieces[0].shape
    return pl.pallas_call(
        bucket_kernel,
        out_shape=tuple(jax.ShapeDtypeStruct(shape, BF if k else F32) for k in range(NX)),
        in_specs=[SMEM, SMEM] + [VMEM] * NY,
        out_specs=(VMEM,) * NX,
        compiler_params=small(),
        name="buckets",
    )(here, copy_list, *pieces)


def wanted_kernel(here_ref, list_ref, *refs):
    pieces, outs = refs[:NX], refs[NX:]
    x, y = here_ref[2], here_ref[3]
    for offset, out in enumerate(outs):
        source = list_ref[x * NY + lax.rem(y + offset, NY)]
        behind = lax.rem(x + NX - lax.div(source, NY), NX)
        for k, piece in zip(FAR_LAST, pieces, strict=True):

            @pl.when(behind == k)
            def _():
                out[...] = piece[...]


def wanted(here, copy_list, pieces):
    shape = pieces[0].shape
    return pl.pallas_call(
        wanted_kernel,
        out_shape=(jax.ShapeDtypeStruct(shape, BF),) * NY,
        in_specs=[SMEM, SMEM] + [VMEM] * NX,
        out_specs=(VMEM,) * NY,
        compiler_params=small(),
        name="wanted",
    )(here, copy_list, *pieces)


def pick_kernel(here_ref, list_ref, *refs):
    pieces, out = refs[:NY], refs[NY]
    x, y = here_ref[2], here_ref[3]
    behind = lax.rem(y + NY - lax.rem(list_ref[x * NY + y], NY), NY)
    for k, piece in zip(FAR_FIRST, pieces, strict=True):

        @pl.when(behind == k)
        def _():
            out[...] = piece[...]


def pick(here, copy_list, pieces):
    return pl.pallas_call(
        pick_kernel,
        out_shape=jax.ShapeDtypeStruct(pieces[0].shape, BF),
        in_specs=[SMEM, SMEM] + [VMEM] * NY,
        out_specs=VMEM,
        compiler_params=small(),
        name="pick",
    )(here, copy_list, *pieces)


CHUNK = 64


def terms_kernel(
    offsets, here_ref, counts_ref, got_counts_ref, acts_ref, got_ref, grads_ref, got_grads_ref, *out_refs
):
    tok_rows, width = grads_ref.shape
    rows = acts_ref.shape[1] // (NZ * NC)
    z, core = here_ref[0], here_ref[1]
    starts = [
        pl.multiple_of((NC * lax.rem(z + NZ + offset, NZ) + core) * rows, rows) for offset in offsets
    ]
    slot = lax.broadcasted_iota(jnp.int32, (tok_rows, width), 0)
    totals = [None, None]
    for acts, grads, counts in (
        (acts_ref, grads_ref, counts_ref),
        (got_ref, got_grads_ref, got_counts_ref),
    ):
        home, copy = counts[0, 0], counts[0, 1]
        left = jnp.concatenate([acts[:, pl.ds(start, rows)] for start in starts], axis=1)
        value = grads[...].astype(F32)
        for which, (low, high) in enumerate(((home, home + copy), (0, home))):
            right = jnp.where((slot >= low) & (slot < high), value, 0.0).astype(BF)
            part = lax.dot_general(
                left, right, (((0,), (0,)), ((), ())), preferred_element_type=F32
            )
            totals[which] = part if totals[which] is None else totals[which] + part
    for index, out_ref in enumerate(out_refs):
        span = slice(index * rows, (index + 1) * rows)
        out_ref[:rows] = totals[0][span].astype(BF)
        out_ref[rows:] = totals[1][span].astype(BF)


def far_kernel(here_ref, counts_ref, acts_ref, grads_ref, *refs):
    *before, copy_ref, home_ref = refs
    rows = copy_ref.shape[0]
    tok_rows, width = grads_ref.shape
    z, core = here_ref[0], here_ref[1]
    start = pl.multiple_of((NC * lax.rem(z + NZ // 2, NZ) + core) * rows, rows)
    left = acts_ref[:, pl.ds(start, rows)]
    slot = lax.broadcasted_iota(jnp.int32, (tok_rows, width), 0)
    home, copy = counts_ref[0, 0], counts_ref[0, 1]
    value = grads_ref[...].astype(F32)
    for which, (low, high, out_ref) in enumerate(
        ((home, home + copy, copy_ref), (0, home, home_ref))
    ):
        right = jnp.where((slot >= low) & (slot < high), value, 0.0).astype(BF)
        total = lax.dot_general(
            left, right, (((0,), (0,)), ((), ())), preferred_element_type=F32
        )
        if before:
            total = total + before[which][...]
        out_ref[...] = total.astype(out_ref.dtype)


def far_terms(here, counts, acts, grads, before=()):
    tok_rows, width = grads.shape
    rows = acts.shape[1] // (NZ * NC)
    return pl.pallas_call(
        far_kernel,
        out_shape=(jax.ShapeDtypeStruct((rows, width), BF if before else F32),) * 2,
        in_specs=[SMEM] * 2 + [VMEM] * (2 + len(before)),
        out_specs=(VMEM, VMEM),
        compiler_params=small(),
        cost_estimate=pl.CostEstimate(
            flops=4 * tok_rows * rows * width, bytes_accessed=4 * tok_rows * width, transcendentals=0
        ),
        name="far_terms",
    )(here, counts, acts, grads, *before)


def terms(here, counts, got_counts, acts, got, grads, got_grads, offsets):
    tok_rows, width = grads.shape
    rows = acts.shape[1] // (NZ * NC)
    return pl.pallas_call(
        functools.partial(terms_kernel, offsets),
        out_shape=(jax.ShapeDtypeStruct((2 * rows, width), BF),) * len(offsets),
        in_specs=[SMEM] * 3 + [VMEM] * 4,
        out_specs=(VMEM,) * len(offsets),
        compiler_params=small(20),
        cost_estimate=pl.CostEstimate(
            flops=8 * tok_rows * rows * len(offsets) * width,
            bytes_accessed=4 * tok_rows * rows * NZ,
            transcendentals=0,
        ),
        name="terms",
    )(here, counts, got_counts, acts, got, grads, got_grads)


def halves(value):
    high = value.astype(BF)
    return high, (value - high.astype(F32)).astype(BF)


def dot(left, right):
    return jnp.dot(left, right, preferred_element_type=F32)


def newton_kernel(
    factor,
    gram_ref,
    other_ref,
    mom_ref,
    weight_ref,
    update_ref,
    fresh_ref,
    s_hi,
    s_lo,
    k_hi,
    k_lo,
    t_hi,
    t_lo,
    iterate_ref,
    side_ref,
    full_ref,
):
    width = gram_ref.shape[0]
    tile = width // 3
    spans = [slice(i * tile, (i + 1) * tile) for i in range(3)]
    pairs = [(i, j) for i in range(3) for j in range(i, 3)]

    def store(hi, lo, i, j, value):
        hi[spans[i], spans[j]], lo[spans[i], spans[j]] = halves(value)
        if i != j:
            hi[spans[j], spans[i]], lo[spans[j], spans[i]] = halves(value.T)

    def load(hi, lo, i, j):
        return hi[spans[i], spans[j]].astype(F32) + lo[spans[i], spans[j]].astype(F32)

    def product(left, right, i, j):
        (l_hi, l_lo), (r_hi, r_lo) = left, right
        rows, cols = spans[i], spans[j]
        out = dot(l_hi[rows, :], r_lo[:, cols]) + dot(l_lo[rows, :], r_hi[:, cols])
        return out + dot(l_hi[rows, :], r_hi[:, cols])

    def times(value, right):
        hi, lo = halves(value)
        r_hi, r_lo = right
        both = dot(jnp.concatenate([hi, lo], axis=0), r_hi[...])
        rows = value.shape[0]
        return both[:rows] + (both[rows:] + dot(hi, r_lo[...]))

    same = lax.broadcasted_iota(jnp.int32, (tile, tile), 0) == lax.broadcasted_iota(
        jnp.int32, (tile, tile), 1
    )
    total = jnp.zeros((1, 1), F32)
    for span in spans:
        value = gram_ref[span, :] + lax.dot_general(
            other_ref[:, span],
            other_ref[...],
            (((0,), (0,)), ((), ())),
            preferred_element_type=F32,
        )
        full_ref[span, :] = value
        on = jnp.where(same, value[:, span], 0.0)
        total = total + jnp.sum(jnp.sum(on, axis=1, keepdims=True), axis=0, keepdims=True)
    scale = 1.0 / (jnp.sqrt(total) + norm_eps)

    @pl.loop(0, width // CHUNK)
    def _(index):
        chunk = pl.ds(pl.multiple_of(index * CHUNK, CHUNK), CHUNK)
        s_hi[chunk, :], s_lo[chunk, :] = halves(full_ref[chunk, :] * scale * scale)

    iterate_ref[...] = mom_ref[...] * scale
    s, k, t = (s_hi, s_lo), (k_hi, k_lo), (t_hi, t_lo)

    @pl.loop(0, 2)
    def _(step):
        for i, j in pairs:
            store(*k, i, j, coef_b * load(*s, i, j) + coef_c * product(s, s, i, j))
        iterate_ref[...] = coef_a * iterate_ref[...] + times(iterate_ref[...], k)

        @pl.when(step == 0)
        def _():
            for i, j in pairs:
                store(*t, i, j, coef_a * load(*s, i, j) + product(s, k, i, j))
            for i, j in pairs:
                store(*s, i, j, coef_a * load(*t, i, j) + product(t, k, i, j))

    side_ref[...] = iterate_ref[...]
    iterate_ref[...] = coef_a * iterate_ref[...]

    @pl.loop(0, 2)
    def _(index):
        side = side_ref[...]
        side = times(coef_a * side + times(side, k), s)
        side = coef_a * side + times(side, k)
        side_ref[...] = side
        iterate_ref[...] += jnp.where(index == 0, coef_b, coef_c) * side

    iterate = iterate_ref[...]
    update = factor * iterate
    update_ref[...] = update
    fresh_ref[...] = (weight_ref[...].astype(F32) - learn_rate * update).astype(BF)


def newton_schulz(gram, other, mom, weight, longest):
    rows, width = mom.shape
    vmem = pl.BlockSpec(memory_space=pltpu.VMEM)
    return pl.pallas_call(
        functools.partial(newton_kernel, 0.2 * math.sqrt(longest)),
        out_shape=(
            jax.ShapeDtypeStruct((rows, width), F32),
            jax.ShapeDtypeStruct((rows, width), BF),
        ),
        in_specs=[vmem] * 4,
        out_specs=(vmem, vmem),
        scratch_shapes=[pltpu.VMEM((width, width), BF)] * 6
        + [pltpu.VMEM((rows, width), F32)] * 2
        + [pltpu.VMEM((width, width), F32)],
        compiler_params=small(20),
        cost_estimate=pl.CostEstimate(
            flops=28 * width**3, bytes_accessed=8 * width * width, transcendentals=0
        ),
        name="newton_schulz",
    )(gram, other, mom, weight)


def after(value, *others):
    return lax.optimization_barrier((value, *others))


def ring_sum(far, near):
    rows = far[0].shape[0]
    up3, up2, up1, mine, down1, down2, down3 = near
    copies, homes = up(far[0]), down(far[1])
    below = jnp.concatenate([add_bf(up3[:rows], copies), up3[rows:]], axis=0)
    above = jnp.concatenate([down3[:rows], add_bf(down3[rows:], homes)], axis=0)
    for near_up, near_down in ((up2, down2), (up1, down1)):
        below, above = add_bf(near_up, up(below)), add_bf(near_down, down(above))
    return mine.astype(F32) + up(below).astype(F32) + down(above).astype(F32)


def ring(block, unroll=1):
    rows, width = block.shape

    def one(step, carry):
        below, above, got = carry
        got = lax.dynamic_update_slice(got, below, ((4 - step) * rows, 0))
        got = lax.dynamic_update_slice(got, above, ((4 + step) * rows, 0))
        return up(below), down(above), got

    got = jnp.zeros((NZ * rows, width), block.dtype)
    far, _, got = lax.fori_loop(0, 4, one, (block, block, got), unroll=unroll)
    return lax.dynamic_update_slice(got, far, (0, 0))


def body(tokens_in, out_grads, counts, copy_list, weights, momentum):
    acts = tokens_in[0]
    grads = out_grads[0]
    model_width = acts.shape[1]
    width = grads.shape[1]
    here = jnp.stack([lax.axis_index(name) for name in ("z", "core", "x", "y")]).astype(jnp.int32)

    tokens = (counts[0], swap(counts[0]), acts, swap(acts), grads, swap(grads))
    got_counts, got, got_grads = tokens[1::2]
    far = far_terms(here, counts[0], acts, grads)
    far = far_terms(here, got_counts, got, got_grads, far)
    near = terms(here, *tokens, (3, 2, 1, 0, -1, -2, -3))
    total = ring_sum(far, near)
    rows = total.shape[0] // 2
    copy_sum, home_sum = total[:rows].astype(BF), total[rows:]

    pieces = [copy_sum] + [shift(copy_sum, "y", offset) for offset in FAR_LAST[1:]]
    copies, *sent = buckets(here, copy_list, pieces)
    for ahead in (2, 1, 3):
        copies = copies + shift(sent[ahead - 1], "x", ahead).astype(F32)
    fresh_mom = beta_mom * momentum[0] + (home_sum + copies)

    own = ring(fresh_mom.astype(BF))
    gram = lax.dot_general(own, own, (((0,), (0,)), ((), ())), preferred_element_type=F32)
    update, fresh = newton_schulz(
        gram, swap(own), fresh_mom, weights[0], max(model_width, width)
    )

    pieces = [fresh] + [shift(fresh, "x", offset) for offset in FAR_LAST[1:]]
    kept, *sent = wanted(here, copy_list, pieces)
    pieces = [kept] + [shift(sent[offset - 1], "y", offset) for offset in FAR_FIRST[1:]]
    replica = pick(here, copy_list, pieces)

    own = ring(replica, 2)
    full = place(1, here, swap(own), place(0, here, own))
    return (fresh_mom[None], update[None], full[None])


def solution(mesh):
    grid = Mesh(mesh.devices.reshape(NZ, NC, NX, NY), ("z", "core", "x", "y"))
    split = P(("x", "y"), ("z", "core"), None)
    return jax.shard_map(
        body,
        mesh=grid,
        in_specs=(split, split, split, P(), split, split),
        out_specs=(split, split, P(("x", "y"), None, None)),
        check_vma=False,
    )
```
